32 devices in a mesh: dp: 2 (over x), chan: 16 (over z, y, core).
Axes of the slice: x: 2, y: 2, z: 4, core: 2. Of those that a mesh axis runs over, the one named last changes fastest.
Arguments:
- features: bfloat16 [2, 2048, 16, 128], P('dp', 'chan'), may hold values from -7 to 7
- w_one: bfloat16 [2048, 256], P('chan'), may hold values from -0.1875 to 0.1875
- w_atrous: bfloat16 [3, 9, 2048, 256], P(None, None, 'chan'), may hold values from -0.0625 to 0.0625
- w_pool: bfloat16 [2048, 256], P('chan'), may hold values from -0.1875 to 0.1875
- w_proj: bfloat16 [5, 256, 256], P(None, 'chan'), may hold values from -0.25 to 0.25
- gains: float32 [5, 256], P(None, 'chan'), may hold values from 0.1 to 1.9
- biases: float32 [5, 256], P(None, 'chan'), may hold values from -3 to 3
- out_grad: bfloat16 [2, 256, 16, 128], P('dp', 'chan'), may hold values from -6 to 6
Outputs:
- output: float32 [2, 256, 16, 128], P('dp', 'chan')
- features_grad: float32 [2, 2048, 16, 128], P('dp', 'chan')
- w_one_grad: float32 [2048, 256], P('chan')
- w_atrous_grad: float32 [3, 9, 2048, 256], P(None, None, 'chan')
- w_pool_grad: float32 [2048, 256], P('chan')
- w_proj_grad: float32 [5, 256, 256], P(None, 'chan')
- gains_grad: float32 [5, 256], P(None, 'chan')
- biases_grad: float32 [5, 256], P(None, 'chan')
The draws below stay inside these ranges and needn't reach their ends.
All inputs are finite; a program needn't handle non-finite values.
Results may differ from the reference program's by a relative error of at most 0.009.
Values may be sent and summed in bfloat16 or wider, within the bound.
A program may use at most 128 MiB of HBM per device.

```python
import jax
import jax.numpy as jnp
from jax import lax

CIN = 2048
COUT = 256
H = 16
W = 128
IMAGES = 2


def draw_features(key, part):
    key = jax.random.fold_in(key, 7)
    offset_key, noise_key = jax.random.split(key, 2)
    offset = jnp.clip(jax.random.normal(offset_key, (IMAGES, CIN, 1, 1), jnp.float32), -3.0, 3.0)
    noise = jnp.clip(jax.random.normal(noise_key, (IMAGES, CIN, H, W), jnp.float32), -4.0, 4.0)
    values = offset + noise
    return values.astype(jnp.bfloat16)


def raised(array, own_key, source, target, parts, factor):
    owner, partner = [(jnp.arange(array.shape[dim]) // (array.shape[dim] // parts)).reshape([-1 if axis == dim else 1 for axis in range(array.ndim)]) for dim in (source, target)]
    chosen = jax.random.permutation(own_key, parts)[partner]
    strong = (owner == chosen) | (owner == (partner + parts // 2) % parts)
    return jnp.where(strong, factor * array, array)


def block_levels(key, dims, cuts, low, high):
    def one(dim, blocks):
        draws = jax.random.uniform(jax.random.fold_in(jax.random.fold_in(key, 6), dim), (blocks,), jnp.float32, low / len(cuts), high / len(cuts))
        return jnp.repeat(jnp.exp(draws), dims[dim] // blocks).reshape((-1,) + (1,) * (len(dims) - dim - 1))

    level = one(*cuts[0])
    for cut in cuts[1:]:
        level = level * one(*cut)
    return level


def centred(stream_key, dims, scale, reach, cuts=(), held_as=jnp.bfloat16):
    drawn = scale * jax.random.normal(stream_key, dims, jnp.float32)
    if cuts:
        drawn = drawn * block_levels(stream_key, dims, cuts, -0.22, 0.18)
    return jnp.clip(drawn, -reach, reach).astype(held_as)


def gaussian_with(rng, dims, deviation, bound, cuts, heavy, dtype=jnp.bfloat16):
    result = deviation * jax.random.normal(rng, dims, jnp.float32)
    if cuts:
        result = result * block_levels(rng, dims, cuts, -0.22, 0.18)
    return jnp.clip(raised(result, jax.random.fold_in(rng, 3), *heavy), -bound, bound).astype(dtype)


def setup_inputs(seed: int = 0) -> dict:
    seeds = jax.random.split(jax.random.key(seed), 9)
    features = draw_features(jax.random.fold_in(seeds[8], 71), 0)
    w_one = gaussian_with(seeds[1], (CIN, COUT), CIN ** -0.5, 0.1875, ((0, 16),), (0, 1, 16, 2.0))
    w_atrous = gaussian_with(seeds[2], (3, 9, CIN, COUT), (9 * CIN) ** -0.5, 0.0625, ((2, 16),), (2, 3, 16, 2.0))
    w_pool = gaussian_with(seeds[3], (CIN, COUT), CIN ** -0.5, 0.1875, ((0, 16),), (0, 1, 16, 2.0))
    w_proj = gaussian_with(seeds[4], (5, COUT, COUT), (5 * COUT) ** -0.5, 0.25, ((1, 16),), (1, 2, 16, 2.0))
    gains = jnp.clip(1.0 + 0.18 * jax.random.normal(seeds[5], (5, COUT), jnp.float32), 0.1, 1.9)
    biases = centred(seeds[6], (5, COUT), 0.5, 3.0, ((1, 16),), jnp.float32)
    out_grad = centred(seeds[7], (IMAGES, COUT, H, W), 1.0, 6.0, ((0, 2), (1, 16)))
    return {"features": features, "w_one": w_one, "w_atrous": w_atrous, "w_pool": w_pool, "w_proj": w_proj, "gains": gains, "biases": biases, "out_grad": out_grad}


atrous_rates = (6, 12, 18)
norm_eps = 1e-05

@jax.custom_vjp
def low(v):
    return lax.optimization_barrier(v.astype(jnp.bfloat16)).astype(jnp.float32)

@jax.custom_vjp
def low_back(v):
    return v

def low_keep(v):
    return (low(v), None)

def low_pass(kept, grad):
    return (grad,)

def back_keep(v):
    return (v, None)

def back_low(kept, grad):
    return (low(grad),)
low.defvjp(low_keep, low_pass)
low_back.defvjp(back_keep, back_low)

def normalize(values, gain, bias):
    average = lax.optimization_barrier(jnp.mean(values, axis=(0, 2, 3)))
    square = lax.optimization_barrier(jnp.mean(values * values, axis=(0, 2, 3)))
    scale = gain * lax.rsqrt(square - average * average + norm_eps)
    shaped = (values - average[None, :, None, None]) * scale[None, :, None, None] + bias[None, :, None, None]
    return jax.nn.silu(shaped)

def forward(features, w_one, w_atrous, w_pool, w_proj, gains, biases):
    highest = lax.Precision.HIGHEST
    branch_list = [jnp.einsum('nchw,co->nohw', features, w_one, precision=highest)]
    for branch, dilation in enumerate(atrous_rates):
        kernel = w_atrous[branch].reshape(3, 3, CIN, COUT)
        branch_list.append(lax.conv_general_dilated(features, kernel, (1, 1), [(dilation, dilation), (dilation, dilation)], rhs_dilation=(dilation, dilation), dimension_numbers=('NCHW', 'HWIO', 'NCHW'), precision=highest))
    projected = jnp.zeros((IMAGES, COUT, H, W), jnp.float32)
    for branch in range(4):
        branch_pre = low_back(branch_list[branch])
        branch_act = low(normalize(branch_pre, gains[branch], biases[branch]))
        projected = projected + jnp.einsum('nohw,od->ndhw', branch_act, w_proj[branch], precision=highest)
    pooled = lax.optimization_barrier(jnp.mean(features, axis=(2, 3)))
    pool_pre = low_back(jnp.dot(pooled, w_pool, precision=highest))
    pool_act = low(jax.nn.silu(pool_pre))
    projected = projected + jnp.dot(pool_act, w_proj[4], precision=highest)[:, :, None, None]
    projected = low_back(projected)
    return normalize(projected, gains[4], biases[4])

def reference(features, w_one, w_atrous, w_pool, w_proj, gains, biases, out_grad):
    inputs = (features.astype(jnp.float32), w_one.astype(jnp.float32), w_atrous.astype(jnp.float32), w_pool.astype(jnp.float32), w_proj.astype(jnp.float32), gains.astype(jnp.float32), biases.astype(jnp.float32))
    output, pullback = jax.vjp(forward, *inputs)
    grads = pullback(out_grad.astype(jnp.float32))
    return (output, grads[0], grads[1], grads[2], grads[3], grads[4], grads[5], grads[6])
```

```python
import functools

import jax
import jax.numpy as jnp
from jax import lax
from jax.experimental import pallas as pl
from jax.experimental.pallas import tpu as pltpu
from jax.sharding import PartitionSpec as P

atrous_rates = (6, 12, 18)
norm_eps = 1e-05


def shifted(values, vertical, horizontal):
    margin = max(abs(vertical), abs(horizontal))
    if margin == 0:
        return values
    height = values.shape[-2]
    breadth = values.shape[-1]
    spacing = [(0, 0)] * (values.ndim - 2) + [(margin, margin), (margin, margin)]
    padded = jnp.pad(values, spacing)
    return padded[
        ...,
        margin + vertical : margin + vertical + height,
        margin + horizontal : margin + horizontal + breadth,
    ]


def tap_offsets(dilation):
    return [
        ((along_rows - 1) * dilation, (along_cols - 1) * dilation)
        for along_rows in range(3)
        for along_cols in range(3)
    ]


def make_patches(features, dilation):
    return jnp.stack(
        [shifted(features, vertical, horizontal) for vertical, horizontal in tap_offsets(dilation)]
    )


def silu_slope(values):
    sigmoid = jax.nn.sigmoid(values)
    return sigmoid * (1.0 + values * (1.0 - sigmoid))


def expand_tail(values, extra):
    return values.reshape(values.shape + (1,) * extra)


def local(features, w_one, w_atrous, w_pool, w_proj, gains, biases, out_grad):
    highest = lax.Precision.HIGHEST
    images, local_in, height, columns = features.shape
    pixels = height * columns
    population = images * pixels * lax.axis_size("dp")
    patches = jnp.stack([make_patches(features, dilation) for dilation in atrous_rates])
    pooled = jnp.sum(features, axis=(2, 3), dtype=jnp.float32) / pixels
    one_term = jnp.einsum("nchw,co->onhw", features, w_one, preferred_element_type=jnp.float32)
    rate_terms = jnp.einsum(
        "rtnchw,rtco->ronhw", patches, w_atrous, preferred_element_type=jnp.float32
    )
    spatial_term = jnp.concatenate([one_term[None], rate_terms])
    pool_term = jnp.dot(pooled, w_pool.astype(jnp.float32), precision=highest).T[None]
    branch_pre, pool_pre = (
        lax.psum_scatter(spatial_term, "chan", scatter_dimension=1, tiled=True),
        lax.psum_scatter(pool_term, "chan", scatter_dimension=1, tiled=True),
    )
    branch_totals, branch_squares = lax.psum(
        (jnp.sum(branch_pre, axis=(2, 3, 4)), jnp.sum(branch_pre * branch_pre, axis=(2, 3, 4))),
        "dp",
    )
    branch_mean = branch_totals / population
    branch_inv = lax.rsqrt(branch_squares / population - branch_mean * branch_mean + norm_eps)
    centred = branch_pre - expand_tail(branch_mean, 3)
    branch_z = centred * expand_tail(gains[:4] * branch_inv, 3) + expand_tail(biases[:4], 3)
    branch_hat = centred * expand_tail(branch_inv, 3)
    act_low = jax.nn.silu(branch_z).astype(jnp.bfloat16)
    pool_act = jax.nn.silu(pool_pre).astype(jnp.bfloat16)
    window = w_proj
    spatial = jnp.einsum("bonhw,bod->dnhw", act_low, window[:4], preferred_element_type=jnp.float32)
    pool_part = jnp.einsum("bon,bod->dn", pool_act, window[4:], preferred_element_type=jnp.float32)
    proj_pre = lax.psum_scatter(
        spatial + pool_part[:, :, None, None], "chan", scatter_dimension=0, tiled=True
    )
    proj_totals, proj_squares = lax.psum(
        (jnp.sum(proj_pre, axis=(1, 2, 3)), jnp.sum(proj_pre * proj_pre, axis=(1, 2, 3))), "dp"
    )
    proj_mean = proj_totals / population
    proj_inv = lax.rsqrt(proj_squares / population - proj_mean * proj_mean + norm_eps)
    proj_centred = proj_pre - expand_tail(proj_mean, 3)
    proj_z = proj_centred * expand_tail(gains[4] * proj_inv, 3) + expand_tail(biases[4], 3)
    proj_hat = proj_centred * expand_tail(proj_inv, 3)
    output = jnp.transpose(jax.nn.silu(proj_z), (1, 0, 2, 3))
    grad_out = jnp.transpose(out_grad, (1, 0, 2, 3)).astype(jnp.float32)
    proj_dz = grad_out * silu_slope(proj_z)
    proj_dbias, proj_dgain = lax.psum(
        (jnp.sum(proj_dz, axis=(1, 2, 3)), jnp.sum(proj_dz * proj_hat, axis=(1, 2, 3))), "dp"
    )
    proj_dpre = expand_tail(gains[4] * proj_inv, 3) * (
        proj_dz
        - expand_tail(proj_dbias / population, 3)
        - proj_hat * expand_tail(proj_dgain / population, 3)
    )
    proj_low = proj_dpre.astype(jnp.bfloat16)
    pool_act_wide = pool_act.astype(jnp.float32)
    portion = lax.all_gather(proj_low, "chan", axis=0, tiled=True)
    window = w_proj
    act_grad = jnp.einsum(
        "bod,dnhw->bonhw", window[:4], portion, preferred_element_type=jnp.float32
    )
    portion_sum = jnp.sum(portion, axis=(2, 3), dtype=jnp.float32)
    pool_grad = jnp.einsum(
        "bod,dn->bon", window[4:].astype(jnp.float32), portion_sum, precision=highest
    )
    spatial_part = jnp.einsum(
        "bonhw,dnhw->bod", act_low, portion, preferred_element_type=jnp.float32
    )
    pool_part = jnp.einsum("bon,dn->bod", pool_act_wide, portion_sum, precision=highest)
    weight_grad = jnp.concatenate([spatial_part, pool_part])
    act_grad, pool_grad, proj_wgrad = (act_grad, pool_grad, weight_grad)
    branch_dz = act_grad * silu_slope(branch_z)
    branch_dbias, branch_dgain = lax.psum(
        (jnp.sum(branch_dz, axis=(2, 3, 4)), jnp.sum(branch_dz * branch_hat, axis=(2, 3, 4))), "dp"
    )
    branch_dpre = expand_tail(gains[:4] * branch_inv, 3) * (
        branch_dz
        - expand_tail(branch_dbias / population, 3)
        - branch_hat * expand_tail(branch_dgain / population, 3)
    )
    branch_low = branch_dpre.astype(jnp.bfloat16)
    pool_low = (pool_grad * silu_slope(pool_pre)).astype(jnp.bfloat16)
    spatial_portion = lax.all_gather(branch_low, "chan", axis=1, tiled=True)
    pool_portion = lax.all_gather(pool_low, "chan", axis=1, tiled=True)
    pool_cols = w_pool.astype(jnp.float32)
    feature_grad = jnp.einsum(
        "co,onhw->nchw", w_one, spatial_portion[0], preferred_element_type=jnp.float32
    )
    patch_grad = jnp.einsum(
        "rtco,ronhw->rtnchw", w_atrous, spatial_portion[1:], preferred_element_type=jnp.float32
    )
    pool_wide = pool_portion[0].astype(jnp.float32)
    pooled_grad = jnp.dot(pool_wide.T, pool_cols.T, precision=highest)
    one_piece = jnp.einsum(
        "nchw,onhw->co", features, spatial_portion[0], preferred_element_type=jnp.float32
    )
    rate_piece = jnp.einsum(
        "rtnchw,ronhw->rtco", patches, spatial_portion[1:], preferred_element_type=jnp.float32
    )
    pool_piece = jnp.dot(pooled.T, pool_wide.T, precision=highest)
    one_grad = one_piece
    rate_grad = rate_piece
    pool_wgrad = pool_piece
    feature_grad, patch_grad, pooled_grad, one_grad, rate_grad, pool_wgrad = (
        feature_grad,
        patch_grad,
        pooled_grad,
        one_grad,
        rate_grad,
        pool_wgrad,
    )
    for branch, dilation in enumerate(atrous_rates):
        for tap_index, (vertical, horizontal) in enumerate(tap_offsets(dilation)):
            feature_grad = feature_grad + shifted(
                patch_grad[branch, tap_index], -vertical, -horizontal
            )
    feature_grad = feature_grad + (pooled_grad / pixels)[:, :, None, None]
    one_grad, rate_grad, pool_wgrad, proj_wgrad = (
        lax.psum(one_grad.astype(jnp.bfloat16), "dp").astype(jnp.float32),
        lax.psum(rate_grad.astype(jnp.bfloat16), "dp").astype(jnp.float32),
        lax.psum(pool_wgrad.astype(jnp.bfloat16), "dp").astype(jnp.float32),
        lax.psum(proj_wgrad.astype(jnp.bfloat16), "dp").astype(jnp.float32),
    )
    gains_grad = jnp.concatenate([branch_dgain, proj_dgain[None]])
    biases_grad = jnp.concatenate([branch_dbias, proj_dbias[None]])
    return (
        output,
        feature_grad,
        one_grad,
        rate_grad,
        pool_wgrad,
        proj_wgrad,
        gains_grad,
        biases_grad,
    )


MESH = pl.DeviceIdType.MESH
F32 = jnp.float32
BF16 = jnp.bfloat16
ROWS = 16
COLS = 128
PIXELS = ROWS * COLS
WIDE = PIXELS + 128
CIN_PART = 128
COUT = 256
GROUPS = 8
BLOCK = 256
ORDER = (0, 3, 2, 1)


def branch_rows(branch):
    if branch == 0:
        return [(None, 0)]
    rate = atrous_rates[branch - 1]
    return [(i, (i - 1) * rate) for i in (1, 0, 2) if abs((i - 1) * rate) < ROWS]


def weight_slots():
    slots = {}
    count = 0
    spans = {}
    for branch in ORDER:
        begin = count
        for i, _ in branch_rows(branch):
            slots[(branch, i)] = count
            count += 1 if branch == 0 else 3
        if branch == 0:
            slots["pool"] = count
            count += 1
        spans[branch] = (begin, count)
    return slots, spans, count


SLOTS, SPANS, NSLOTS = weight_slots()


def width_of(branch):
    return WIDE if branch == 0 else PIXELS


def dot(a, b):
    return jnp.dot(a, b, preferred_element_type=F32)


def dot_nt(a, b):
    return lax.dot_general(a, b, (((1,), (1,)), ((), ())), preferred_element_type=F32)


def iota(shape, dim):
    return lax.broadcasted_iota(jnp.int32, shape, dim)


def lane_sum(v):
    return jnp.sum(v, axis=1, keepdims=True)


def split_lanes(column, lanes=(0, 1, 2)):
    high = column.astype(BF16).astype(F32)
    mid = (column - high).astype(BF16).astype(F32)
    low = column - high - mid
    lane = iota((column.shape[0], 128), 1)
    out = jnp.where(lane == lanes[0], high, 0.0)
    out = out + jnp.where(lane == lanes[1], mid, 0.0)
    return out + jnp.where(lane == lanes[2], low, 0.0)


def encode_pair(v):
    lane = iota(v.shape, v.ndim - 1)
    high = v.astype(BF16).astype(F32)
    low = v - high
    return jnp.where(lane == 0, high, jnp.where(lane == 1, low, 0.0)).astype(BF16)


def decode_pair(e):
    return jnp.broadcast_to(jnp.sum(e.astype(F32), axis=-1, keepdims=True), e.shape)


def shift_cols(v, by):
    if by == 0:
        return v
    lane = iota((v.shape[0], 128), 1)
    keep = (lane >= by) if by > 0 else (lane < 128 + by)
    parts = []
    for h in range(v.shape[1] // 128):
        tile = v[:, h * 128 : (h + 1) * 128]
        parts.append(jnp.where(keep, pltpu.roll(tile, by % 128, 1), 0.0))
    return jnp.concatenate(parts, axis=1) if len(parts) > 1 else parts[0]


def sigmoid(z):
    return 0.5 * jnp.tanh(0.5 * z) + 0.5


INPUTS = ("feat", "og", "w1", "wa", "wpool", "wproj", "par")
OUTPUTS = ("out", "fg", "dw1", "dwa", "dwpool", "dwproj", "dpar")


def scratch_table(sems):
    vm = pltpu.VMEM
    return {
        "fsib": vm((2048, 128), BF16),
        "foth": vm((2048, 128), BF16),
        "x": vm((256, PIXELS), BF16),
        "tw": vm((NSLOTS, GROUPS, 2, 16, 128), BF16),
        "lw": vm((NSLOTS, GROUPS, 16, 256), BF16),
        "acc": vm((4, GROUPS, 16, PIXELS), F32),
        "acp": vm((GROUPS, 16, 128), F32),
        "ys": vm((4, 4, 16, WIDE), BF16),
        "yr": vm((4, 4, 16, WIDE), BF16),
        "zs": vm((4, 4, 16, WIDE), BF16),
        "zr": vm((4, 4, 16, WIDE), BF16),
        "g": vm((4, 2, GROUPS, 16, WIDE), BF16),
        "ogs": vm((2, GROUPS, 16, PIXELS), BF16),
        "pt": vm((GROUPS, 16, 128), F32),
        "wp": vm((GROUPS, 5, 16, 256), BF16),
        "wpt": vm((256, 640), BF16),
        "xs": vm((2, 3, 3, 128, PIXELS), BF16),
        "act": vm((2, 4, GROUPS, 16, PIXELS), BF16),
        "ao": vm((2, 4, 16, PIXELS), BF16),
        "pa": vm((5, 128, 128), F32),
        "pb": vm((5, 128, 128), F32),
        "pm": vm((5, 128, 128), F32),
        "pi": vm((5, 128, 128), F32),
        "s1": vm((5, 128, 128), F32),
        "s2": vm((5, 128, 128), F32),
        "pr": vm((2, GROUPS, 16, PIXELS), F32),
        "dzp": vm((2, GROUPS, 16, PIXELS), F32),
        "dp": vm((2, GROUPS, 2, 16, PIXELS), BF16),
        "dpo": vm((GROUPS, 2, 16, 128), BF16),
        "d": vm((4, 2, GROUPS, 2, 16, PIXELS), BF16),
        "fga": vm((128, PIXELS), F32),
        "pooled": vm((2, 128, 128), F32),
        "ppool": vm((2, 128, 128), F32),
        "ss": pltpu.SemaphoreType.DMA((sems,)),
        "rs": pltpu.SemaphoreType.DMA((sems,)),
    }


class Refs:
    pass


NSEMS = 160


def head_kernel(*refs):
    names = INPUTS + OUTPUTS + tuple(scratch_table(NSEMS))
    r = Refs()
    for name, ref in zip(names, refs, strict=True):
        setattr(r, name, ref)
    x = lax.axis_index("dp")
    c = lax.axis_index("chan")
    k = lax.rem(c, 2)
    y = lax.rem(lax.div(c, 2), 2)
    z = lax.div(c, 4)

    def dev(xx, zz, yy, kk):
        return {"dp": xx, "chan": (zz * 2 + yy) * 2 + kk}

    sibling = dev(x, z, y, 1 - k)
    xdev = dev(1 - x, z, y, k)
    ydev = dev(x, z, 1 - y, k)
    zpos = [None] + [lax.rem(z + i, 4) for i in (1, 2, 3)]
    zfrom = [None] + [lax.rem(z + 4 - i, 4) for i in (1, 2, 3)]
    zdev = [None] + [dev(x, zpos[i], y, k) for i in (1, 2, 3)]

    counter = [0]
    sent = []

    def new(n=1):
        first = counter[0]
        counter[0] += n
        assert counter[0] <= NSEMS
        return first

    def rcopy(src, dst, n, device):
        return pltpu.make_async_remote_copy(
            src_ref=src,
            dst_ref=dst,
            send_sem=r.ss.at[n],
            recv_sem=r.rs.at[n],
            device_id=device,
            device_id_type=MESH,
        )

    def send(src, dst, n, device, group=None):
        copy = rcopy(src, dst, n, device)
        copy.start()
        (sent if group is None else group).append(copy)

    def arrived(ref, n, device):
        rcopy(ref, ref, n, device).wait_recv()

    barrier = pltpu.get_barrier_semaphore()
    partners = [sibling, xdev, ydev] + zdev[1:]
    for partner in partners:
        pl.semaphore_signal(barrier, inc=1, device_id=partner, device_id_type=MESH)
    pl.semaphore_wait(barrier, len(partners))

    n_feat = new()
    send(r.feat, r.fsib, n_feat, sibling)

    rr = iota((256, 256), 0)
    cc = iota((256, 256), 1)
    perm = jnp.where(cc == lax.rem(rr, 16) * 16 + lax.div(rr, 16), 1.0, 0.0).astype(BF16)
    eye = jnp.where(rr == cc, 1.0, 0.0).astype(BF16)

    def permuted(ref, block):
        return dot(perm, ref[block * 256 : (block + 1) * 256, :]).astype(BF16)

    def pre_group(yy, zz):
        return yy * 4 + zz

    def own_group(yy, zz):
        return zz * 2 + yy

    class Gather:
        def __init__(self, slot, group, across):
            self.slot, self.group, self.across = slot, group, across
            self.nz, self.ny, self.nx = new(3), new(4), new(8) if across else None

        def start(self):
            mine = self.slot(self.group(y, z))
            for i in (1, 2, 3):
                send(mine, mine, self.nz + i - 1, zdev[i])
            send(mine, mine, self.ny, ydev)
            if self.across:
                send(mine, mine, self.nx, xdev)

        def forward_z(self):
            for i in (1, 2, 3):
                ref = self.slot(self.group(y, zfrom[i]))
                arrived(ref, self.nz + i - 1, zdev[i])
                send(ref, ref, self.ny + i, ydev)
                if self.across:
                    send(ref, ref, self.nx + i, xdev)

        def forward_y(self):
            for i in range(4):
                ref = self.slot(self.group(1 - y, z if i == 0 else zfrom[i]))
                arrived(ref, self.ny + i, ydev)
                if self.across:
                    send(ref, ref, self.nx + 4 + i, xdev)

        def finish(self, other):
            if self.across:
                for i in range(8):
                    yy = y if i < 4 else 1 - y
                    zz = z if i % 4 == 0 else zfrom[i % 4]
                    arrived(other(self.group(yy, zz)), self.nx + i, xdev)

    g_og = Gather(lambda g: r.ogs.at[x, g], own_group, True)
    g_par = Gather(lambda g: r.pt.at[g], own_group, False)
    g_wp = Gather(lambda g: r.wp.at[g], own_group, False)
    g_pre = {}
    for b in ORDER:
        w = width_of(b)
        g_pre[b] = Gather(lambda g, b=b, w=w: r.g.at[b, x, g, :, pl.ds(0, w)], pre_group, True)

    mine = own_group(y, z)
    og = permuted(r.og, 0)
    for h in range(ROWS):
        r.ogs[x, mine, :, h * 128 : (h + 1) * 128] = og[h * 16 : (h + 1) * 16]
    r.pt[mine] = r.par[...]
    r.wp[mine] = r.wproj[...]

    n_w = {b: new() for b in ORDER}

    def weight_ref(b, i, j):
        return r.w1 if b == 0 else r.wa.at[(b - 1) * 9 + 3 * i + j]

    def transpose_into(slot, ref):
        t = dot_nt(eye, ref[...]).astype(BF16)
        r.tw[slot] = t.reshape(GROUPS, 2, 16, 128)
        r.lw[slot, :, :, 0:128] = r.tw[slot, :, k]

    def prepare_weights(b):
        for i, _ in branch_rows(b):
            slot = SLOTS[(b, i)]
            if b == 0:
                transpose_into(slot, r.w1)
                transpose_into(SLOTS["pool"], r.wpool)
            else:
                for j in range(3):
                    transpose_into(slot + j, weight_ref(b, i, j))
        lo, hi = SPANS[b]
        send(
            r.tw.at[pl.ds(lo, hi - lo), :, 1 - k],
            r.lw.at[pl.ds(lo, hi - lo), :, :, pl.ds(128, 128)],
            n_w[b],
            sibling,
        )

    def wait_weights(b):
        lo, hi = SPANS[b]
        arrived(r.lw.at[pl.ds(lo, hi - lo), :, :, pl.ds(128, 128)], n_w[b], sibling)

    prepare_weights(0)

    def place(ref, base):
        for block in range(8):
            t = permuted(ref, block)
            for h in range(ROWS):
                r.x[base + block * 16 : base + (block + 1) * 16, h * 128 : (h + 1) * 128] = t[
                    h * 16 : (h + 1) * 16
                ]

    place(r.feat, 0)
    arrived(r.fsib, n_feat, sibling)
    place(r.fsib, 128)

    def convolve(b):
        for q in range(PIXELS // BLOCK):
            px = slice(q * BLOCK, (q + 1) * BLOCK)
            total = None
            for i, offset in branch_rows(b):
                source = q + offset * COLS // BLOCK
                if source < 0 or source >= PIXELS // BLOCK:
                    continue
                slot = SLOTS[(b, i)]
                count = 1 if b == 0 else 3
                weights = r.lw[slot : slot + count].reshape(count * 128, 256)
                part = dot(weights, r.x[:, source * BLOCK : (source + 1) * BLOCK])
                total = part if total is None else total + part
            if b:
                rate = atrous_rates[b - 1]
                total = (
                    total[128:256]
                    + shift_cols(total[0:128], rate)
                    + shift_cols(total[256:384], -rate)
                )
            r.acc[b, :, :, px] = total.reshape(GROUPS, 16, BLOCK)
        if b == 0:
            pooled = jnp.zeros((256, 128), F32)
            for h in range(ROWS):
                pooled = pooled + r.x[:, h * 128 : (h + 1) * 128].astype(F32)
            column = lane_sum(pooled) / PIXELS
            r.pooled[x] = jnp.broadcast_to(column[0:128], (128, 128))
            terms = split_lanes(column).astype(BF16)
            slot = SLOTS["pool"]
            sums = lane_sum(dot(r.lw[slot].reshape(128, 256), terms))
            r.acp[...] = jnp.broadcast_to(sums, (128, 128)).reshape(GROUPS, 16, 128)

    n_ry = {b: new() for b in ORDER}
    n_rz = {b: new(3) for b in ORDER}

    def reduce_y_send(b):
        w = width_of(b)
        r.ys[b, :, :, 0:PIXELS] = r.acc[b, pl.ds(4 * (1 - y), 4)].astype(BF16)
        if b == 0:
            r.ys[b, :, :, PIXELS:WIDE] = encode_pair(r.acp[pl.ds(4 * (1 - y), 4)])
        send(r.ys.at[b, :, :, pl.ds(0, w)], r.yr.at[b, :, :, pl.ds(0, w)], n_ry[b], ydev)

    def reduce_z_send(b):
        w = width_of(b)
        arrived(r.yr.at[b, :, :, pl.ds(0, w)], n_ry[b], ydev)
        for i in (1, 2, 3, 0):
            zz = z if i == 0 else zpos[i]
            g = 4 * y + zz
            s = r.acc[b, g] + r.yr[b, zz, :, 0:PIXELS].astype(F32)
            if b == 0:
                e = r.acp[g] + decode_pair(r.yr[b, zz, :, PIXELS:WIDE])
            if i == 0:
                r.acc[b, g] = s
                if b == 0:
                    r.acp[g] = e
            else:
                r.zs[b, i, :, 0:PIXELS] = s.astype(BF16)
                if b == 0:
                    r.zs[b, i, :, PIXELS:WIDE] = encode_pair(e)
                send(
                    r.zs.at[b, i, :, pl.ds(0, w)],
                    r.zr.at[b, i, :, pl.ds(0, w)],
                    n_rz[b] + i - 1,
                    zdev[i],
                )

    def reduce_finish(b):
        w = width_of(b)
        g = pre_group(y, z)
        total = r.acc[b, g]
        extra = r.acp[g] if b == 0 else None
        for i in (1, 2, 3):
            arrived(r.zr.at[b, i, :, pl.ds(0, w)], n_rz[b] + i - 1, zdev[i])
            total = total + r.zr[b, i, :, 0:PIXELS].astype(F32)
            if b == 0:
                extra = extra + decode_pair(r.zr[b, i, :, PIXELS:WIDE])
        r.g[b, x, g, :, 0:PIXELS] = total.astype(BF16)
        if b == 0:
            r.g[b, x, g, :, PIXELS:WIDE] = encode_pair(extra)
        g_pre[b].start()

    def other_pre(b):
        w = width_of(b)
        return lambda g: r.g.at[b, 1 - x, g, :, pl.ds(0, w)]

    shift_pairs = []
    lane_r = iota((128, 128), 0)
    lane_c = iota((128, 128), 1)
    for rate in atrous_rates:
        left = jnp.where(lane_r == lane_c - rate, 1.0, 0.0).astype(BF16)
        right = jnp.where(lane_r == lane_c + rate, 1.0, 0.0).astype(BF16)
        shift_pairs.append(jnp.concatenate([left, right], axis=1))

    def place_shifted(ref, image):
        for block in range(8):
            t = permuted(ref, block)
            rows = slice(block * 16, (block + 1) * 16)
            for a in range(3):
                both = dot(t, shift_pairs[a]).astype(BF16)
                for h in range(ROWS):
                    px = slice(h * 128, (h + 1) * 128)
                    hc = slice(h * 16, (h + 1) * 16)
                    r.xs[image, a, 0, rows, px] = both[hc, 0:128]
                    r.xs[image, a, 1, rows, px] = t[hc]
                    r.xs[image, a, 2, rows, px] = both[hc, 128:256]

    n_foth = new()

    count = float(2 * PIXELS)

    def finish_norm(b, rows, s, q, gain, bias):
        mean = lane_sum(s) / count
        inv = lax.rsqrt(lane_sum(q) / count - mean * mean + norm_eps)
        scale = gain * inv
        r.pa[b, rows] = jnp.broadcast_to(scale, (16, 128))
        r.pb[b, rows] = jnp.broadcast_to(bias - mean * scale, (16, 128))
        r.pm[b, rows] = jnp.broadcast_to(mean, (16, 128))
        r.pi[b, rows] = jnp.broadcast_to(inv, (16, 128))

    def branch_norm(b):
        def group(g, _):
            rows = pl.ds(pl.multiple_of(g * 16, 16), 16)
            s = jnp.zeros((16, 128), F32)
            q = jnp.zeros((16, 128), F32)
            for image in range(2):
                for h in range(ROWS):
                    v = r.g[b, image, g, :, h * 128 : (h + 1) * 128].astype(F32)
                    s = s + v
                    q = q + v * v
            par = r.pt[g]
            finish_norm(b, rows, s, q, par[:, b : b + 1], par[:, 8 + b : 9 + b])
            scale, base = r.pa[b, rows], r.pb[b, rows]
            for image in range(2):
                for h in range(ROWS):
                    px = slice(h * 128, (h + 1) * 128)
                    zed = r.g[b, image, g, :, px].astype(F32) * scale + base
                    r.act[image, b, g, :, px] = (zed * sigmoid(zed)).astype(BF16)
            return 0

        lax.fori_loop(0, GROUPS, group, 0)

    g_par.start()
    g_wp.start()
    steps = len(ORDER)
    for s in range(steps + 3):
        if s < steps:
            b = ORDER[s]
            wait_weights(b)
            convolve(b)
            reduce_y_send(b)
            if s + 1 < steps:
                prepare_weights(ORDER[s + 1])
        if s == 0:
            g_og.start()
        if 1 <= s <= steps:
            reduce_z_send(ORDER[s - 1])
        if s == 1:
            g_par.forward_z()
            g_wp.forward_z()
            g_og.forward_z()
        if s == 2:
            g_par.forward_y()
            g_wp.forward_y()
        if 2 <= s <= steps + 1:
            reduce_finish(ORDER[s - 2])
        if s == 3:
            place_shifted(r.feat, x)
        if 3 <= s <= steps + 2:
            g_pre[ORDER[s - 3]].forward_z()
        if s >= 4:
            g_pre[ORDER[s - 4]].forward_y()
    g_pre[ORDER[steps - 1]].forward_y()
    g_og.forward_y()
    send(r.feat, r.foth, n_foth, xdev)

    for b in range(5):
        r.wpt[:, b * 128 : (b + 1) * 128] = dot_nt(eye, r.wp[:, b].reshape(128, 256)).astype(BF16)

    for b in ORDER:
        g_pre[b].finish(other_pre(b))
        branch_norm(b)

    pool_act = []
    lane128 = iota((128, 128), 1)
    pool_cols = jnp.zeros((128, 128), F32)
    for image in range(2):
        pre = decode_pair(r.g[0, image, :, :, PIXELS:WIDE]).reshape(128, 128)
        r.ppool[image] = pre
        pool_cols = pool_cols + jnp.where(lane128 == image, pre * sigmoid(pre), 0.0)
    pool_cols = pool_cols.astype(BF16)
    pool_out = dot(r.wpt[:, 512:640], pool_cols)

    n_pp = new(2)
    pp_sent = []
    for image in range(2):
        column = pool_out[:, image : image + 1]
        for q in range(PIXELS // BLOCK):
            px = slice(q * BLOCK, (q + 1) * BLOCK)
            part = dot(r.wpt[:, 0:512], r.act[image, :, :, :, px].reshape(512, BLOCK)) + column
            part = part.reshape(GROUPS, 2, 16, BLOCK)
            r.acc[2 * image, :, :, px] = part[:, 0]
            r.acc[2 * image + 1, :, :, px] = part[:, 1]
        send(r.acc.at[2 * image + 1 - k], r.pr.at[image], n_pp + image, sibling, pp_sent)

    for image in range(2):
        for b in range(4):
            r.ao[image, b] = r.act[image, b, mine]

    g_og.finish(lambda g: r.ogs.at[1 - x, g])
    for image in range(2):
        arrived(r.pr.at[image], n_pp + image, sibling)

    def proj_group(g, _):
        rows = pl.ds(pl.multiple_of(g * 16, 16), 16)
        s = jnp.zeros((16, 128), F32)
        q = jnp.zeros((16, 128), F32)
        for image in range(2):
            for h in range(ROWS):
                px = slice(h * 128, (h + 1) * 128)
                v = r.acc[2 * image + k, g, :, px] + r.pr[image, g, :, px]
                r.pr[image, g, :, px] = v
                s = s + v
                q = q + v * v
        par = r.pt[g]
        finish_norm(4, rows, s, q, par[:, 4:5], par[:, 12:13])
        scale, base = r.pa[4, rows], r.pb[4, rows]
        mean, inv = r.pm[4, rows], r.pi[4, rows]
        s1 = jnp.zeros((16, 128), F32)
        s2 = jnp.zeros((16, 128), F32)
        for image in range(2):
            for h in range(ROWS):
                px = slice(h * 128, (h + 1) * 128)
                v = r.pr[image, g, :, px]
                zed = v * scale + base
                sg = sigmoid(zed)
                dz = r.ogs[image, g, :, px].astype(F32) * (sg * (1.0 + zed * (1.0 - sg)))
                r.dzp[image, g, :, px] = dz
                s1 = s1 + dz
                s2 = s2 + dz * (v - mean)
        s1 = jnp.broadcast_to(lane_sum(s1), (16, 128))
        s2 = jnp.broadcast_to(lane_sum(s2), (16, 128)) * inv
        r.s1[4, rows] = s1
        r.s2[4, rows] = s2
        c1 = -scale * s1 / count
        c2 = -scale * inv * s2 / count
        for image in range(2):
            for h in range(ROWS):
                px = slice(h * 128, (h + 1) * 128)
                v = r.pr[image, g, :, px]
                low = scale * r.dzp[image, g, :, px] + ((v - mean) * c2 + c1)
                r.dp[image, g, k, :, px] = low.astype(BF16)
        return 0

    lax.fori_loop(0, GROUPS, proj_group, 0)

    n_dp = new(2)
    for image in range(2):
        ref = r.dp.at[image, :, k]
        send(ref, ref, n_dp + image, sibling)

    my_rows = pl.ds(pl.multiple_of(mine * 16, 16), 16)
    scale, base = r.pa[4, my_rows], r.pb[4, my_rows]
    for h in range(ROWS):
        zed = r.pr[x, mine, :, h * 128 : (h + 1) * 128] * scale + base
        r.out[pl.ds(h, 16, stride=16), :] = zed * sigmoid(zed)

    for image in range(2):
        arrived(r.dp.at[image, :, 1 - k], n_dp + image, sibling)

    ones = jnp.ones((PIXELS, 128), BF16)
    wp4 = r.wp[:, 4].reshape(128, 256)
    dpo = jnp.zeros((128, 128), F32)
    dwp4 = jnp.zeros((16, 256), F32)
    lane16 = iota((16, 128), 1)
    for image in range(2):
        dps = r.dp[image].reshape(256, PIXELS)
        row_sums = dot(dps, ones)[:, 0:1]
        pool_grad = lane_sum(dot(wp4, split_lanes(row_sums).astype(BF16)))
        pre = r.ppool[image][:, 0:1]
        sg = sigmoid(pre)
        low = (pool_grad * (sg * (1.0 + pre * (1.0 - sg)))).astype(BF16).astype(F32)
        for lane in (image, image + 2, image + 4):
            dpo = dpo + jnp.where(lane128 == lane, low, 0.0)
        mine_pre = r.ppool[image, my_rows][:, 0:1]
        mine_act = (mine_pre * sigmoid(mine_pre)).astype(BF16).astype(F32)
        dwp4 = dwp4 + mine_act * dot_nt(jnp.ones((16, PIXELS), BF16), dps)
    r.dwproj[4] = dwp4
    r.dpo[:, k] = dpo.astype(BF16).reshape(GROUPS, 16, 128)
    n_dpo = new()
    ref = r.dpo.at[:, k]
    send(ref, ref, n_dpo, sibling)

    dwp = jnp.zeros((64, 256), F32)
    for image in range(2):
        dwp = dwp + dot_nt(r.ao[image].reshape(64, PIXELS), r.dp[image].reshape(256, PIXELS))
    r.dwproj[0:4] = dwp.reshape(4, 16, 256)

    for copy in pp_sent:
        copy.wait_send()
    for image in range(2):
        for q in range(PIXELS // BLOCK):
            px = slice(q * BLOCK, (q + 1) * BLOCK)
            dblock = r.dp[image, :, :, :, px].reshape(256, BLOCK)
            for b in range(4):
                part = dot(r.wp[:, b].reshape(128, 256), dblock)
                r.acc[b, :, :, px] = part.reshape(GROUPS, 16, BLOCK)
        for b in ORDER:

            def slope_group(g, _, b=b, image=image):
                rows = pl.ds(pl.multiple_of(g * 16, 16), 16)
                scale, base, mean = r.pa[b, rows], r.pb[b, rows], r.pm[b, rows]
                s1 = jnp.zeros((16, 128), F32)
                s2 = jnp.zeros((16, 128), F32)
                for h in range(ROWS):
                    px = slice(h * 128, (h + 1) * 128)
                    v = r.g[b, image, g, :, px].astype(F32)
                    zed = v * scale + base
                    sg = sigmoid(zed)
                    dz = r.acc[b, g, :, px] * (sg * (1.0 + zed * (1.0 - sg)))
                    s1 = s1 + dz
                    s2 = s2 + dz * (v - mean)
                    r.act[image, b, g, :, px] = dz.astype(BF16)
                if image == 0:
                    r.s1[b, rows] = s1
                    r.s2[b, rows] = s2
                else:
                    r.s1[b, rows] = jnp.broadcast_to(lane_sum(r.s1[b, rows] + s1), (16, 128))
                    r.s2[b, rows] = jnp.broadcast_to(lane_sum(r.s2[b, rows] + s2), (16, 128)) * (
                        r.pi[b, rows]
                    )
                return 0

            lax.fori_loop(0, GROUPS, slope_group, 0)

    n_d = {b: new(2) for b in ORDER}
    for b in ORDER:
        for image in range(2):

            def low_group(g, _, b=b, image=image):
                rows = pl.ds(pl.multiple_of(g * 16, 16), 16)
                scale, mean = r.pa[b, rows], r.pm[b, rows]
                c1 = -scale * r.s1[b, rows] / count
                c2 = -scale * r.pi[b, rows] * r.s2[b, rows] / count
                for h in range(ROWS):
                    px = slice(h * 128, (h + 1) * 128)
                    v = r.g[b, image, g, :, px].astype(F32)
                    low = scale * r.act[image, b, g, :, px].astype(F32) + ((v - mean) * c2 + c1)
                    r.d[b, image, g, k, :, px] = low.astype(BF16)
                return 0

            lax.fori_loop(0, GROUPS, low_group, 0)
            ref = r.d.at[b, image, :, k]
            send(ref, ref, n_d[b] + image, sibling)

    tile = jnp.zeros((16, 128), F32)
    for b in range(5):
        tile = tile + jnp.where(lane16 == b, r.s2[b, my_rows], 0.0)
        tile = tile + jnp.where(lane16 == 8 + b, r.s1[b, my_rows], 0.0)
    r.dpar[...] = tile

    arrived(r.foth, n_foth, xdev)
    place_shifted(r.foth, 1 - x)
    pooled = jnp.zeros((128, 128), F32)
    for h in range(ROWS):
        pooled = pooled + r.xs[1 - x, 0, 1, :, h * 128 : (h + 1) * 128].astype(F32)
    r.pooled[1 - x] = jnp.broadcast_to(lane_sum(pooled) / PIXELS, (128, 128))

    arrived(r.dpo.at[:, 1 - k], n_dpo, sibling)
    dpo = r.dpo[...].reshape(256, 128)
    pooled = jnp.zeros((128, 128), F32)
    for image in range(2):
        pooled = pooled + split_lanes(r.pooled[image][:, 0:1], (image, image + 2, image + 4))
    r.dwpool[...] = dot_nt(pooled.astype(BF16), dpo)
    spread = dot(r.wpool[...], dpo)
    fg_pool = lane_sum(jnp.where(lane128 == x, spread, 0.0)) / PIXELS

    for b in ORDER:
        for image in range(2):
            arrived(r.d.at[b, image, :, 1 - k], n_d[b] + image, sibling)
        if b == 0:
            total = jnp.zeros((128, 256), F32)
            for image in range(2):
                total = total + dot_nt(r.xs[image, 0, 1], r.d[0, image].reshape(256, PIXELS))
            r.dw1[...] = total
        else:
            met = dict(branch_rows(b))
            for i in range(3):
                where = pl.ds((b - 1) * 9 + 3 * i, 3)
                if i not in met:
                    r.dwa[where] = jnp.zeros((3, 128, 256), F32)
                    continue
                offset = met[i]
                first, last = max(0, -offset), min(ROWS, ROWS - offset)
                there = slice((first + offset) * 128, (last + offset) * 128)
                here = slice(first * 128, last * 128)
                total = jnp.zeros((384, 256), F32)
                for image in range(2):
                    total = total + dot_nt(
                        r.xs[image, b - 1, :, :, there].reshape(384, (last - first) * 128),
                        r.d[b, image, :, :, :, here].reshape(256, (last - first) * 128),
                    )
                r.dwa[where] = total.reshape(3, 128, 256)
        for q in range(PIXELS // BLOCK):
            px = slice(q * BLOCK, (q + 1) * BLOCK)
            if b == 0:
                part = dot(r.w1[...], r.d[0, x, :, :, :, px].reshape(256, BLOCK)) + fg_pool
                r.fga[:, px] = part
                continue
            total = None
            for i, offset in branch_rows(b):
                source = q - offset * COLS // BLOCK
                if source < 0 or source >= PIXELS // BLOCK:
                    continue
                weights = r.wa[pl.ds((b - 1) * 9 + 3 * i, 3)].reshape(384, 256)
                dblock = r.d[b, x, :, :, :, source * BLOCK : (source + 1) * BLOCK]
                part = dot(weights, dblock.reshape(256, BLOCK))
                total = part if total is None else total + part
            rate = atrous_rates[b - 1]
            total = (
                total[128:256]
                + shift_cols(total[0:128], -rate)
                + shift_cols(total[256:384], rate)
            )
            r.fga[:, px] = r.fga[:, px] + total

    for h in range(ROWS):
        r.fg[pl.ds(h, 128, stride=16), :] = r.fga[:, h * 128 : (h + 1) * 128]

    for copy in sent:
        copy.wait_send()


def fused(features, w_one, w_atrous, w_pool, w_proj, gains, biases, out_grad):
    zeros = jnp.zeros((16, 3), F32)
    par = jnp.concatenate([gains.T, zeros, biases.T, jnp.zeros((16, 115), F32)], axis=1)
    vmem = pl.BlockSpec(memory_space=pltpu.VMEM)
    shapes = (
        (256, 128),
        (2048, 128),
        (128, 256),
        (27, 128, 256),
        (128, 256),
        (5, 16, 256),
        (16, 128),
    )
    out, fg, dw1, dwa, dwpool, dwproj, dpar = pl.pallas_call(
        head_kernel,
        out_shape=[jax.ShapeDtypeStruct(s, F32) for s in shapes],
        in_specs=[vmem] * len(INPUTS),
        out_specs=[vmem] * len(OUTPUTS),
        scratch_shapes=list(scratch_table(NSEMS).values()),
        compiler_params=pltpu.CompilerParams(
            collective_id=0, has_side_effects=True, vmem_limit_bytes=64 * 2**20
        ),
    )(
        features.reshape(2048, 128),
        out_grad.reshape(256, 128),
        w_one,
        w_atrous.reshape(27, 128, 256),
        w_pool,
        w_proj,
        par,
    )
    return (
        out.reshape(1, 16, ROWS, COLS),
        fg.reshape(1, 128, ROWS, COLS),
        dw1,
        dwa.reshape(3, 9, 128, 256),
        dwpool,
        dwproj,
        dpar[:, 0:5].T,
        dpar[:, 8:13].T,
    )


def solution(mesh):
    placed = (
        P("dp", "chan", None, None),
        P("chan", None),
        P(None, None, "chan", None),
        P("chan", None),
        P(None, "chan", None),
        P(None, "chan"),
        P(None, "chan"),
        P("dp", "chan", None, None),
    )
    small = mesh.shape["dp"] == 2 and mesh.shape["chan"] == 16
    return jax.shard_map(
        fused if small else local,
        mesh=mesh,
        in_specs=placed,
        out_specs=(
            P("dp", "chan", None, None),
            P("dp", "chan", None, None),
            P("chan", None),
            P(None, None, "chan", None),
            P("chan", None),
            P(None, "chan", None),
            P(None, "chan"),
            P(None, "chan"),
        ),
        check_vma=False,
    )
```

```python
import functools

import jax
import jax.numpy as jnp
from jax import lax
from jax.experimental import pallas as pl
from jax.experimental.pallas import tpu as pltpu
from jax.sharding import PartitionSpec as P

atrous_rates = (6, 12, 18)
norm_eps = 1e-05


def shifted(values, vertical, horizontal):
    margin = max(abs(vertical), abs(horizontal))
    if margin == 0:
        return values
    height = values.shape[-2]
    breadth = values.shape[-1]
    spacing = [(0, 0)] * (values.ndim - 2) + [(margin, margin), (margin, margin)]
    padded = jnp.pad(values, spacing)
    return padded[
        ...,
        margin + vertical : margin + vertical + height,
        margin + horizontal : margin + horizontal + breadth,
    ]


def tap_offsets(dilation):
    return [
        ((along_rows - 1) * dilation, (along_cols - 1) * dilation)
        for along_rows in range(3)
        for along_cols in range(3)
    ]


def make_patches(features, dilation):
    return jnp.stack(
        [shifted(features, vertical, horizontal) for vertical, horizontal in tap_offsets(dilation)]
    )


def silu_slope(values):
    sigmoid = jax.nn.sigmoid(values)
    return sigmoid * (1.0 + values * (1.0 - sigmoid))


def expand_tail(values, extra):
    return values.reshape(values.shape + (1,) * extra)


def local(features, w_one, w_atrous, w_pool, w_proj, gains, biases, out_grad):
    highest = lax.Precision.HIGHEST
    images, local_in, height, columns = features.shape
    pixels = height * columns
    population = images * pixels * lax.axis_size("dp")
    patches = jnp.stack([make_patches(features, dilation) for dilation in atrous_rates])
    pooled = jnp.sum(features, axis=(2, 3), dtype=jnp.float32) / pixels
    one_term = jnp.einsum("nchw,co->onhw", features, w_one, preferred_element_type=jnp.float32)
    rate_terms = jnp.einsum(
        "rtnchw,rtco->ronhw", patches, w_atrous, preferred_element_type=jnp.float32
    )
    spatial_term = jnp.concatenate([one_term[None], rate_terms])
    pool_term = jnp.dot(pooled, w_pool.astype(jnp.float32), precision=highest).T[None]
    branch_pre, pool_pre = (
        lax.psum_scatter(spatial_term, "chan", scatter_dimension=1, tiled=True),
        lax.psum_scatter(pool_term, "chan", scatter_dimension=1, tiled=True),
    )
    branch_totals, branch_squares = lax.psum(
        (jnp.sum(branch_pre, axis=(2, 3, 4)), jnp.sum(branch_pre * branch_pre, axis=(2, 3, 4))),
        "dp",
    )
    branch_mean = branch_totals / population
    branch_inv = lax.rsqrt(branch_squares / population - branch_mean * branch_mean + norm_eps)
    centred = branch_pre - expand_tail(branch_mean, 3)
    branch_z = centred * expand_tail(gains[:4] * branch_inv, 3) + expand_tail(biases[:4], 3)
    branch_hat = centred * expand_tail(branch_inv, 3)
    act_low = jax.nn.silu(branch_z).astype(jnp.bfloat16)
    pool_act = jax.nn.silu(pool_pre).astype(jnp.bfloat16)
    window = w_proj
    spatial = jnp.einsum("bonhw,bod->dnhw", act_low, window[:4], preferred_element_type=jnp.float32)
    pool_part = jnp.einsum("bon,bod->dn", pool_act, window[4:], preferred_element_type=jnp.float32)
    proj_pre = lax.psum_scatter(
        spatial + pool_part[:, :, None, None], "chan", scatter_dimension=0, tiled=True
    )
    proj_totals, proj_squares = lax.psum(
        (jnp.sum(proj_pre, axis=(1, 2, 3)), jnp.sum(proj_pre * proj_pre, axis=(1, 2, 3))), "dp"
    )
    proj_mean = proj_totals / population
    proj_inv = lax.rsqrt(proj_squares / population - proj_mean * proj_mean + norm_eps)
    proj_centred = proj_pre - expand_tail(proj_mean, 3)
    proj_z = proj_centred * expand_tail(gains[4] * proj_inv, 3) + expand_tail(biases[4], 3)
    proj_hat = proj_centred * expand_tail(proj_inv, 3)
    output = jnp.transpose(jax.nn.silu(proj_z), (1, 0, 2, 3))
    grad_out = jnp.transpose(out_grad, (1, 0, 2, 3)).astype(jnp.float32)
    proj_dz = grad_out * silu_slope(proj_z)
    proj_dbias, proj_dgain = lax.psum(
        (jnp.sum(proj_dz, axis=(1, 2, 3)), jnp.sum(proj_dz * proj_hat, axis=(1, 2, 3))), "dp"
    )
    proj_dpre = expand_tail(gains[4] * proj_inv, 3) * (
        proj_dz
        - expand_tail(proj_dbias / population, 3)
        - proj_hat * expand_tail(proj_dgain / population, 3)
    )
    proj_low = proj_dpre.astype(jnp.bfloat16)
    pool_act_wide = pool_act.astype(jnp.float32)
    portion = lax.all_gather(proj_low, "chan", axis=0, tiled=True)
    window = w_proj
    act_grad = jnp.einsum(
        "bod,dnhw->bonhw", window[:4], portion, preferred_element_type=jnp.float32
    )
    portion_sum = jnp.sum(portion, axis=(2, 3), dtype=jnp.float32)
    pool_grad = jnp.einsum(
        "bod,dn->bon", window[4:].astype(jnp.float32), portion_sum, precision=highest
    )
    spatial_part = jnp.einsum(
        "bonhw,dnhw->bod", act_low, portion, preferred_element_type=jnp.float32
    )
    pool_part = jnp.einsum("bon,dn->bod", pool_act_wide, portion_sum, precision=highest)
    weight_grad = jnp.concatenate([spatial_part, pool_part])
    act_grad, pool_grad, proj_wgrad = (act_grad, pool_grad, weight_grad)
    branch_dz = act_grad * silu_slope(branch_z)
    branch_dbias, branch_dgain = lax.psum(
        (jnp.sum(branch_dz, axis=(2, 3, 4)), jnp.sum(branch_dz * branch_hat, axis=(2, 3, 4))), "dp"
    )
    branch_dpre = expand_tail(gains[:4] * branch_inv, 3) * (
        branch_dz
        - expand_tail(branch_dbias / population, 3)
        - branch_hat * expand_tail(branch_dgain / population, 3)
    )
    branch_low = branch_dpre.astype(jnp.bfloat16)
    pool_low = (pool_grad * silu_slope(pool_pre)).astype(jnp.bfloat16)
    spatial_portion = lax.all_gather(branch_low, "chan", axis=1, tiled=True)
    pool_portion = lax.all_gather(pool_low, "chan", axis=1, tiled=True)
    pool_cols = w_pool.astype(jnp.float32)
    feature_grad = jnp.einsum(
        "co,onhw->nchw", w_one, spatial_portion[0], preferred_element_type=jnp.float32
    )
    patch_grad = jnp.einsum(
        "rtco,ronhw->rtnchw", w_atrous, spatial_portion[1:], preferred_element_type=jnp.float32
    )
    pool_wide = pool_portion[0].astype(jnp.float32)
    pooled_grad = jnp.dot(pool_wide.T, pool_cols.T, precision=highest)
    one_piece = jnp.einsum(
        "nchw,onhw->co", features, spatial_portion[0], preferred_element_type=jnp.float32
    )
    rate_piece = jnp.einsum(
        "rtnchw,ronhw->rtco", patches, spatial_portion[1:], preferred_element_type=jnp.float32
    )
    pool_piece = jnp.dot(pooled.T, pool_wide.T, precision=highest)
    one_grad = one_piece
    rate_grad = rate_piece
    pool_wgrad = pool_piece
    feature_grad, patch_grad, pooled_grad, one_grad, rate_grad, pool_wgrad = (
        feature_grad,
        patch_grad,
        pooled_grad,
        one_grad,
        rate_grad,
        pool_wgrad,
    )
    for branch, dilation in enumerate(atrous_rates):
        for tap_index, (vertical, horizontal) in enumerate(tap_offsets(dilation)):
            feature_grad = feature_grad + shifted(
                patch_grad[branch, tap_index], -vertical, -horizontal
            )
    feature_grad = feature_grad + (pooled_grad / pixels)[:, :, None, None]
    one_grad, rate_grad, pool_wgrad, proj_wgrad = (
        lax.psum(one_grad.astype(jnp.bfloat16), "dp").astype(jnp.float32),
        lax.psum(rate_grad.astype(jnp.bfloat16), "dp").astype(jnp.float32),
        lax.psum(pool_wgrad.astype(jnp.bfloat16), "dp").astype(jnp.float32),
        lax.psum(proj_wgrad.astype(jnp.bfloat16), "dp").astype(jnp.float32),
    )
    gains_grad = jnp.concatenate([branch_dgain, proj_dgain[None]])
    biases_grad = jnp.concatenate([branch_dbias, proj_dbias[None]])
    return (
        output,
        feature_grad,
        one_grad,
        rate_grad,
        pool_wgrad,
        proj_wgrad,
        gains_grad,
        biases_grad,
    )


MESH = pl.DeviceIdType.MESH
F32 = jnp.float32
BF16 = jnp.bfloat16
ROWS = 16
COLS = 128
PIXELS = ROWS * COLS
WIDE = PIXELS + 128
CIN_PART = 128
COUT = 256
GROUPS = 8
BLOCK = 256
ORDER = (0, 3, 2, 1)


def branch_rows(branch):
    if branch == 0:
        return [(None, 0)]
    rate = atrous_rates[branch - 1]
    return [(i, (i - 1) * rate) for i in (1, 0, 2) if abs((i - 1) * rate) < ROWS]


def weight_slots():
    slots = {}
    count = 0
    spans = {}
    for branch in ORDER:
        begin = count
        for i, _ in branch_rows(branch):
            slots[(branch, i)] = count
            count += 1 if branch == 0 else 3
        if branch == 0:
            slots["pool"] = count
            count += 1
        spans[branch] = (begin, count)
    return slots, spans, count


SLOTS, SPANS, NSLOTS = weight_slots()


HALVES = 2
SPAN = PIXELS // HALVES
PIECES = [(b, half * SPAN) for b in ORDER for half in range(HALVES)]


def carries_pool(piece):
    return piece == (0, PIXELS - SPAN)


def lanes_of(piece):
    return pl.ds(piece[1], SPAN + (128 if carries_pool(piece) else 0))


def dot(a, b):
    return jnp.dot(a, b, preferred_element_type=F32)


def dot_nt(a, b):
    return lax.dot_general(a, b, (((1,), (1,)), ((), ())), preferred_element_type=F32)


def iota(shape, dim):
    return lax.broadcasted_iota(jnp.int32, shape, dim)


def lane_sum(v):
    return jnp.sum(v, axis=1, keepdims=True)


def split_lanes(column, lanes=(0, 1, 2)):
    high = column.astype(BF16).astype(F32)
    mid = (column - high).astype(BF16).astype(F32)
    low = column - high - mid
    lane = iota((column.shape[0], 128), 1)
    out = jnp.where(lane == lanes[0], high, 0.0)
    out = out + jnp.where(lane == lanes[1], mid, 0.0)
    return out + jnp.where(lane == lanes[2], low, 0.0)


def encode_pair(v):
    lane = iota(v.shape, v.ndim - 1)
    high = v.astype(BF16).astype(F32)
    low = v - high
    return jnp.where(lane == 0, high, jnp.where(lane == 1, low, 0.0)).astype(BF16)


def decode_pair(e):
    return jnp.broadcast_to(jnp.sum(e.astype(F32), axis=-1, keepdims=True), e.shape)


def shift_cols(v, by):
    if by == 0:
        return v
    lane = iota((v.shape[0], 128), 1)
    keep = (lane >= by) if by > 0 else (lane < 128 + by)
    parts = []
    for h in range(v.shape[1] // 128):
        tile = v[:, h * 128 : (h + 1) * 128]
        parts.append(jnp.where(keep, pltpu.roll(tile, by % 128, 1), 0.0))
    return jnp.concatenate(parts, axis=1) if len(parts) > 1 else parts[0]


def sigmoid(z):
    return 0.5 * jnp.tanh(0.5 * z) + 0.5


INPUTS = ("feat", "og", "w1", "wa", "wpool", "wproj", "gains", "biases")
OUTPUTS = ("out", "dwpool", "dwproj", "dgains", "dbiases", "fgb", "dwb")


def scratch_table(sems):
    vm = pltpu.VMEM
    return {
        "feat": vm((2048, 128), BF16),
        "og": vm((256, 128), BF16),
        "w1": vm((128, 256), BF16),
        "wa": vm((27, 128, 256), BF16),
        "wpool": vm((128, 256), BF16),
        "wproj": vm((5, 16, 256), BF16),
        "gains": vm((5, 16), F32),
        "biases": vm((5, 16), F32),
        "fsib": vm((2048, 128), BF16),
        "foth": vm((2048, 128), BF16),
        "x": vm((256, PIXELS), BF16),
        "tw": vm((NSLOTS, GROUPS, 2, 16, 128), BF16),
        "lw": vm((NSLOTS, GROUPS, 16, 256), BF16),
        "acc": vm((4, GROUPS, 16, PIXELS), F32),
        "acp": vm((GROUPS, 16, 128), F32),
        "ys": vm((4, 4, 16, WIDE), BF16),
        "yr": vm((4, 4, 16, WIDE), BF16),
        "zs": vm((4, 4, 16, WIDE), BF16),
        "zr": vm((4, 4, 16, WIDE), BF16),
        "g": vm((4, 2, GROUPS, 16, WIDE), BF16),
        "ogs": vm((2, GROUPS, 16, PIXELS), BF16),
        "pt": vm((GROUPS, 16, 128), F32),
        "wp": vm((GROUPS, 5, 16, 256), BF16),
        "wpt": vm((256, 640), BF16),
        "xv": vm((2, 7, 128, PIXELS), BF16),
        "sl": vm((2, 4, GROUPS, 16, PIXELS), BF16),
        "flip": vm((128, 128), F32),
        "c1": vm((5, 128, 128), F32),
        "c2": vm((5, 128, 128), F32),
        "act": vm((2, 4, GROUPS, 16, PIXELS), BF16),
        "ao": vm((2, 4, 16, PIXELS), BF16),
        "pa": vm((5, 128, 128), F32),
        "pb": vm((5, 128, 128), F32),
        "pm": vm((5, 128, 128), F32),
        "pi": vm((5, 128, 128), F32),
        "s1": vm((5, 128, 128), F32),
        "s2": vm((5, 128, 128), F32),
        "pr": vm((2, GROUPS, 16, PIXELS), F32),
        "dzp": vm((2, GROUPS, 16, PIXELS), F32),
        "dp": vm((2, GROUPS, 2, 16, PIXELS), BF16),
        "dpo": vm((GROUPS, 2, 16, 128), BF16),
        "d": vm((4, 2, GROUPS, 2, 16, PIXELS), BF16),
        "dwv": vm((28, 128, 256), BF16),
        "fga": vm((128, PIXELS), F32),
        "fgv": vm((128, PIXELS), BF16),
        "pooled": vm((2, 128, 128), F32),
        "ppool": vm((2, 128, 128), F32),
        "ss": pltpu.SemaphoreType.DMA((sems,)),
        "rs": pltpu.SemaphoreType.DMA((sems,)),
        "ls": pltpu.SemaphoreType.DMA((32,)),
        "li": pltpu.SemaphoreType.DMA((8,)),
    }


class Refs:
    pass


NSEMS = 224


def head_kernel(*refs):
    names = tuple(n + "_hbm" for n in INPUTS) + OUTPUTS + tuple(scratch_table(NSEMS))
    r = Refs()
    for name, ref in zip(names, refs, strict=True):
        setattr(r, name, ref)
    x = lax.axis_index("dp")
    c = lax.axis_index("chan")
    k = lax.rem(c, 2)
    y = lax.rem(lax.div(c, 2), 2)
    z = lax.div(c, 4)

    def dev(xx, zz, yy, kk):
        return {"dp": xx, "chan": (zz * 2 + yy) * 2 + kk}

    sibling = dev(x, z, y, 1 - k)
    xdev = dev(1 - x, z, y, k)
    ydev = dev(x, z, 1 - y, k)
    zpos = [None] + [lax.rem(z + i, 4) for i in (1, 2, 3)]
    zfrom = [None] + [lax.rem(z + 4 - i, 4) for i in (1, 2, 3)]
    zdev = [None] + [dev(x, zpos[i], y, k) for i in (1, 2, 3)]

    counter = [0]
    sent = []
    due = {}

    def new(n=1):
        first = counter[0]
        counter[0] += n
        assert counter[0] <= NSEMS
        return first

    def rcopy(src, dst, n, device):
        return pltpu.make_async_remote_copy(
            src_ref=src,
            dst_ref=dst,
            send_sem=r.ss.at[n],
            recv_sem=r.rs.at[n],
            device_id=device,
            device_id_type=MESH,
        )

    def send(src, dst, n, device, group=None):
        copy = rcopy(src, dst, n, device)
        copy.start()
        (sent if group is None else group).append(copy)
        due[n] = (dst, device)

    def arrived(ref, n, device):
        del due[n]
        rcopy(ref, ref, n, device).wait_recv()

    barrier = pltpu.get_barrier_semaphore()
    partners = [sibling, xdev, ydev] + zdev[1:]
    for partner in partners:
        pl.semaphore_signal(barrier, inc=1, device_id=partner, device_id_type=MESH)

    loads = {}
    for n, name in enumerate(("feat", "w1", "wpool", "og", "gains", "biases", "wproj", "wa")):
        loads[name] = pltpu.make_async_copy(getattr(r, name + "_hbm"), getattr(r, name), r.li.at[n])
        loads[name].start()

    rr = iota((256, 256), 0)
    cc = iota((256, 256), 1)
    perm = jnp.where(cc == lax.rem(rr, 16) * 16 + lax.div(rr, 16), 1.0, 0.0).astype(BF16)
    eye = jnp.where(rr == cc, 1.0, 0.0).astype(BF16)

    def permuted(ref, block):
        return dot(perm, ref[block * 256 : (block + 1) * 256, :]).astype(BF16)

    def pre_group(yy, zz):
        return yy * 4 + zz

    def own_group(yy, zz):
        return zz * 2 + yy

    class Gather:
        def __init__(self, slot, group, across):
            self.slot, self.group, self.across = slot, group, across
            self.nz, self.ny, self.nx = new(3), new(4), new(8) if across else None

        def start(self):
            mine = self.slot(self.group(y, z))
            for i in (1, 2, 3):
                send(mine, mine, self.nz + i - 1, zdev[i])
            send(mine, mine, self.ny, ydev)
            if self.across:
                send(mine, mine, self.nx, xdev)

        def forward_z(self):
            for i in (1, 2, 3):
                ref = self.slot(self.group(y, zfrom[i]))
                arrived(ref, self.nz + i - 1, zdev[i])
                send(ref, ref, self.ny + i, ydev)
                if self.across:
                    send(ref, ref, self.nx + i, xdev)

        def forward_y(self):
            for i in range(4):
                ref = self.slot(self.group(1 - y, z if i == 0 else zfrom[i]))
                arrived(ref, self.ny + i, ydev)
                if self.across:
                    send(ref, ref, self.nx + 4 + i, xdev)

        def finish(self, other):
            if self.across:
                for i in range(8):
                    yy = y if i < 4 else 1 - y
                    zz = z if i % 4 == 0 else zfrom[i % 4]
                    arrived(other(self.group(yy, zz)), self.nx + i, xdev)

    g_og = Gather(lambda g: r.ogs.at[x, g], own_group, True)
    g_par = Gather(lambda g: r.pt.at[g], own_group, False)
    g_wp = Gather(lambda g: r.wp.at[g], own_group, False)
    g_pre = {}
    for piece in PIECES:
        g_pre[piece] = Gather(
            lambda g, b=piece[0], w=lanes_of(piece): r.g.at[b, x, g, :, w], pre_group, True
        )

    mine = own_group(y, z)
    loads["og"].wait()
    og = permuted(r.og, 0)
    for h in range(ROWS):
        r.ogs[x, mine, :, h * 128 : (h + 1) * 128] = og[h * 16 : (h + 1) * 16]
    r.flip[...] = jnp.zeros((128, 128), F32)
    for name in ("gains", "biases", "wproj"):
        loads[name].wait()
    r.flip[0:5, 0:16] = r.gains[...]
    r.flip[8:13, 0:16] = r.biases[...]
    r.pt[mine] = r.flip[...].T[0:16, :]
    r.wp[mine] = r.wproj[...]

    n_w = {b: new() for b in ORDER}

    def weight_ref(b, i, j):
        return r.w1 if b == 0 else r.wa.at[(b - 1) * 9 + 3 * i + j]

    def transpose_into(slot, ref):
        t = dot_nt(eye, ref[...]).astype(BF16)
        r.tw[slot] = t.reshape(GROUPS, 2, 16, 128)
        r.lw[slot, :, :, 0:128] = r.tw[slot, :, k]

    def prepare_weights(b):
        for i, _ in branch_rows(b):
            slot = SLOTS[(b, i)]
            if b == 0:
                transpose_into(slot, r.w1)
                transpose_into(SLOTS["pool"], r.wpool)
            else:
                for j in range(3):
                    transpose_into(slot + j, weight_ref(b, i, j))

    def send_weights(b):
        lo, hi = SPANS[b]
        send(
            r.tw.at[pl.ds(lo, hi - lo), :, 1 - k],
            r.lw.at[pl.ds(lo, hi - lo), :, :, pl.ds(128, 128)],
            n_w[b],
            sibling,
        )

    def wait_weights(b):
        lo, hi = SPANS[b]
        arrived(r.lw.at[pl.ds(lo, hi - lo), :, :, pl.ds(128, 128)], n_w[b], sibling)

    def place(ref, base):
        for block in range(8):
            t = permuted(ref, block)
            for h in range(ROWS):
                r.x[base + block * 16 : base + (block + 1) * 16, h * 128 : (h + 1) * 128] = t[
                    h * 16 : (h + 1) * 16
                ]

    for name in ("w1", "wpool", "feat"):
        loads[name].wait()
    prepare_weights(0)
    place(r.feat, 0)
    loads["wa"].wait()
    prepare_weights(ORDER[1])

    pl.semaphore_wait(barrier, len(partners))

    n_feat = new()
    n_foth = new()
    send(r.feat, r.fsib, n_feat, sibling)
    send_weights(0)
    send_weights(ORDER[1])
    send(r.feat, r.foth, n_foth, xdev)
    arrived(r.fsib, n_feat, sibling)
    place(r.fsib, 128)

    def convolve(piece):
        b = piece[0]
        for q in range(piece[1] // BLOCK, (piece[1] + SPAN) // BLOCK):
            px = slice(q * BLOCK, (q + 1) * BLOCK)
            total = None
            for i, offset in branch_rows(b):
                source = q + offset * COLS // BLOCK
                if source < 0 or source >= PIXELS // BLOCK:
                    continue
                slot = SLOTS[(b, i)]
                count = 1 if b == 0 else 3
                weights = r.lw[slot : slot + count].reshape(count * 128, 256)
                part = dot(weights, r.x[:, source * BLOCK : (source + 1) * BLOCK])
                total = part if total is None else total + part
            if b:
                rate = atrous_rates[b - 1]
                total = (
                    total[128:256]
                    + shift_cols(total[0:128], rate)
                    + shift_cols(total[256:384], -rate)
                )
            r.acc[b, :, :, px] = total.reshape(GROUPS, 16, BLOCK)
        if carries_pool(piece):
            pooled = jnp.zeros((256, 128), F32)
            for h in range(ROWS):
                pooled = pooled + r.x[:, h * 128 : (h + 1) * 128].astype(F32)
            column = lane_sum(pooled) / PIXELS
            r.pooled[x] = jnp.broadcast_to(column[0:128], (128, 128))
            terms = split_lanes(column).astype(BF16)
            slot = SLOTS["pool"]
            sums = lane_sum(dot(r.lw[slot].reshape(128, 256), terms))
            r.acp[...] = jnp.broadcast_to(sums, (128, 128)).reshape(GROUPS, 16, 128)

    n_ry = {piece: new() for piece in PIECES}
    n_rz = {piece: new(3) for piece in PIECES}

    def reduce_y_send(piece):
        b, w = piece[0], lanes_of(piece)
        px = pl.ds(piece[1], SPAN)
        r.ys[b, :, :, px] = r.acc[b, pl.ds(4 * (1 - y), 4), :, px].astype(BF16)
        if carries_pool(piece):
            r.ys[b, :, :, PIXELS:WIDE] = encode_pair(r.acp[pl.ds(4 * (1 - y), 4)])
        send(r.ys.at[b, :, :, w], r.yr.at[b, :, :, w], n_ry[piece], ydev)

    def reduce_z_send(piece):
        b, w = piece[0], lanes_of(piece)
        px = pl.ds(piece[1], SPAN)
        arrived(r.yr.at[b, :, :, w], n_ry[piece], ydev)
        for i in (2, 1, 3, 0):
            zz = z if i == 0 else zpos[i]
            g = 4 * y + zz
            s = r.acc[b, g, :, px] + r.yr[b, zz, :, px].astype(F32)
            if carries_pool(piece):
                e = r.acp[g] + decode_pair(r.yr[b, zz, :, PIXELS:WIDE])
            if i == 0:
                r.acc[b, g, :, px] = s
                if carries_pool(piece):
                    r.acp[g] = e
            else:
                r.zs[b, i, :, px] = s.astype(BF16)
                if carries_pool(piece):
                    r.zs[b, i, :, PIXELS:WIDE] = encode_pair(e)
                send(r.zs.at[b, i, :, w], r.zr.at[b, i, :, w], n_rz[piece] + i - 1, zdev[i])

    def reduce_finish(piece):
        b, w = piece[0], lanes_of(piece)
        px = pl.ds(piece[1], SPAN)
        g = pre_group(y, z)
        total = r.acc[b, g, :, px]
        extra = r.acp[g] if carries_pool(piece) else None
        for i in (1, 2, 3):
            arrived(r.zr.at[b, i, :, w], n_rz[piece] + i - 1, zdev[i])
            total = total + r.zr[b, i, :, px].astype(F32)
            if carries_pool(piece):
                extra = extra + decode_pair(r.zr[b, i, :, PIXELS:WIDE])
        r.g[b, x, g, :, px] = total.astype(BF16)
        if carries_pool(piece):
            r.g[b, x, g, :, PIXELS:WIDE] = encode_pair(extra)
        g_pre[piece].start()

    def other_pre(piece):
        return lambda g: r.g.at[piece[0], 1 - x, g, :, lanes_of(piece)]

    shift_pairs = []
    lane_r = iota((128, 128), 0)
    lane_c = iota((128, 128), 1)
    for rate in atrous_rates:
        left = jnp.where(lane_r == lane_c - rate, 1.0, 0.0).astype(BF16)
        right = jnp.where(lane_r == lane_c + rate, 1.0, 0.0).astype(BF16)
        shift_pairs.append(jnp.concatenate([left, right], axis=1))

    local = []

    def keep(src, dst):
        copy = pltpu.make_async_copy(src, dst, r.ls.at[len(local)])
        copy.start()
        local.append(copy)

    def place_shifted(ref, image):
        for block in range(8):
            t = permuted(ref, block)
            rows = slice(block * 16, (block + 1) * 16)
            for a in range(3):
                both = dot(t, shift_pairs[a]).astype(BF16)
                for h in range(ROWS):
                    px = slice(h * 128, (h + 1) * 128)
                    hc = slice(h * 16, (h + 1) * 16)
                    if a == 0:
                        r.xv[image, 0, rows, px] = t[hc]
                    r.xv[image, 1 + 2 * a, rows, px] = both[hc, 0:128]
                    r.xv[image, 2 + 2 * a, rows, px] = both[hc, 128:256]

    count = float(2 * PIXELS)

    def each_group(body):
        def step(g, _):
            body(g, pl.ds(pl.multiple_of(g * 16, 16), 16))
            return 0

        lax.fori_loop(0, GROUPS, step, 0)

    tiles = [(image, slice(h * 128, (h + 1) * 128)) for image in range(2) for h in range(ROWS)]
    zero_tile = jnp.zeros((16, 128), F32)

    def spread_lanes(column):
        return jnp.broadcast_to(column, (128, 128))

    def norm_params(b):
        mean = lane_sum(r.s1[b]) / count
        inv = lax.rsqrt(lane_sum(r.s2[b]) / count - mean * mean + norm_eps)
        par = r.pt[...].reshape(128, 128)
        scale = par[:, b : b + 1] * inv
        r.pa[b] = spread_lanes(scale)
        r.pb[b] = spread_lanes(par[:, 8 + b : 9 + b] - mean * scale)
        r.pm[b] = spread_lanes(mean)
        r.pi[b] = spread_lanes(inv)

    def grad_params(b):
        s1 = lane_sum(r.s1[b])
        inv, mean = r.pi[b][:, 0:1], r.pm[b][:, 0:1]
        s2 = (lane_sum(r.s2[b]) - mean * s1) * inv
        scale = r.pa[b][:, 0:1]
        c2 = -scale * inv * s2 / count
        r.s1[b] = spread_lanes(s1)
        r.s2[b] = spread_lanes(s2)
        r.c2[b] = spread_lanes(c2)
        r.c1[b] = spread_lanes(-scale * s1 / count - mean * c2)

    def act_and_slope(zed):
        u = 0.5 * jnp.tanh(0.5 * zed)
        sg = 0.5 + u
        act = zed * sg
        return act, sg + act * (0.5 - u)

    def branch_norm(b):
        def sums(g, rows):
            s, q = zero_tile, zero_tile
            for image, px in tiles:
                v = r.g[b, image, g, :, px].astype(F32)
                s = s + v
                q = q + v * v
            r.s1[b, rows] = s
            r.s2[b, rows] = q

        each_group(sums)
        norm_params(b)

        def apply(g, rows):
            scale, base = r.pa[b, rows], r.pb[b, rows]
            for image, px in tiles:
                act, slope = act_and_slope(r.g[b, image, g, :, px].astype(F32) * scale + base)
                r.act[image, b, g, :, px] = act.astype(BF16)
                r.sl[image, b, g, :, px] = slope.astype(BF16)

        each_group(apply)

    g_par.start()
    g_wp.start()
    steps = len(PIECES)
    for s in range(steps + 4):
        if s < steps:
            b = PIECES[s][0]
            if s % HALVES == 0:
                wait_weights(b)
            convolve(PIECES[s])
            reduce_y_send(PIECES[s])
            if s % HALVES == 0 and s // HALVES + 2 < len(ORDER):
                prepare_weights(ORDER[s // HALVES + 2])
                send_weights(ORDER[s // HALVES + 2])
        if 1 <= s <= steps:
            reduce_z_send(PIECES[s - 1])
        if s == 1:
            g_og.start()
        if s == 2:
            g_par.forward_z()
            g_wp.forward_z()
            g_og.forward_z()
        if 2 <= s <= steps + 1:
            reduce_finish(PIECES[s - 2])
        if s == 4:
            g_par.forward_y()
            g_wp.forward_y()
        if 3 <= s <= steps + 2:
            g_pre[PIECES[s - 3]].forward_z()
        if s >= 4:
            g_pre[PIECES[s - 4]].forward_y()
        if s == steps - 2:
            place_shifted(r.feat, x)
        if s == steps - 1:
            arrived(r.foth, n_foth, xdev)
            place_shifted(r.foth, 1 - x)
    g_og.forward_y()

    for b in range(5):
        r.wpt[:, b * 128 : (b + 1) * 128] = dot_nt(eye, r.wp[:, b].reshape(128, 256)).astype(BF16)

    for piece in PIECES:
        g_pre[piece].finish(other_pre(piece))
        if piece[1] == PIXELS - SPAN:
            branch_norm(piece[0])

    pool_act = []
    lane128 = iota((128, 128), 1)
    pool_cols = jnp.zeros((128, 128), F32)
    for image in range(2):
        pre = decode_pair(r.g[0, image, :, :, PIXELS:WIDE]).reshape(128, 128)
        r.ppool[image] = pre
        pool_cols = pool_cols + jnp.where(lane128 == image, pre * sigmoid(pre), 0.0)
    pool_cols = pool_cols.astype(BF16)
    pool_out = dot(r.wpt[:, 512:640], pool_cols)

    n_pp = new(2)
    pp_sent = []
    for image in range(2):
        column = pool_out[:, image : image + 1]
        for q in range(PIXELS // BLOCK):
            px = slice(q * BLOCK, (q + 1) * BLOCK)
            part = dot(r.wpt[:, 0:512], r.act[image, :, :, :, px].reshape(512, BLOCK)) + column
            part = part.reshape(GROUPS, 2, 16, BLOCK)
            r.acc[2 * image, :, :, px] = part[:, 0]
            r.acc[2 * image + 1, :, :, px] = part[:, 1]
        send(r.acc.at[2 * image + 1 - k], r.pr.at[image], n_pp + image, sibling, pp_sent)

    for image in range(2):
        for b in range(4):
            r.ao[image, b] = r.act[image, b, mine]

    g_og.finish(lambda g: r.ogs.at[1 - x, g])
    for image in range(2):
        arrived(r.pr.at[image], n_pp + image, sibling)

    def proj_sums(g, rows):
        s, q = zero_tile, zero_tile
        for image, px in tiles:
            v = r.acc[2 * image + k, g, :, px] + r.pr[image, g, :, px]
            r.pr[image, g, :, px] = v
            s = s + v
            q = q + v * v
        r.s1[4, rows] = s
        r.s2[4, rows] = q

    each_group(proj_sums)
    norm_params(4)

    def proj_slope(g, rows):
        scale, base = r.pa[4, rows], r.pb[4, rows]
        s1, s2 = zero_tile, zero_tile
        for image, px in tiles:
            v = r.pr[image, g, :, px]
            _, slope = act_and_slope(v * scale + base)
            dz = r.ogs[image, g, :, px].astype(F32) * slope
            r.dzp[image, g, :, px] = dz
            s1 = s1 + dz
            s2 = s2 + dz * v
        r.s1[4, rows] = s1
        r.s2[4, rows] = s2

    each_group(proj_slope)
    grad_params(4)
    n_dp = new(2)
    for image in range(2):

        def proj_low(g, rows, image=image):
            scale, c1, c2 = r.pa[4, rows], r.c1[4, rows], r.c2[4, rows]
            for h in range(ROWS):
                px = slice(h * 128, (h + 1) * 128)
                low = scale * r.dzp[image, g, :, px] + (r.pr[image, g, :, px] * c2 + c1)
                r.dp[image, g, k, :, px] = low.astype(BF16)

        each_group(proj_low)
        ref = r.dp.at[image, :, k]
        send(ref, ref, n_dp + image, sibling)

    my_rows = pl.ds(pl.multiple_of(mine * 16, 16), 16)
    scale, base = r.pa[4, my_rows], r.pb[4, my_rows]
    for h in range(ROWS):
        zed = r.pr[x, mine, :, h * 128 : (h + 1) * 128] * scale + base
        r.out[pl.ds(h, 16, stride=16), :] = zed * sigmoid(zed)

    for image in range(2):
        arrived(r.dp.at[image, :, 1 - k], n_dp + image, sibling)

    for copy in pp_sent:
        copy.wait_send()
    n_d = {b: new(2) for b in ORDER}

    def branch_back(b, turn):
        weights = r.wp[:, b].reshape(128, 256)
        for image in range(2):
            for q in range(PIXELS // 512):
                px = slice(q * 512, (q + 1) * 512)
                back = dot(weights, r.dp[image, :, :, :, px].reshape(256, 512))
                r.acc[2 * turn + image, :, :, px] = back.reshape(GROUPS, 16, 512)

        def slope(g, rows):
            s1, s2 = zero_tile, zero_tile
            for image, px in tiles:
                dz = r.acc[2 * turn + image, g, :, px] * r.sl[image, b, g, :, px].astype(F32)
                r.acc[2 * turn + image, g, :, px] = dz
                s1 = s1 + dz
                s2 = s2 + dz * r.g[b, image, g, :, px].astype(F32)
            r.s1[b, rows] = s1
            r.s2[b, rows] = s2

        each_group(slope)
        grad_params(b)
        for image in range(2):

            def lower(g, rows, image=image):
                scale, c1, c2 = r.pa[b, rows], r.c1[b, rows], r.c2[b, rows]
                for h in range(ROWS):
                    px = slice(h * 128, (h + 1) * 128)
                    v = r.g[b, image, g, :, px].astype(F32)
                    low = scale * r.acc[2 * turn + image, g, :, px] + (v * c2 + c1)
                    r.d[b, image, g, k, :, px] = low.astype(BF16)

            each_group(lower)
            there = r.d.at[b, image, :, k]
            send(there, there, n_d[b] + image, sibling)

    def branch_grads(b, first_branch, last_branch):
        for image in range(2):
            arrived(r.d.at[b, image, :, 1 - k], n_d[b] + image, sibling)
        planes = (2 * b - 1, 0, 2 * b)
        for i, offset in branch_rows(b):
            first, last = max(0, -offset), min(ROWS, ROWS - offset)
            there = slice((first + offset) * 128, (last + offset) * 128)
            here = slice(first * 128, last * 128)
            total = None
            for image in range(2):
                if b == 0:
                    rows = r.xv[image, 0]
                else:
                    rows = jnp.concatenate([r.xv[image, p, :, there] for p in planes], axis=0)
                part = dot_nt(rows, r.d[b, image, :, :, :, here].reshape(256, -1))
                total = part if total is None else total + part
            total = total.astype(BF16)
            if b == 0:
                slot = pl.ds(27, 1)
                r.dwv[27] = total
            else:
                slot = pl.ds((b - 1) * 9 + 3 * i, 3)
                r.dwv[slot] = total.reshape(3, 128, 256)
            keep(r.dwv.at[slot], r.dwb.at[slot])
        for q in range(PIXELS // BLOCK):
            px = slice(q * BLOCK, (q + 1) * BLOCK)
            total = None
            for i, offset in branch_rows(b):
                source = q - offset * COLS // BLOCK
                if source < 0 or source >= PIXELS // BLOCK:
                    continue
                if b == 0:
                    weights = r.w1[...]
                else:
                    weights = r.wa[pl.ds((b - 1) * 9 + 3 * i, 3)].reshape(384, 256)
                dblock = r.d[b, x, :, :, :, source * BLOCK : (source + 1) * BLOCK]
                part = dot(weights, dblock.reshape(256, BLOCK))
                total = part if total is None else total + part
            if b:
                rate = atrous_rates[b - 1]
                total = (
                    total[128:256]
                    + shift_cols(total[0:128], -rate)
                    + shift_cols(total[256:384], rate)
                )
            if not first_branch:
                total = total + r.fga[:, px]
            if last_branch:
                r.fgv[:, px] = (total + fg_pool).astype(BF16)
            else:
                r.fga[:, px] = total

    back_order = (1, 2, 3, 0)
    branch_back(back_order[0], 0)

    ones = jnp.ones((PIXELS, 128), BF16)
    wp4 = r.wp[:, 4].reshape(128, 256)
    dpo = jnp.zeros((128, 128), F32)
    dwp4 = jnp.zeros((16, 256), F32)
    lane16 = iota((16, 128), 1)
    for image in range(2):
        dps = r.dp[image].reshape(256, PIXELS)
        row_sums = dot(dps, ones)[:, 0:1]
        pool_grad = lane_sum(dot(wp4, split_lanes(row_sums).astype(BF16)))
        pre = r.ppool[image][:, 0:1]
        _, slope = act_and_slope(pre)
        low = (pool_grad * slope).astype(BF16).astype(F32)
        for lane in (image, image + 2, image + 4):
            dpo = dpo + jnp.where(lane128 == lane, low, 0.0)
        mine_act, _ = act_and_slope(r.ppool[image, my_rows][:, 0:1])
        mine_act = mine_act.astype(BF16).astype(F32)
        dwp4 = dwp4 + mine_act * dot_nt(jnp.ones((16, PIXELS), BF16), dps)
    r.dwproj[4] = dwp4
    r.dpo[:, k] = dpo.astype(BF16).reshape(GROUPS, 16, 128)
    n_dpo = new()
    ref = r.dpo.at[:, k]
    send(ref, ref, n_dpo, sibling)

    branch_back(back_order[1], 1)
    branch_grads(back_order[0], True, False)
    branch_back(back_order[2], 0)

    dwp = jnp.zeros((64, 256), F32)
    for image in range(2):
        dwp = dwp + dot_nt(r.ao[image].reshape(64, PIXELS), r.dp[image].reshape(256, PIXELS))
    r.dwproj[0:4] = dwp.reshape(4, 16, 256)

    branch_grads(back_order[1], False, False)
    branch_back(back_order[3], 1)

    tile = jnp.zeros((16, 128), F32)
    for b in range(5):
        tile = tile + jnp.where(lane16 == b, r.s2[b, my_rows], 0.0)
        tile = tile + jnp.where(lane16 == 8 + b, r.s1[b, my_rows], 0.0)
    r.flip[0:16, :] = tile
    flipped = r.flip[...].T
    r.dgains[...] = flipped[0:5, 0:16]
    r.dbiases[...] = flipped[8:13, 0:16]

    branch_grads(back_order[2], False, False)

    pooled = jnp.zeros((128, 128), F32)
    for h in range(ROWS):
        pooled = pooled + r.xv[1 - x, 0, :, h * 128 : (h + 1) * 128].astype(F32)
    r.pooled[1 - x] = spread_lanes(lane_sum(pooled) / PIXELS)
    arrived(r.dpo.at[:, 1 - k], n_dpo, sibling)
    dpo = r.dpo[...].reshape(256, 128)
    pooled = jnp.zeros((128, 128), F32)
    for image in range(2):
        pooled = pooled + split_lanes(r.pooled[image][:, 0:1], (image, image + 2, image + 4))
    r.dwpool[...] = dot_nt(pooled.astype(BF16), dpo)
    spread = dot(r.wpool[...], dpo)
    fg_pool = lane_sum(jnp.where(lane128 == x, spread, 0.0)) / PIXELS

    branch_grads(back_order[3], False, True)
    keep(r.fgv, r.fgb)
    for copy in sent:
        copy.wait_send()
    for copy in local:
        copy.wait()


COPY_INPUTS = ("out", "dwpool", "dwproj", "dgains", "dbiases", "fgb", "dwb")
COPY_OUTPUTS = ("out_o", "dwpool_o", "dwproj_o", "dgains_o", "dbiases_o", "fg", "dw1", "dwa")
COPY_SCRATCH = {
    "outv": pltpu.VMEM((256, 128), F32),
    "dwpoolv": pltpu.VMEM((128, 256), F32),
    "dwprojv": pltpu.VMEM((5, 16, 256), F32),
    "fgbv": pltpu.VMEM((128, PIXELS), BF16),
    "dwbv": pltpu.VMEM((28, 128, 256), BF16),
    "fgv": pltpu.VMEM((2048, 128), F32),
    "dwv": pltpu.VMEM((28, 128, 256), F32),
    "si": pltpu.SemaphoreType.DMA((16,)),
    "so": pltpu.SemaphoreType.DMA((16,)),
}


def copy_kernel(*refs):
    r = Refs()
    names = COPY_INPUTS + COPY_OUTPUTS + tuple(COPY_SCRATCH)
    for name, ref in zip(names, refs, strict=True):
        setattr(r, name, ref)
    loads = []
    stores = []

    def load(src, dst):
        copy = pltpu.make_async_copy(src, dst, r.si.at[len(loads)])
        copy.start()
        loads.append(copy)
        return copy

    def store(src, dst):
        copy = pltpu.make_async_copy(src, dst, r.so.at[len(stores)])
        copy.start()
        stores.append(copy)

    met = [
        (b - 1) * 9 + 3 * i for b in (1, 2, 3) for i in range(3) if i in dict(branch_rows(b))
    ]
    taps = [(n, load(r.dwb.at[pl.ds(n, 3)], r.dwbv.at[pl.ds(n, 3)])) for n in met]
    one = load(r.dwb.at[pl.ds(27, 1)], r.dwbv.at[pl.ds(27, 1)])
    fg = load(r.fgb, r.fgbv)
    passed = [
        (load(getattr(r, name), getattr(r, name + "v")), name)
        for name in ("out", "dwpool", "dwproj")
    ]
    r.dgains_o[...] = r.dgains[...]
    r.dbiases_o[...] = r.dbiases[...]
    for n in range(0, 27, 3):
        if n not in met:
            r.dwv[n : n + 3] = jnp.zeros((3, 128, 256), F32)
            store(r.dwv.at[pl.ds(n, 3)], r.dwa.at[pl.ds(n, 3)])
    for n, copy in taps:
        copy.wait()
        r.dwv[n : n + 3] = r.dwbv[n : n + 3].astype(F32)
        store(r.dwv.at[pl.ds(n, 3)], r.dwa.at[pl.ds(n, 3)])
    one.wait()
    r.dwv[27] = r.dwbv[27].astype(F32)
    store(r.dwv.at[27], r.dw1)
    fg.wait()
    for h in range(ROWS):
        r.fgv[pl.ds(h, 128, stride=16), :] = r.fgbv[:, h * 128 : (h + 1) * 128].astype(F32)
    store(r.fgv, r.fg)
    for copy, name in passed:
        copy.wait()
        store(getattr(r, name + "v"), getattr(r, name + "_o"))
    for copy in stores:
        copy.wait()


def fused(features, w_one, w_atrous, w_pool, w_proj, gains, biases, out_grad):
    vmem = pl.BlockSpec(memory_space=pltpu.VMEM)
    hbm = pl.BlockSpec(memory_space=pl.ANY)
    passed = [(256, 128), (128, 256), (5, 16, 256), (5, 16), (5, 16)]
    shapes = [jax.ShapeDtypeStruct(s, F32) for s in passed]
    shapes.append(jax.ShapeDtypeStruct((128, PIXELS), BF16))
    shapes.append(jax.ShapeDtypeStruct((28, 128, 256), BF16))
    parts = pl.pallas_call(
        head_kernel,
        out_shape=shapes,
        in_specs=[hbm] * len(INPUTS),
        out_specs=[vmem] * 5 + [hbm] * 2,
        scratch_shapes=list(scratch_table(NSEMS).values()),
        compiler_params=pltpu.CompilerParams(
            collective_id=0, has_side_effects=True, vmem_limit_bytes=64 * 2**20
        ),
    )(
        features.reshape(2048, 128),
        out_grad.reshape(256, 128),
        w_one,
        w_atrous.reshape(27, 128, 256),
        w_pool,
        w_proj,
        gains,
        biases,
    )
    result = passed + [(2048, 128), (128, 256), (27, 128, 256)]
    out, dwpool, dwproj, dgains, dbiases, fg, dw1, dwa = pl.pallas_call(
        copy_kernel,
        out_shape=[jax.ShapeDtypeStruct(s, F32) for s in result],
        in_specs=[hbm] * 3 + [vmem] * 2 + [hbm] * 2,
        out_specs=[hbm] * 3 + [vmem] * 2 + [hbm] * 3,
        scratch_shapes=list(COPY_SCRATCH.values()),
        compiler_params=pltpu.CompilerParams(vmem_limit_bytes=64 * 2**20),
    )(*parts)
    return (
        out.reshape(1, 16, ROWS, COLS),
        fg.reshape(1, 128, ROWS, COLS),
        dw1,
        dwa.reshape(3, 9, 128, 256),
        dwpool,
        dwproj,
        dgains,
        dbiases,
    )


def solution(mesh):
    placed = (
        P("dp", "chan", None, None),
        P("chan", None),
        P(None, None, "chan", None),
        P("chan", None),
        P(None, "chan", None),
        P(None, "chan"),
        P(None, "chan"),
        P("dp", "chan", None, None),
    )
    small = mesh.shape["dp"] == 2 and mesh.shape["chan"] == 16
    return jax.shard_map(
        fused if small else local,
        mesh=mesh,
        in_specs=placed,
        out_specs=(
            P("dp", "chan", None, None),
            P("dp", "chan", None, None),
            P("chan", None),
            P(None, None, "chan", None),
            P("chan", None),
            P(None, "chan", None),
            P(None, "chan"),
            P(None, "chan"),
        ),
        check_vma=False,
    )
```

```python
import functools

import jax
import jax.numpy as jnp
from jax import lax
from jax.experimental import pallas as pl
from jax.experimental.pallas import tpu as pltpu
from jax.sharding import PartitionSpec as P

atrous_rates = (6, 12, 18)
norm_eps = 1e-05


def shifted(values, vertical, horizontal):
    margin = max(abs(vertical), abs(horizontal))
    if margin == 0:
        return values
    height = values.shape[-2]
    breadth = values.shape[-1]
    spacing = [(0, 0)] * (values.ndim - 2) + [(margin, margin), (margin, margin)]
    padded = jnp.pad(values, spacing)
    return padded[
        ...,
        margin + vertical : margin + vertical + height,
        margin + horizontal : margin + horizontal + breadth,
    ]


def tap_offsets(dilation):
    return [
        ((along_rows - 1) * dilation, (along_cols - 1) * dilation)
        for along_rows in range(3)
        for along_cols in range(3)
    ]


def make_patches(features, dilation):
    return jnp.stack(
        [shifted(features, vertical, horizontal) for vertical, horizontal in tap_offsets(dilation)]
    )


def silu_slope(values):
    sigmoid = jax.nn.sigmoid(values)
    return sigmoid * (1.0 + values * (1.0 - sigmoid))


def expand_tail(values, extra):
    return values.reshape(values.shape + (1,) * extra)


def local(features, w_one, w_atrous, w_pool, w_proj, gains, biases, out_grad):
    highest = lax.Precision.HIGHEST
    images, local_in, height, columns = features.shape
    pixels = height * columns
    population = images * pixels * lax.axis_size("dp")
    patches = jnp.stack([make_patches(features, dilation) for dilation in atrous_rates])
    pooled = jnp.sum(features, axis=(2, 3), dtype=jnp.float32) / pixels
    one_term = jnp.einsum("nchw,co->onhw", features, w_one, preferred_element_type=jnp.float32)
    rate_terms = jnp.einsum(
        "rtnchw,rtco->ronhw", patches, w_atrous, preferred_element_type=jnp.float32
    )
    spatial_term = jnp.concatenate([one_term[None], rate_terms])
    pool_term = jnp.dot(pooled, w_pool.astype(jnp.float32), precision=highest).T[None]
    branch_pre, pool_pre = (
        lax.psum_scatter(spatial_term, "chan", scatter_dimension=1, tiled=True),
        lax.psum_scatter(pool_term, "chan", scatter_dimension=1, tiled=True),
    )
    branch_totals, branch_squares = lax.psum(
        (jnp.sum(branch_pre, axis=(2, 3, 4)), jnp.sum(branch_pre * branch_pre, axis=(2, 3, 4))),
        "dp",
    )
    branch_mean = branch_totals / population
    branch_inv = lax.rsqrt(branch_squares / population - branch_mean * branch_mean + norm_eps)
    centred = branch_pre - expand_tail(branch_mean, 3)
    branch_z = centred * expand_tail(gains[:4] * branch_inv, 3) + expand_tail(biases[:4], 3)
    branch_hat = centred * expand_tail(branch_inv, 3)
    act_low = jax.nn.silu(branch_z).astype(jnp.bfloat16)
    pool_act = jax.nn.silu(pool_pre).astype(jnp.bfloat16)
    window = w_proj
    spatial = jnp.einsum("bonhw,bod->dnhw", act_low, window[:4], preferred_element_type=jnp.float32)
    pool_part = jnp.einsum("bon,bod->dn", pool_act, window[4:], preferred_element_type=jnp.float32)
    proj_pre = lax.psum_scatter(
        spatial + pool_part[:, :, None, None], "chan", scatter_dimension=0, tiled=True
    )
    proj_totals, proj_squares = lax.psum(
        (jnp.sum(proj_pre, axis=(1, 2, 3)), jnp.sum(proj_pre * proj_pre, axis=(1, 2, 3))), "dp"
    )
    proj_mean = proj_totals / population
    proj_inv = lax.rsqrt(proj_squares / population - proj_mean * proj_mean + norm_eps)
    proj_centred = proj_pre - expand_tail(proj_mean, 3)
    proj_z = proj_centred * expand_tail(gains[4] * proj_inv, 3) + expand_tail(biases[4], 3)
    proj_hat = proj_centred * expand_tail(proj_inv, 3)
    output = jnp.transpose(jax.nn.silu(proj_z), (1, 0, 2, 3))
    grad_out = jnp.transpose(out_grad, (1, 0, 2, 3)).astype(jnp.float32)
    proj_dz = grad_out * silu_slope(proj_z)
    proj_dbias, proj_dgain = lax.psum(
        (jnp.sum(proj_dz, axis=(1, 2, 3)), jnp.sum(proj_dz * proj_hat, axis=(1, 2, 3))), "dp"
    )
    proj_dpre = expand_tail(gains[4] * proj_inv, 3) * (
        proj_dz
        - expand_tail(proj_dbias / population, 3)
        - proj_hat * expand_tail(proj_dgain / population, 3)
    )
    proj_low = proj_dpre.astype(jnp.bfloat16)
    pool_act_wide = pool_act.astype(jnp.float32)
    portion = lax.all_gather(proj_low, "chan", axis=0, tiled=True)
    window = w_proj
    act_grad = jnp.einsum(
        "bod,dnhw->bonhw", window[:4], portion, preferred_element_type=jnp.float32
    )
    portion_sum = jnp.sum(portion, axis=(2, 3), dtype=jnp.float32)
    pool_grad = jnp.einsum(
        "bod,dn->bon", window[4:].astype(jnp.float32), portion_sum, precision=highest
    )
    spatial_part = jnp.einsum(
        "bonhw,dnhw->bod", act_low, portion, preferred_element_type=jnp.float32
    )
    pool_part = jnp.einsum("bon,dn->bod", pool_act_wide, portion_sum, precision=highest)
    weight_grad = jnp.concatenate([spatial_part, pool_part])
    act_grad, pool_grad, proj_wgrad = (act_grad, pool_grad, weight_grad)
    branch_dz = act_grad * silu_slope(branch_z)
    branch_dbias, branch_dgain = lax.psum(
        (jnp.sum(branch_dz, axis=(2, 3, 4)), jnp.sum(branch_dz * branch_hat, axis=(2, 3, 4))), "dp"
    )
    branch_dpre = expand_tail(gains[:4] * branch_inv, 3) * (
        branch_dz
        - expand_tail(branch_dbias / population, 3)
        - branch_hat * expand_tail(branch_dgain / population, 3)
    )
    branch_low = branch_dpre.astype(jnp.bfloat16)
    pool_low = (pool_grad * silu_slope(pool_pre)).astype(jnp.bfloat16)
    spatial_portion = lax.all_gather(branch_low, "chan", axis=1, tiled=True)
    pool_portion = lax.all_gather(pool_low, "chan", axis=1, tiled=True)
    pool_cols = w_pool.astype(jnp.float32)
    feature_grad = jnp.einsum(
        "co,onhw->nchw", w_one, spatial_portion[0], preferred_element_type=jnp.float32
    )
    patch_grad = jnp.einsum(
        "rtco,ronhw->rtnchw", w_atrous, spatial_portion[1:], preferred_element_type=jnp.float32
    )
    pool_wide = pool_portion[0].astype(jnp.float32)
    pooled_grad = jnp.dot(pool_wide.T, pool_cols.T, precision=highest)
    one_piece = jnp.einsum(
        "nchw,onhw->co", features, spatial_portion[0], preferred_element_type=jnp.float32
    )
    rate_piece = jnp.einsum(
        "rtnchw,ronhw->rtco", patches, spatial_portion[1:], preferred_element_type=jnp.float32
    )
    pool_piece = jnp.dot(pooled.T, pool_wide.T, precision=highest)
    one_grad = one_piece
    rate_grad = rate_piece
    pool_wgrad = pool_piece
    feature_grad, patch_grad, pooled_grad, one_grad, rate_grad, pool_wgrad = (
        feature_grad,
        patch_grad,
        pooled_grad,
        one_grad,
        rate_grad,
        pool_wgrad,
    )
    for branch, dilation in enumerate(atrous_rates):
        for tap_index, (vertical, horizontal) in enumerate(tap_offsets(dilation)):
            feature_grad = feature_grad + shifted(
                patch_grad[branch, tap_index], -vertical, -horizontal
            )
    feature_grad = feature_grad + (pooled_grad / pixels)[:, :, None, None]
    one_grad, rate_grad, pool_wgrad, proj_wgrad = (
        lax.psum(one_grad.astype(jnp.bfloat16), "dp").astype(jnp.float32),
        lax.psum(rate_grad.astype(jnp.bfloat16), "dp").astype(jnp.float32),
        lax.psum(pool_wgrad.astype(jnp.bfloat16), "dp").astype(jnp.float32),
        lax.psum(proj_wgrad.astype(jnp.bfloat16), "dp").astype(jnp.float32),
    )
    gains_grad = jnp.concatenate([branch_dgain, proj_dgain[None]])
    biases_grad = jnp.concatenate([branch_dbias, proj_dbias[None]])
    return (
        output,
        feature_grad,
        one_grad,
        rate_grad,
        pool_wgrad,
        proj_wgrad,
        gains_grad,
        biases_grad,
    )


MESH = pl.DeviceIdType.MESH
F32 = jnp.float32
BF16 = jnp.bfloat16
ROWS = 16
COLS = 128
PIXELS = ROWS * COLS
WIDE = PIXELS + 128
CIN_PART = 128
COUT = 256
GROUPS = 8
BLOCK = 256
ORDER = (0, 3, 2, 1)


def branch_rows(branch):
    if branch == 0:
        return [(None, 0)]
    rate = atrous_rates[branch - 1]
    return [(i, (i - 1) * rate) for i in (1, 0, 2) if abs((i - 1) * rate) < ROWS]


def weight_slots():
    slots = {}
    count = 0
    spans = {}
    for branch in ORDER:
        begin = count
        for i, _ in branch_rows(branch):
            slots[(branch, i)] = count
            count += 1 if branch == 0 else 3
        if branch == 0:
            slots["pool"] = count
            count += 1
        spans[branch] = (begin, count)
    return slots, spans, count


SLOTS, SPANS, NSLOTS = weight_slots()


HALVES = 2
SPAN = PIXELS // HALVES
PIECES = [(b, half * SPAN) for b in ORDER for half in range(HALVES)]


CROSS_FIRST = PIECES[-2:]


def carries_pool(piece):
    return piece == (0, PIXELS - SPAN)


def lanes_of(piece):
    return pl.ds(piece[1], SPAN + (128 if carries_pool(piece) else 0))


def dot(a, b):
    return jnp.dot(a, b, preferred_element_type=F32)


def dot_nt(a, b):
    return lax.dot_general(a, b, (((1,), (1,)), ((), ())), preferred_element_type=F32)


def iota(shape, dim):
    return lax.broadcasted_iota(jnp.int32, shape, dim)


def lane_sum(v):
    return jnp.sum(v, axis=1, keepdims=True)


def split_lanes(column, lanes=(0, 1, 2)):
    high = column.astype(BF16).astype(F32)
    mid = (column - high).astype(BF16).astype(F32)
    low = column - high - mid
    lane = iota((column.shape[0], 128), 1)
    out = jnp.where(lane == lanes[0], high, 0.0)
    out = out + jnp.where(lane == lanes[1], mid, 0.0)
    return out + jnp.where(lane == lanes[2], low, 0.0)


def encode_pair(v):
    lane = iota(v.shape, v.ndim - 1)
    high = v.astype(BF16).astype(F32)
    low = v - high
    return jnp.where(lane == 0, high, jnp.where(lane == 1, low, 0.0)).astype(BF16)


def decode_pair(e):
    return jnp.broadcast_to(jnp.sum(e.astype(F32), axis=-1, keepdims=True), e.shape)


def shift_cols(v, by):
    if by == 0:
        return v
    lane = iota((v.shape[0], 128), 1)
    keep = (lane >= by) if by > 0 else (lane < 128 + by)
    parts = []
    for h in range(v.shape[1] // 128):
        tile = v[:, h * 128 : (h + 1) * 128]
        parts.append(jnp.where(keep, pltpu.roll(tile, by % 128, 1), 0.0))
    return jnp.concatenate(parts, axis=1) if len(parts) > 1 else parts[0]


def sigmoid(z):
    return 0.5 * jnp.tanh(0.5 * z) + 0.5


INPUTS = ("feat", "og", "w1", "wa", "wpool", "wproj", "gains", "biases")
OUTPUTS = ("out", "dwpool", "dwproj", "dgains", "dbiases", "fgb", "dwb")


def scratch_table(sems):
    vm = pltpu.VMEM
    return {
        "feat": vm((2048, 128), BF16),
        "og": vm((256, 128), BF16),
        "w1": vm((128, 256), BF16),
        "wa": vm((27, 128, 256), BF16),
        "wpool": vm((128, 256), BF16),
        "wproj": vm((5, 16, 256), BF16),
        "gains": vm((5, 16), F32),
        "biases": vm((5, 16), F32),
        "fsib": vm((2048, 128), BF16),
        "foth": vm((2048, 128), BF16),
        "x": vm((256, PIXELS), BF16),
        "tw": vm((NSLOTS, GROUPS, 2, 16, 128), BF16),
        "lw": vm((NSLOTS, GROUPS, 16, 256), BF16),
        "acc": vm((4, GROUPS, 16, PIXELS), F32),
        "acp": vm((GROUPS, 16, 128), F32),
        "ys": vm((4, 4, 16, WIDE), BF16),
        "yr": vm((4, 4, 16, WIDE), BF16),
        "zs": vm((4, 4, 16, WIDE), BF16),
        "zr": vm((4, 4, 16, WIDE), BF16),
        "g": vm((4, 2, GROUPS, 16, WIDE), BF16),
        "ogs": vm((2, GROUPS, 16, PIXELS), BF16),
        "pt": vm((GROUPS, 16, 128), F32),
        "wp": vm((GROUPS, 5, 16, 256), BF16),
        "wpt": vm((256, 640), BF16),
        "wps": vm((GROUPS, 2, 16, 128), BF16),
        "pps": vm((2, GROUPS, 16, PIXELS), BF16),
        "xv": vm((2, 7, 128, PIXELS), BF16),
        "sl": vm((2, 4, GROUPS, 16, PIXELS), BF16),
        "flip": vm((128, 128), F32),
        "c1": vm((5, 128, 128), F32),
        "c2": vm((5, 128, 128), F32),
        "act": vm((2, 4, GROUPS, 16, PIXELS), BF16),
        "ao": vm((2, 4, 16, PIXELS), BF16),
        "pa": vm((5, 128, 128), F32),
        "pb": vm((5, 128, 128), F32),
        "pm": vm((5, 128, 128), F32),
        "pi": vm((5, 128, 128), F32),
        "s1": vm((5, 128, 128), F32),
        "s2": vm((5, 128, 128), F32),
        "pr": vm((2, GROUPS, 16, PIXELS), BF16),
        "dzp": vm((2, GROUPS, 16, PIXELS), F32),
        "dp": vm((2, GROUPS, 2, 16, PIXELS), BF16),
        "dpo": vm((GROUPS, 2, 16, 128), BF16),
        "d": vm((4, 2, GROUPS, 2, 16, PIXELS), BF16),
        "dwv": vm((28, 128, 256), BF16),
        "rsum": vm((GROUPS, 2, 16, 128), F32),
        "fga": vm((128, PIXELS), F32),
        "fgv": vm((128, PIXELS), BF16),
        "pooled": vm((2, 128, 128), F32),
        "ppool": vm((2, 128, 128), F32),
        "ss": pltpu.SemaphoreType.DMA((sems,)),
        "rs": pltpu.SemaphoreType.DMA((sems,)),
        "ls": pltpu.SemaphoreType.DMA((32,)),
        "li": pltpu.SemaphoreType.DMA((8,)),
    }


class Refs:
    pass


NSEMS = 224


def head_kernel(*refs):
    names = tuple(n + "_hbm" for n in INPUTS) + OUTPUTS + tuple(scratch_table(NSEMS))
    r = Refs()
    for name, ref in zip(names, refs, strict=True):
        setattr(r, name, ref)
    x = lax.axis_index("dp")
    c = lax.axis_index("chan")
    k = lax.rem(c, 2)
    y = lax.rem(lax.div(c, 2), 2)
    z = lax.div(c, 4)

    def dev(xx, zz, yy, kk):
        return {"dp": xx, "chan": (zz * 2 + yy) * 2 + kk}

    sibling = dev(x, z, y, 1 - k)
    xdev = dev(1 - x, z, y, k)
    ydev = dev(x, z, 1 - y, k)
    zpos = [None] + [lax.rem(z + i, 4) for i in (1, 2, 3)]
    zfrom = [None] + [lax.rem(z + 4 - i, 4) for i in (1, 2, 3)]
    zdev = [None] + [dev(x, zpos[i], y, k) for i in (1, 2, 3)]

    counter = [0]
    sent = []
    due = {}

    def new(n=1):
        first = counter[0]
        counter[0] += n
        assert counter[0] <= NSEMS
        return first

    def rcopy(src, dst, n, device):
        return pltpu.make_async_remote_copy(
            src_ref=src,
            dst_ref=dst,
            send_sem=r.ss.at[n],
            recv_sem=r.rs.at[n],
            device_id=device,
            device_id_type=MESH,
        )

    def send(src, dst, n, device, group=None):
        copy = rcopy(src, dst, n, device)
        copy.start()
        (sent if group is None else group).append(copy)
        due[n] = (dst, device)

    def arrived(ref, n, device):
        del due[n]
        rcopy(ref, ref, n, device).wait_recv()

    barrier = pltpu.get_barrier_semaphore()
    partners = [sibling, xdev, ydev] + zdev[1:]
    for partner in partners:
        pl.semaphore_signal(barrier, inc=1, device_id=partner, device_id_type=MESH)

    loads = {}
    for n, name in enumerate(("feat", "w1", "wpool", "og", "gains", "biases", "wproj", "wa")):
        loads[name] = pltpu.make_async_copy(getattr(r, name + "_hbm"), getattr(r, name), r.li.at[n])
        loads[name].start()

    rr = iota((256, 256), 0)
    cc = iota((256, 256), 1)
    perm = jnp.where(cc == lax.rem(rr, 16) * 16 + lax.div(rr, 16), 1.0, 0.0).astype(BF16)
    eye = jnp.where(rr == cc, 1.0, 0.0).astype(BF16)

    def permuted(ref, block):
        return dot(perm, ref[block * 256 : (block + 1) * 256, :]).astype(BF16)

    def pre_group(yy, zz):
        return yy * 4 + zz

    def own_group(yy, zz):
        return zz * 2 + yy

    class Gather:
        def __init__(self, slot, group, across):
            self.slot, self.group, self.across = slot, group, across
            self.nz, self.ny, self.nx = new(3), new(4), new(8) if across else None

        def start(self):
            mine = self.slot(self.group(y, z))
            for i in (2, 1, 3):
                send(mine, mine, self.nz + i - 1, zdev[i])
            send(mine, mine, self.ny, ydev)
            if self.across:
                send(mine, mine, self.nx, xdev)

        def forward_z(self):
            for i in (1, 2, 3):
                ref = self.slot(self.group(y, zfrom[i]))
                arrived(ref, self.nz + i - 1, zdev[i])
                send(ref, ref, self.ny + i, ydev)
                if self.across:
                    send(ref, ref, self.nx + i, xdev)

        def forward_y(self):
            for i in range(4):
                ref = self.slot(self.group(1 - y, z if i == 0 else zfrom[i]))
                arrived(ref, self.ny + i, ydev)
                if self.across:
                    send(ref, ref, self.nx + 4 + i, xdev)

        def finish(self, other):
            if self.across:
                for i in range(8):
                    yy = y if i < 4 else 1 - y
                    zz = z if i % 4 == 0 else zfrom[i % 4]
                    arrived(other(self.group(yy, zz)), self.nx + i, xdev)

    g_og = Gather(lambda g: r.ogs.at[x, g], own_group, True)
    g_par = Gather(lambda g: r.pt.at[g], own_group, False)
    g_wp = Gather(lambda g: r.wp.at[g], own_group, False)
    def sums_slot(piece, image):
        return lambda g: r.g.at[piece[0], image, g, :, lanes_of(piece)]

    g_pre = {}
    g_other = {}
    n_cross = {}
    for piece in PIECES:
        g_pre[piece] = Gather(sums_slot(piece, x), pre_group, piece not in CROSS_FIRST)
        if piece in CROSS_FIRST:
            g_other[piece] = Gather(sums_slot(piece, 1 - x), pre_group, False)
            n_cross[piece] = new()

    mine = own_group(y, z)
    loads["og"].wait()
    og = permuted(r.og, 0)
    for h in range(ROWS):
        r.ogs[x, mine, :, h * 128 : (h + 1) * 128] = og[h * 16 : (h + 1) * 16]
    r.flip[...] = jnp.zeros((128, 128), F32)
    for name in ("gains", "biases", "wproj"):
        loads[name].wait()
    r.flip[0:5, 0:16] = r.gains[...]
    r.flip[8:13, 0:16] = r.biases[...]
    r.pt[mine] = r.flip[...].T[0:16, :]
    r.wp[mine] = r.wproj[...]

    n_w = {b: new() for b in ORDER}

    def weight_ref(b, i, j):
        return r.w1 if b == 0 else r.wa.at[(b - 1) * 9 + 3 * i + j]

    def transpose_into(slot, ref):
        t = dot_nt(eye, ref[...]).astype(BF16)
        r.tw[slot] = t.reshape(GROUPS, 2, 16, 128)
        r.lw[slot, :, :, 0:128] = r.tw[slot, :, k]

    def prepare_weights(b):
        for i, _ in branch_rows(b):
            slot = SLOTS[(b, i)]
            if b == 0:
                transpose_into(slot, r.w1)
                transpose_into(SLOTS["pool"], r.wpool)
            else:
                for j in range(3):
                    transpose_into(slot + j, weight_ref(b, i, j))

    def send_weights(b):
        lo, hi = SPANS[b]
        send(
            r.tw.at[pl.ds(lo, hi - lo), :, 1 - k],
            r.lw.at[pl.ds(lo, hi - lo), :, :, pl.ds(128, 128)],
            n_w[b],
            sibling,
        )

    def wait_weights(b):
        lo, hi = SPANS[b]
        arrived(r.lw.at[pl.ds(lo, hi - lo), :, :, pl.ds(128, 128)], n_w[b], sibling)

    def place(ref, base):
        for block in range(8):
            t = permuted(ref, block)
            for h in range(ROWS):
                r.x[base + block * 16 : base + (block + 1) * 16, h * 128 : (h + 1) * 128] = t[
                    h * 16 : (h + 1) * 16
                ]

    for name in ("w1", "wpool", "feat"):
        loads[name].wait()
    prepare_weights(0)
    place(r.feat, 0)
    loads["wa"].wait()
    prepare_weights(ORDER[1])

    pl.semaphore_wait(barrier, len(partners))

    n_feat = new()
    n_foth = new()
    send(r.feat, r.fsib, n_feat, sibling)
    send_weights(0)
    send_weights(ORDER[1])
    send(r.feat, r.foth, n_foth, xdev)
    arrived(r.fsib, n_feat, sibling)
    place(r.fsib, 128)

    def convolve(piece):
        b = piece[0]
        for q in range(piece[1] // BLOCK, (piece[1] + SPAN) // BLOCK):
            px = slice(q * BLOCK, (q + 1) * BLOCK)
            total = None
            for i, offset in branch_rows(b):
                source = q + offset * COLS // BLOCK
                if source < 0 or source >= PIXELS // BLOCK:
                    continue
                slot = SLOTS[(b, i)]
                count = 1 if b == 0 else 3
                weights = r.lw[slot : slot + count].reshape(count * 128, 256)
                part = dot(weights, r.x[:, source * BLOCK : (source + 1) * BLOCK])
                total = part if total is None else total + part
            if b:
                rate = atrous_rates[b - 1]
                total = (
                    total[128:256]
                    + shift_cols(total[0:128], rate)
                    + shift_cols(total[256:384], -rate)
                )
            r.acc[b, :, :, px] = total.reshape(GROUPS, 16, BLOCK)
        if carries_pool(piece):
            pooled = jnp.zeros((256, 128), F32)
            for h in range(ROWS):
                pooled = pooled + r.x[:, h * 128 : (h + 1) * 128].astype(F32)
            column = lane_sum(pooled) / PIXELS
            r.pooled[x] = jnp.broadcast_to(column[0:128], (128, 128))
            terms = split_lanes(column).astype(BF16)
            slot = SLOTS["pool"]
            sums = lane_sum(dot(r.lw[slot].reshape(128, 256), terms))
            r.acp[...] = jnp.broadcast_to(sums, (128, 128)).reshape(GROUPS, 16, 128)

    n_ry = {piece: new() for piece in PIECES}
    n_rz = {piece: new(3) for piece in PIECES}

    def reduce_y_send(piece):
        b, w = piece[0], lanes_of(piece)
        px = pl.ds(piece[1], SPAN)
        r.ys[b, :, :, px] = r.acc[b, pl.ds(4 * (1 - y), 4), :, px].astype(BF16)
        if carries_pool(piece):
            r.ys[b, :, :, PIXELS:WIDE] = encode_pair(r.acp[pl.ds(4 * (1 - y), 4)])
        send(r.ys.at[b, :, :, w], r.yr.at[b, :, :, w], n_ry[piece], ydev)

    def reduce_z_send(piece):
        b, w = piece[0], lanes_of(piece)
        px = pl.ds(piece[1], SPAN)
        arrived(r.yr.at[b, :, :, w], n_ry[piece], ydev)
        for i in (2, 1, 3, 0):
            zz = z if i == 0 else zpos[i]
            g = 4 * y + zz
            s = r.acc[b, g, :, px] + r.yr[b, zz, :, px].astype(F32)
            if carries_pool(piece):
                e = r.acp[g] + decode_pair(r.yr[b, zz, :, PIXELS:WIDE])
            if i == 0:
                r.acc[b, g, :, px] = s
                if carries_pool(piece):
                    r.acp[g] = e
            else:
                r.zs[b, i, :, px] = s.astype(BF16)
                if carries_pool(piece):
                    r.zs[b, i, :, PIXELS:WIDE] = encode_pair(e)
                send(r.zs.at[b, i, :, w], r.zr.at[b, i, :, w], n_rz[piece] + i - 1, zdev[i])

    def reduce_finish(piece):
        b, w = piece[0], lanes_of(piece)
        px = pl.ds(piece[1], SPAN)
        g = pre_group(y, z)
        total = r.acc[b, g, :, px]
        extra = r.acp[g] if carries_pool(piece) else None
        for i in (1, 2, 3):
            arrived(r.zr.at[b, i, :, w], n_rz[piece] + i - 1, zdev[i])
            total = total + r.zr[b, i, :, px].astype(F32)
            if carries_pool(piece):
                extra = extra + decode_pair(r.zr[b, i, :, PIXELS:WIDE])
        r.g[b, x, g, :, px] = total.astype(BF16)
        if carries_pool(piece):
            r.g[b, x, g, :, PIXELS:WIDE] = encode_pair(extra)
        g_pre[piece].start()
        if piece in CROSS_FIRST:
            ref = sums_slot(piece, x)(g)
            send(ref, ref, n_cross[piece], xdev)

    def cross(piece):
        arrived(sums_slot(piece, 1 - x)(pre_group(y, z)), n_cross[piece], xdev)
        g_other[piece].start()

    shift_pairs = []
    lane_r = iota((128, 128), 0)
    lane_c = iota((128, 128), 1)
    for rate in atrous_rates:
        left = jnp.where(lane_r == lane_c - rate, 1.0, 0.0).astype(BF16)
        right = jnp.where(lane_r == lane_c + rate, 1.0, 0.0).astype(BF16)
        shift_pairs.append(jnp.concatenate([left, right], axis=1))

    local = []

    def keep(src, dst):
        copy = pltpu.make_async_copy(src, dst, r.ls.at[len(local)])
        copy.start()
        local.append(copy)

    def place_shifted(ref, image):
        for block in range(8):
            t = permuted(ref, block)
            rows = slice(block * 16, (block + 1) * 16)
            for a in range(3):
                both = dot(t, shift_pairs[a]).astype(BF16)
                for h in range(ROWS):
                    px = slice(h * 128, (h + 1) * 128)
                    hc = slice(h * 16, (h + 1) * 16)
                    if a == 0:
                        r.xv[image, 0, rows, px] = t[hc]
                    r.xv[image, 1 + 2 * a, rows, px] = both[hc, 0:128]
                    r.xv[image, 2 + 2 * a, rows, px] = both[hc, 128:256]

    count = float(2 * PIXELS)

    def each_group(body):
        def step(g, _):
            body(g, pl.ds(pl.multiple_of(g * 16, 16), 16))
            return 0

        lax.fori_loop(0, GROUPS, step, 0)

    tiles = [(image, slice(h * 128, (h + 1) * 128)) for image in range(2) for h in range(ROWS)]
    zero_tile = jnp.zeros((16, 128), F32)

    def spread_lanes(column):
        return jnp.broadcast_to(column, (128, 128))

    def norm_params(b):
        mean = lane_sum(r.s1[b]) / count
        inv = lax.rsqrt(lane_sum(r.s2[b]) / count - mean * mean + norm_eps)
        par = r.pt[...].reshape(128, 128)
        scale = par[:, b : b + 1] * inv
        r.pa[b] = spread_lanes(scale)
        r.pb[b] = spread_lanes(par[:, 8 + b : 9 + b] - mean * scale)
        r.pm[b] = spread_lanes(mean)
        r.pi[b] = spread_lanes(inv)

    def grad_params(b):
        s1 = lane_sum(r.s1[b])
        inv, mean = r.pi[b][:, 0:1], r.pm[b][:, 0:1]
        s2 = (lane_sum(r.s2[b]) - mean * s1) * inv
        scale = r.pa[b][:, 0:1]
        c2 = -scale * inv * s2 / count
        r.s1[b] = spread_lanes(s1)
        r.s2[b] = spread_lanes(s2)
        r.c2[b] = spread_lanes(c2)
        r.c1[b] = spread_lanes(-scale * s1 / count - mean * c2)

    def act_and_slope(zed):
        u = 0.5 * jnp.tanh(0.5 * zed)
        sg = 0.5 + u
        act = zed * sg
        return act, sg + act * (0.5 - u)

    def branch_norm(b):
        def sums(g, rows):
            s, q = zero_tile, zero_tile
            for image, px in tiles:
                v = r.g[b, image, g, :, px].astype(F32)
                s = s + v
                q = q + v * v
            r.s1[b, rows] = s
            r.s2[b, rows] = q

        each_group(sums)
        norm_params(b)

        def apply(g, rows):
            scale, base = r.pa[b, rows], r.pb[b, rows]
            for image, px in tiles:
                act, slope = act_and_slope(r.g[b, image, g, :, px].astype(F32) * scale + base)
                r.act[image, b, g, :, px] = act.astype(BF16)
                r.sl[image, b, g, :, px] = slope.astype(BF16)

        each_group(apply)

    g_par.start()
    g_wp.start()
    steps = len(PIECES)
    for s in range(steps + 6):
        if s < steps:
            b = PIECES[s][0]
            if s % HALVES == 0:
                wait_weights(b)
            convolve(PIECES[s])
            reduce_y_send(PIECES[s])
            if s % HALVES == 0 and s // HALVES + 2 < len(ORDER):
                prepare_weights(ORDER[s // HALVES + 2])
                send_weights(ORDER[s // HALVES + 2])
        if s == 0:
            g_og.start()
        if 0 <= s - 2 < steps:
            reduce_z_send(PIECES[s - 2])
        if s == 2:
            g_par.forward_z()
            g_wp.forward_z()
            g_og.forward_z()
        if 0 <= s - 3 < steps:
            reduce_finish(PIECES[s - 3])
        if s == 4:
            g_par.forward_y()
            g_wp.forward_y()
            g_og.forward_y()
        if 0 <= s - 5 < steps:
            g_pre[PIECES[s - 5]].forward_z()
            if PIECES[s - 5] in CROSS_FIRST:
                cross(PIECES[s - 5])
        if 0 <= s - 6 < steps:
            if PIECES[s - 6] in CROSS_FIRST:
                g_other[PIECES[s - 6]].forward_z()
            else:
                g_pre[PIECES[s - 6]].forward_y()
        if s == 6:
            place_shifted(r.feat, x)
        if s == 7:
            arrived(r.foth, n_foth, xdev)
            place_shifted(r.foth, 1 - x)

    for b in range(5):
        flat = dot_nt(eye, r.wp[:, b].reshape(128, 256)).astype(BF16)
        r.wps[...] = flat.reshape(GROUPS, 2, 16, 128)
        r.wpt[0:128, b * 128 : (b + 1) * 128] = r.wps[:, k].reshape(128, 128)
        r.wpt[128:256, b * 128 : (b + 1) * 128] = r.wps[:, 1 - k].reshape(128, 128)

    for piece in PIECES:
        if piece in CROSS_FIRST:
            g_pre[piece].forward_y()
            g_other[piece].forward_y()
        else:
            g_pre[piece].finish(sums_slot(piece, 1 - x))
        if piece[1] == PIXELS - SPAN:
            branch_norm(piece[0])

    pool_act = []
    lane128 = iota((128, 128), 1)
    pool_cols = jnp.zeros((128, 128), F32)
    for image in range(2):
        pre = decode_pair(r.g[0, image, :, :, PIXELS:WIDE]).reshape(128, 128)
        r.ppool[image] = pre
        pool_cols = pool_cols + jnp.where(lane128 == image, pre * sigmoid(pre), 0.0)
    pool_cols = pool_cols.astype(BF16)
    pool_out = dot(r.wpt[:, 512:640], pool_cols)

    n_pp = new(2)
    for image in range(2):
        column = pool_out[:, image : image + 1]
        for q in range(PIXELS // BLOCK):
            px = slice(q * BLOCK, (q + 1) * BLOCK)
            part = dot(r.wpt[:, 0:512], r.act[image, :, :, :, px].reshape(512, BLOCK)) + column
            r.acc[image, :, :, px] = part[0:128].reshape(GROUPS, 16, BLOCK)
            r.pps[image, :, :, px] = part[128:256].astype(BF16).reshape(GROUPS, 16, BLOCK)
        send(r.pps.at[image], r.pr.at[image], n_pp + image, sibling)

    for image in range(2):
        for b in range(4):
            r.ao[image, b] = r.act[image, b, mine]

    g_og.finish(lambda g: r.ogs.at[1 - x, g])
    for image in range(2):
        arrived(r.pr.at[image], n_pp + image, sibling)

    def proj_sums(g, rows):
        s, q = zero_tile, zero_tile
        for image, px in tiles:
            v = r.acc[image, g, :, px] + r.pr[image, g, :, px].astype(F32)
            r.acc[image, g, :, px] = v
            s = s + v
            q = q + v * v
        r.s1[4, rows] = s
        r.s2[4, rows] = q

    each_group(proj_sums)
    norm_params(4)

    def proj_slope(g, rows):
        scale, base = r.pa[4, rows], r.pb[4, rows]
        s1, s2 = zero_tile, zero_tile
        for image, px in tiles:
            v = r.acc[image, g, :, px]
            _, slope = act_and_slope(v * scale + base)
            dz = r.ogs[image, g, :, px].astype(F32) * slope
            r.dzp[image, g, :, px] = dz
            s1 = s1 + dz
            s2 = s2 + dz * v
        r.s1[4, rows] = s1
        r.s2[4, rows] = s2

    each_group(proj_slope)
    grad_params(4)
    n_dp = new(2)
    for image in range(2):

        def proj_low(g, rows, image=image):
            scale, c1, c2 = r.pa[4, rows], r.c1[4, rows], r.c2[4, rows]
            total = zero_tile
            for h in range(ROWS):
                px = slice(h * 128, (h + 1) * 128)
                low = scale * r.dzp[image, g, :, px] + (r.acc[image, g, :, px] * c2 + c1)
                low = low.astype(BF16)
                r.dp[image, g, k, :, px] = low
                total = total + low.astype(F32)
            r.s1[image, rows] = total

        each_group(proj_low)
        ref = r.dp.at[image, :, k]
        send(ref, ref, n_dp + image, sibling)

    n_rsum = new()
    row_sums = jnp.where(lane128 == 0, lane_sum(r.s1[0]), 0.0)
    row_sums = row_sums + jnp.where(lane128 == 1, lane_sum(r.s1[1]), 0.0)
    r.rsum[:, k] = row_sums.reshape(GROUPS, 16, 128)
    ref = r.rsum.at[:, k]
    send(ref, ref, n_rsum, sibling)

    my_rows = pl.ds(pl.multiple_of(mine * 16, 16), 16)
    scale, base = r.pa[4, my_rows], r.pb[4, my_rows]
    for h in range(ROWS):
        zed = r.acc[x, mine, :, h * 128 : (h + 1) * 128] * scale + base
        r.out[pl.ds(h, 16, stride=16), :] = zed * sigmoid(zed)

    for image in range(2):
        arrived(r.dp.at[image, :, 1 - k], n_dp + image, sibling)

    n_d = {b: new(2) for b in ORDER}

    def back_block(b, turn, image, q):
        px = slice(q * 512, (q + 1) * 512)
        dblock = r.dp[image, :, :, :, px].reshape(256, 512)
        back = dot(r.wp[:, b].reshape(128, 256), dblock)
        r.acc[2 * turn + image, :, :, px] = back.reshape(GROUPS, 16, 512)

    def branch_back(b, turn):
        for image in range(2):
            for q in range(PIXELS // 512):
                back_block(b, turn, image, q)

        def slope(g, rows):
            s1, s2 = zero_tile, zero_tile
            for image, px in tiles:
                dz = r.acc[2 * turn + image, g, :, px] * r.sl[image, b, g, :, px].astype(F32)
                r.acc[2 * turn + image, g, :, px] = dz
                s1 = s1 + dz
                s2 = s2 + dz * r.g[b, image, g, :, px].astype(F32)
            r.s1[b, rows] = s1
            r.s2[b, rows] = s2

        each_group(slope)
        grad_params(b)
        for image in range(2):

            def lower(g, rows, image=image):
                scale, c1, c2 = r.pa[b, rows], r.c1[b, rows], r.c2[b, rows]
                for h in range(ROWS):
                    px = slice(h * 128, (h + 1) * 128)
                    v = r.g[b, image, g, :, px].astype(F32)
                    low = scale * r.acc[2 * turn + image, g, :, px] + (v * c2 + c1)
                    r.d[b, image, g, k, :, px] = low.astype(BF16)

            each_group(lower)
            there = r.d.at[b, image, :, k]
            send(there, there, n_d[b] + image, sibling)

    def branch_grads(b, first_branch, last_branch):
        for image in range(2):
            arrived(r.d.at[b, image, :, 1 - k], n_d[b] + image, sibling)
        planes = (2 * b - 1, 0, 2 * b)
        for i, offset in branch_rows(b):
            first, last = max(0, -offset), min(ROWS, ROWS - offset)
            there = slice((first + offset) * 128, (last + offset) * 128)
            here = slice(first * 128, last * 128)
            total = None
            for image in range(2):
                if b == 0:
                    rows = r.xv[image, 0]
                else:
                    rows = jnp.concatenate([r.xv[image, p, :, there] for p in planes], axis=0)
                part = dot_nt(rows, r.d[b, image, :, :, :, here].reshape(256, -1))
                total = part if total is None else total + part
            total = total.astype(BF16)
            if b == 0:
                slot = pl.ds(27, 1)
                r.dwv[27] = total
            else:
                slot = pl.ds((b - 1) * 9 + 3 * i, 3)
                r.dwv[slot] = total.reshape(3, 128, 256)
            keep(r.dwv.at[slot], r.dwb.at[slot])
        for q in range(PIXELS // BLOCK):
            px = slice(q * BLOCK, (q + 1) * BLOCK)
            total = None
            for i, offset in branch_rows(b):
                source = q - offset * COLS // BLOCK
                if source < 0 or source >= PIXELS // BLOCK:
                    continue
                if b == 0:
                    weights = r.w1[...]
                else:
                    weights = r.wa[pl.ds((b - 1) * 9 + 3 * i, 3)].reshape(384, 256)
                dblock = r.d[b, x, :, :, :, source * BLOCK : (source + 1) * BLOCK]
                part = dot(weights, dblock.reshape(256, BLOCK))
                total = part if total is None else total + part
            if b:
                rate = atrous_rates[b - 1]
                total = (
                    total[128:256]
                    + shift_cols(total[0:128], -rate)
                    + shift_cols(total[256:384], rate)
                )
            if not first_branch:
                total = total + r.fga[:, px]
            if last_branch:
                r.fgv[:, px] = (total + fg_pool).astype(BF16)
            else:
                r.fga[:, px] = total

    back_order = (1, 2, 3, 0)
    for n, b in enumerate(back_order):
        branch_back(b, n % 2)
    branch_grads(back_order[0], True, False)

    arrived(r.rsum.at[:, 1 - k], n_rsum, sibling)
    wp4 = r.wp[:, 4].reshape(128, 256)
    dpo = jnp.zeros((128, 128), F32)
    dwp4 = jnp.zeros((16, 256), F32)
    lane16 = iota((16, 128), 1)
    for image in range(2):
        terms = split_lanes(r.rsum[...].reshape(256, 128)[:, image : image + 1]).astype(BF16)
        pool_grad = lane_sum(dot(wp4, terms))
        pre = r.ppool[image][:, 0:1]
        _, slope = act_and_slope(pre)
        low = (pool_grad * slope).astype(BF16).astype(F32)
        for lane in (image, image + 2, image + 4):
            dpo = dpo + jnp.where(lane128 == lane, low, 0.0)
        mine_act, _ = act_and_slope(r.ppool[image, my_rows][:, 0:1])
        mine_act = mine_act.astype(BF16).astype(F32)
        dwp4 = dwp4 + mine_act * dot_nt(jnp.ones((16, 128), BF16), terms)
    r.dwproj[4] = dwp4
    r.dpo[:, k] = dpo.astype(BF16).reshape(GROUPS, 16, 128)
    n_dpo = new()
    ref = r.dpo.at[:, k]
    send(ref, ref, n_dpo, sibling)

    branch_grads(back_order[1], False, False)

    dwp = jnp.zeros((64, 256), F32)
    for image in range(2):
        dwp = dwp + dot_nt(r.ao[image].reshape(64, PIXELS), r.dp[image].reshape(256, PIXELS))
    r.dwproj[0:4] = dwp.reshape(4, 16, 256)

    tile = jnp.zeros((16, 128), F32)
    for b in range(5):
        tile = tile + jnp.where(lane16 == b, r.s2[b, my_rows], 0.0)
        tile = tile + jnp.where(lane16 == 8 + b, r.s1[b, my_rows], 0.0)
    r.flip[0:16, :] = tile
    flipped = r.flip[...].T
    r.dgains[...] = flipped[0:5, 0:16]
    r.dbiases[...] = flipped[8:13, 0:16]

    branch_grads(back_order[2], False, False)

    pooled = jnp.zeros((128, 128), F32)
    for h in range(ROWS):
        pooled = pooled + r.xv[1 - x, 0, :, h * 128 : (h + 1) * 128].astype(F32)
    r.pooled[1 - x] = spread_lanes(lane_sum(pooled) / PIXELS)
    arrived(r.dpo.at[:, 1 - k], n_dpo, sibling)
    dpo = r.dpo[...].reshape(256, 128)
    pooled = jnp.zeros((128, 128), F32)
    for image in range(2):
        pooled = pooled + split_lanes(r.pooled[image][:, 0:1], (image, image + 2, image + 4))
    r.dwpool[...] = dot_nt(pooled.astype(BF16), dpo)
    spread = dot(r.wpool[...], dpo)
    fg_pool = lane_sum(jnp.where(lane128 == x, spread, 0.0)) / PIXELS

    branch_grads(back_order[3], False, True)
    keep(r.fgv, r.fgb)
    for copy in sent:
        copy.wait_send()
    for copy in local:
        copy.wait()


COPY_INPUTS = ("out", "dwpool", "dwproj", "dgains", "dbiases", "fgb", "dwb")
COPY_OUTPUTS = ("out_o", "dwpool_o", "dwproj_o", "dgains_o", "dbiases_o", "fg", "dw1", "dwa")
COPY_SCRATCH = {
    "outv": pltpu.VMEM((256, 128), F32),
    "dwpoolv": pltpu.VMEM((128, 256), F32),
    "dwprojv": pltpu.VMEM((5, 16, 256), F32),
    "fgbv": pltpu.VMEM((128, PIXELS), BF16),
    "dwbv": pltpu.VMEM((28, 128, 256), BF16),
    "fgv": pltpu.VMEM((2048, 128), F32),
    "dwv": pltpu.VMEM((28, 128, 256), F32),
    "si": pltpu.SemaphoreType.DMA((16,)),
    "so": pltpu.SemaphoreType.DMA((16,)),
}


def copy_kernel(*refs):
    r = Refs()
    names = COPY_INPUTS + COPY_OUTPUTS + tuple(COPY_SCRATCH)
    for name, ref in zip(names, refs, strict=True):
        setattr(r, name, ref)
    loads = []
    stores = []

    def load(src, dst):
        copy = pltpu.make_async_copy(src, dst, r.si.at[len(loads)])
        copy.start()
        loads.append(copy)
        return copy

    def store(src, dst):
        copy = pltpu.make_async_copy(src, dst, r.so.at[len(stores)])
        copy.start()
        stores.append(copy)

    met = [
        (b - 1) * 9 + 3 * i for b in (1, 2, 3) for i in range(3) if i in dict(branch_rows(b))
    ]
    taps = [(n, load(r.dwb.at[pl.ds(n, 3)], r.dwbv.at[pl.ds(n, 3)])) for n in met]
    one = load(r.dwb.at[pl.ds(27, 1)], r.dwbv.at[pl.ds(27, 1)])
    fg = load(r.fgb, r.fgbv)
    passed = [
        (load(getattr(r, name), getattr(r, name + "v")), name)
        for name in ("out", "dwpool", "dwproj")
    ]
    r.dgains_o[...] = r.dgains[...]
    r.dbiases_o[...] = r.dbiases[...]
    for n in range(0, 27, 3):
        if n not in met:
            r.dwv[n : n + 3] = jnp.zeros((3, 128, 256), F32)
            store(r.dwv.at[pl.ds(n, 3)], r.dwa.at[pl.ds(n, 3)])
    for n, copy in taps:
        copy.wait()
        r.dwv[n : n + 3] = r.dwbv[n : n + 3].astype(F32)
        store(r.dwv.at[pl.ds(n, 3)], r.dwa.at[pl.ds(n, 3)])
    one.wait()
    r.dwv[27] = r.dwbv[27].astype(F32)
    store(r.dwv.at[27], r.dw1)
    fg.wait()
    for h in range(ROWS):
        r.fgv[pl.ds(h, 128, stride=16), :] = r.fgbv[:, h * 128 : (h + 1) * 128].astype(F32)
    store(r.fgv, r.fg)
    for copy, name in passed:
        copy.wait()
        store(getattr(r, name + "v"), getattr(r, name + "_o"))
    for copy in stores:
        copy.wait()


def fused(features, w_one, w_atrous, w_pool, w_proj, gains, biases, out_grad):
    vmem = pl.BlockSpec(memory_space=pltpu.VMEM)
    hbm = pl.BlockSpec(memory_space=pl.ANY)
    passed = [(256, 128), (128, 256), (5, 16, 256), (5, 16), (5, 16)]
    shapes = [jax.ShapeDtypeStruct(s, F32) for s in passed]
    shapes.append(jax.ShapeDtypeStruct((128, PIXELS), BF16))
    shapes.append(jax.ShapeDtypeStruct((28, 128, 256), BF16))
    parts = pl.pallas_call(
        head_kernel,
        out_shape=shapes,
        in_specs=[hbm] * len(INPUTS),
        out_specs=[vmem] * 5 + [hbm] * 2,
        scratch_shapes=list(scratch_table(NSEMS).values()),
        compiler_params=pltpu.CompilerParams(
            collective_id=0, has_side_effects=True, vmem_limit_bytes=64 * 2**20
        ),
    )(
        features.reshape(2048, 128),
        out_grad.reshape(256, 128),
        w_one,
        w_atrous.reshape(27, 128, 256),
        w_pool,
        w_proj,
        gains,
        biases,
    )
    result = passed + [(2048, 128), (128, 256), (27, 128, 256)]
    out, dwpool, dwproj, dgains, dbiases, fg, dw1, dwa = pl.pallas_call(
        copy_kernel,
        out_shape=[jax.ShapeDtypeStruct(s, F32) for s in result],
        in_specs=[hbm] * 3 + [vmem] * 2 + [hbm] * 2,
        out_specs=[hbm] * 3 + [vmem] * 2 + [hbm] * 3,
        scratch_shapes=list(COPY_SCRATCH.values()),
        compiler_params=pltpu.CompilerParams(vmem_limit_bytes=64 * 2**20),
    )(*parts)
    return (
        out.reshape(1, 16, ROWS, COLS),
        fg.reshape(1, 128, ROWS, COLS),
        dw1,
        dwa.reshape(3, 9, 128, 256),
        dwpool,
        dwproj,
        dgains,
        dbiases,
    )


def solution(mesh):
    placed = (
        P("dp", "chan", None, None),
        P("chan", None),
        P(None, None, "chan", None),
        P("chan", None),
        P(None, "chan", None),
        P(None, "chan"),
        P(None, "chan"),
        P("dp", "chan", None, None),
    )
    small = mesh.shape["dp"] == 2 and mesh.shape["chan"] == 16
    return jax.shard_map(
        fused if small else local,
        mesh=mesh,
        in_specs=placed,
        out_specs=(
            P("dp", "chan", None, None),
            P("dp", "chan", None, None),
            P("chan", None),
            P(None, None, "chan", None),
            P("chan", None),
            P(None, "chan", None),
            P(None, "chan"),
            P(None, "chan"),
        ),
        check_vma=False,
    )
```

```python
import functools

import jax
import jax.numpy as jnp
from jax import lax
from jax.experimental import pallas as pl
from jax.experimental.pallas import tpu as pltpu
from jax.sharding import PartitionSpec as P

atrous_rates = (6, 12, 18)
norm_eps = 1e-05


def shifted(values, vertical, horizontal):
    margin = max(abs(vertical), abs(horizontal))
    if margin == 0:
        return values
    height = values.shape[-2]
    breadth = values.shape[-1]
    spacing = [(0, 0)] * (values.ndim - 2) + [(margin, margin), (margin, margin)]
    padded = jnp.pad(values, spacing)
    return padded[
        ...,
        margin + vertical : margin + vertical + height,
        margin + horizontal : margin + horizontal + breadth,
    ]


def tap_offsets(dilation):
    return [
        ((along_rows - 1) * dilation, (along_cols - 1) * dilation)
        for along_rows in range(3)
        for along_cols in range(3)
    ]


def make_patches(features, dilation):
    return jnp.stack(
        [shifted(features, vertical, horizontal) for vertical, horizontal in tap_offsets(dilation)]
    )


def silu_slope(values):
    sigmoid = jax.nn.sigmoid(values)
    return sigmoid * (1.0 + values * (1.0 - sigmoid))


def expand_tail(values, extra):
    return values.reshape(values.shape + (1,) * extra)


def local(features, w_one, w_atrous, w_pool, w_proj, gains, biases, out_grad):
    highest = lax.Precision.HIGHEST
    images, local_in, height, columns = features.shape
    pixels = height * columns
    population = images * pixels * lax.axis_size("dp")
    patches = jnp.stack([make_patches(features, dilation) for dilation in atrous_rates])
    pooled = jnp.sum(features, axis=(2, 3), dtype=jnp.float32) / pixels
    one_term = jnp.einsum("nchw,co->onhw", features, w_one, preferred_element_type=jnp.float32)
    rate_terms = jnp.einsum(
        "rtnchw,rtco->ronhw", patches, w_atrous, preferred_element_type=jnp.float32
    )
    spatial_term = jnp.concatenate([one_term[None], rate_terms])
    pool_term = jnp.dot(pooled, w_pool.astype(jnp.float32), precision=highest).T[None]
    branch_pre, pool_pre = (
        lax.psum_scatter(spatial_term, "chan", scatter_dimension=1, tiled=True),
        lax.psum_scatter(pool_term, "chan", scatter_dimension=1, tiled=True),
    )
    branch_totals, branch_squares = lax.psum(
        (jnp.sum(branch_pre, axis=(2, 3, 4)), jnp.sum(branch_pre * branch_pre, axis=(2, 3, 4))),
        "dp",
    )
    branch_mean = branch_totals / population
    branch_inv = lax.rsqrt(branch_squares / population - branch_mean * branch_mean + norm_eps)
    centred = branch_pre - expand_tail(branch_mean, 3)
    branch_z = centred * expand_tail(gains[:4] * branch_inv, 3) + expand_tail(biases[:4], 3)
    branch_hat = centred * expand_tail(branch_inv, 3)
    act_low = jax.nn.silu(branch_z).astype(jnp.bfloat16)
    pool_act = jax.nn.silu(pool_pre).astype(jnp.bfloat16)
    window = w_proj
    spatial = jnp.einsum("bonhw,bod->dnhw", act_low, window[:4], preferred_element_type=jnp.float32)
    pool_part = jnp.einsum("bon,bod->dn", pool_act, window[4:], preferred_element_type=jnp.float32)
    proj_pre = lax.psum_scatter(
        spatial + pool_part[:, :, None, None], "chan", scatter_dimension=0, tiled=True
    )
    proj_totals, proj_squares = lax.psum(
        (jnp.sum(proj_pre, axis=(1, 2, 3)), jnp.sum(proj_pre * proj_pre, axis=(1, 2, 3))), "dp"
    )
    proj_mean = proj_totals / population
    proj_inv = lax.rsqrt(proj_squares / population - proj_mean * proj_mean + norm_eps)
    proj_centred = proj_pre - expand_tail(proj_mean, 3)
    proj_z = proj_centred * expand_tail(gains[4] * proj_inv, 3) + expand_tail(biases[4], 3)
    proj_hat = proj_centred * expand_tail(proj_inv, 3)
    output = jnp.transpose(jax.nn.silu(proj_z), (1, 0, 2, 3))
    grad_out = jnp.transpose(out_grad, (1, 0, 2, 3)).astype(jnp.float32)
    proj_dz = grad_out * silu_slope(proj_z)
    proj_dbias, proj_dgain = lax.psum(
        (jnp.sum(proj_dz, axis=(1, 2, 3)), jnp.sum(proj_dz * proj_hat, axis=(1, 2, 3))), "dp"
    )
    proj_dpre = expand_tail(gains[4] * proj_inv, 3) * (
        proj_dz
        - expand_tail(proj_dbias / population, 3)
        - proj_hat * expand_tail(proj_dgain / population, 3)
    )
    proj_low = proj_dpre.astype(jnp.bfloat16)
    pool_act_wide = pool_act.astype(jnp.float32)
    portion = lax.all_gather(proj_low, "chan", axis=0, tiled=True)
    window = w_proj
    act_grad = jnp.einsum(
        "bod,dnhw->bonhw", window[:4], portion, preferred_element_type=jnp.float32
    )
    portion_sum = jnp.sum(portion, axis=(2, 3), dtype=jnp.float32)
    pool_grad = jnp.einsum(
        "bod,dn->bon", window[4:].astype(jnp.float32), portion_sum, precision=highest
    )
    spatial_part = jnp.einsum(
        "bonhw,dnhw->bod", act_low, portion, preferred_element_type=jnp.float32
    )
    pool_part = jnp.einsum("bon,dn->bod", pool_act_wide, portion_sum, precision=highest)
    weight_grad = jnp.concatenate([spatial_part, pool_part])
    act_grad, pool_grad, proj_wgrad = (act_grad, pool_grad, weight_grad)
    branch_dz = act_grad * silu_slope(branch_z)
    branch_dbias, branch_dgain = lax.psum(
        (jnp.sum(branch_dz, axis=(2, 3, 4)), jnp.sum(branch_dz * branch_hat, axis=(2, 3, 4))), "dp"
    )
    branch_dpre = expand_tail(gains[:4] * branch_inv, 3) * (
        branch_dz
        - expand_tail(branch_dbias / population, 3)
        - branch_hat * expand_tail(branch_dgain / population, 3)
    )
    branch_low = branch_dpre.astype(jnp.bfloat16)
    pool_low = (pool_grad * silu_slope(pool_pre)).astype(jnp.bfloat16)
    spatial_portion = lax.all_gather(branch_low, "chan", axis=1, tiled=True)
    pool_portion = lax.all_gather(pool_low, "chan", axis=1, tiled=True)
    pool_cols = w_pool.astype(jnp.float32)
    feature_grad = jnp.einsum(
        "co,onhw->nchw", w_one, spatial_portion[0], preferred_element_type=jnp.float32
    )
    patch_grad = jnp.einsum(
        "rtco,ronhw->rtnchw", w_atrous, spatial_portion[1:], preferred_element_type=jnp.float32
    )
    pool_wide = pool_portion[0].astype(jnp.float32)
    pooled_grad = jnp.dot(pool_wide.T, pool_cols.T, precision=highest)
    one_piece = jnp.einsum(
        "nchw,onhw->co", features, spatial_portion[0], preferred_element_type=jnp.float32
    )
    rate_piece = jnp.einsum(
        "rtnchw,ronhw->rtco", patches, spatial_portion[1:], preferred_element_type=jnp.float32
    )
    pool_piece = jnp.dot(pooled.T, pool_wide.T, precision=highest)
    one_grad = one_piece
    rate_grad = rate_piece
    pool_wgrad = pool_piece
    feature_grad, patch_grad, pooled_grad, one_grad, rate_grad, pool_wgrad = (
        feature_grad,
        patch_grad,
        pooled_grad,
        one_grad,
        rate_grad,
        pool_wgrad,
    )
    for branch, dilation in enumerate(atrous_rates):
        for tap_index, (vertical, horizontal) in enumerate(tap_offsets(dilation)):
            feature_grad = feature_grad + shifted(
                patch_grad[branch, tap_index], -vertical, -horizontal
            )
    feature_grad = feature_grad + (pooled_grad / pixels)[:, :, None, None]
    one_grad, rate_grad, pool_wgrad, proj_wgrad = (
        lax.psum(one_grad.astype(jnp.bfloat16), "dp").astype(jnp.float32),
        lax.psum(rate_grad.astype(jnp.bfloat16), "dp").astype(jnp.float32),
        lax.psum(pool_wgrad.astype(jnp.bfloat16), "dp").astype(jnp.float32),
        lax.psum(proj_wgrad.astype(jnp.bfloat16), "dp").astype(jnp.float32),
    )
    gains_grad = jnp.concatenate([branch_dgain, proj_dgain[None]])
    biases_grad = jnp.concatenate([branch_dbias, proj_dbias[None]])
    return (
        output,
        feature_grad,
        one_grad,
        rate_grad,
        pool_wgrad,
        proj_wgrad,
        gains_grad,
        biases_grad,
    )


MESH = pl.DeviceIdType.MESH
F32 = jnp.float32
BF16 = jnp.bfloat16
ROWS = 16
COLS = 128
PIXELS = ROWS * COLS
WIDE = PIXELS + 128
CIN_PART = 128
COUT = 256
GROUPS = 8
BLOCK = 256
ORDER = (0, 3, 2, 1)


def branch_rows(branch):
    if branch == 0:
        return [(None, 0)]
    rate = atrous_rates[branch - 1]
    return [(i, (i - 1) * rate) for i in (1, 0, 2) if abs((i - 1) * rate) < ROWS]


def weight_slots():
    slots = {}
    count = 0
    spans = {}
    for branch in ORDER:
        begin = count
        for i, _ in branch_rows(branch):
            slots[(branch, i)] = count
            count += 1 if branch == 0 else 3
        if branch == 0:
            slots["pool"] = count
            count += 1
        spans[branch] = (begin, count)
    return slots, spans, count


SLOTS, SPANS, NSLOTS = weight_slots()


HALVES = 2
SPAN = PIXELS // HALVES
PIECES = [(b, half * SPAN) for b in ORDER for half in range(HALVES)]


CROSS_FIRST = PIECES[-2:]


def carries_pool(piece):
    return piece == (0, PIXELS - SPAN)


def lanes_of(piece):
    return pl.ds(piece[1], SPAN + (128 if carries_pool(piece) else 0))


def dot(a, b):
    return jnp.dot(a, b, preferred_element_type=F32)


def dot_nt(a, b):
    return lax.dot_general(a, b, (((1,), (1,)), ((), ())), preferred_element_type=F32)


def iota(shape, dim):
    return lax.broadcasted_iota(jnp.int32, shape, dim)


def lane_sum(v):
    return jnp.sum(v, axis=1, keepdims=True)


def split_lanes(column, lanes=(0, 1, 2)):
    high = column.astype(BF16).astype(F32)
    mid = (column - high).astype(BF16).astype(F32)
    low = column - high - mid
    lane = iota((column.shape[0], 128), 1)
    out = jnp.where(lane == lanes[0], high, 0.0)
    out = out + jnp.where(lane == lanes[1], mid, 0.0)
    return out + jnp.where(lane == lanes[2], low, 0.0)


def encode_pair(v):
    lane = iota(v.shape, v.ndim - 1)
    high = v.astype(BF16).astype(F32)
    low = v - high
    return jnp.where(lane == 0, high, jnp.where(lane == 1, low, 0.0)).astype(BF16)


def decode_pair(e):
    return jnp.broadcast_to(jnp.sum(e.astype(F32), axis=-1, keepdims=True), e.shape)


def shift_cols(v, by):
    if by == 0:
        return v
    lane = iota((v.shape[0], 128), 1)
    keep = (lane >= by) if by > 0 else (lane < 128 + by)
    parts = []
    for h in range(v.shape[1] // 128):
        tile = v[:, h * 128 : (h + 1) * 128]
        parts.append(jnp.where(keep, pltpu.roll(tile, by % 128, 1), 0.0))
    return jnp.concatenate(parts, axis=1) if len(parts) > 1 else parts[0]


def sigmoid(z):
    return 0.5 * jnp.tanh(0.5 * z) + 0.5


INPUTS = ("feat", "og", "w1", "wa", "wpool", "wproj", "gains", "biases")
OUTPUTS = ("out", "dwpool", "dwproj", "dgains", "dbiases", "fgb", "dwb")


def scratch_table(sems):
    vm = pltpu.VMEM
    return {
        "outv": vm((256, 128), F32),
        "dwpoolv": vm((128, 256), F32),
        "dwprojv": vm((5, 16, 256), F32),
        "dgainsv": vm((5, 16), F32),
        "dbiasesv": vm((5, 16), F32),
        "feat": vm((2048, 128), BF16),
        "og": vm((256, 128), BF16),
        "w1": vm((128, 256), BF16),
        "wa": vm((27, 128, 256), BF16),
        "wpool": vm((128, 256), BF16),
        "wproj": vm((5, 16, 256), BF16),
        "gains": vm((5, 16), F32),
        "biases": vm((5, 16), F32),
        "xsib": vm((128, PIXELS), BF16),
        "tw": vm((NSLOTS, GROUPS, 2, 16, 128), BF16),
        "lw": vm((NSLOTS, GROUPS, 16, 256), BF16),
        "acc": vm((4, GROUPS, 16, PIXELS), F32),
        "acp": vm((GROUPS, 16, 128), F32),
        "ys": vm((4, 4, 16, WIDE), BF16),
        "yr": vm((4, 4, 16, WIDE), BF16),
        "zs": vm((4, 4, 16, WIDE), BF16),
        "zr": vm((4, 4, 16, WIDE), BF16),
        "g": vm((4, 2, GROUPS, 16, WIDE), BF16),
        "ogs": vm((2, GROUPS, 16, PIXELS), BF16),
        "pt": vm((GROUPS, 16, 128), F32),
        "wp": vm((GROUPS, 5, 16, 256), BF16),
        "wpt": vm((256, 640), BF16),
        "wps": vm((GROUPS, 2, 16, 128), BF16),
        "pps": vm((2, GROUPS, 16, PIXELS), BF16),
        "xv": vm((2, 7, 128, PIXELS), BF16),
        "sl": vm((2, 4, GROUPS, 16, PIXELS), BF16),
        "flip": vm((128, 128), F32),
        "c1": vm((5, 128, 128), F32),
        "c2": vm((5, 128, 128), F32),
        "act": vm((2, 4, GROUPS, 16, PIXELS), BF16),
        "ao": vm((2, 4, 16, PIXELS), BF16),
        "pa": vm((5, 128, 128), F32),
        "pb": vm((5, 128, 128), F32),
        "pm": vm((5, 128, 128), F32),
        "pi": vm((5, 128, 128), F32),
        "s1": vm((5, 128, 128), F32),
        "s2": vm((5, 128, 128), F32),
        "pr": vm((2, GROUPS, 16, PIXELS), BF16),
        "dzp": vm((2, GROUPS, 16, PIXELS), F32),
        "dp": vm((2, GROUPS, 2, 16, PIXELS), BF16),
        "dpo": vm((GROUPS, 2, 16, 128), BF16),
        "d": vm((4, 2, GROUPS, 2, 16, PIXELS), BF16),
        "dwv": vm((28, 128, 256), BF16),
        "rsum": vm((GROUPS, 2, 16, 128), F32),
        "fga": vm((128, PIXELS), F32),
        "fgv": vm((128, PIXELS), BF16),
        "pooled": vm((2, 128, 128), F32),
        "ppool": vm((2, 128, 128), F32),
        "ss": pltpu.SemaphoreType.DMA((sems,)),
        "rs": pltpu.SemaphoreType.DMA((sems,)),
        "ls": pltpu.SemaphoreType.DMA((32,)),
        "li": pltpu.SemaphoreType.DMA((8,)),
    }


class Refs:
    pass


NSEMS = 224


def head_kernel(*refs):
    names = tuple(n + "_hbm" for n in INPUTS) + OUTPUTS + tuple(scratch_table(NSEMS))
    r = Refs()
    for name, ref in zip(names, refs, strict=True):
        setattr(r, name, ref)
    x = lax.axis_index("dp")
    c = lax.axis_index("chan")
    k = lax.rem(c, 2)
    y = lax.rem(lax.div(c, 2), 2)
    z = lax.div(c, 4)

    def dev(xx, zz, yy, kk):
        return {"dp": xx, "chan": (zz * 2 + yy) * 2 + kk}

    sibling = dev(x, z, y, 1 - k)
    xdev = dev(1 - x, z, y, k)
    ydev = dev(x, z, 1 - y, k)
    zpos = [None] + [lax.rem(z + i, 4) for i in (1, 2, 3)]
    zfrom = [None] + [lax.rem(z + 4 - i, 4) for i in (1, 2, 3)]
    zdev = [None] + [dev(x, zpos[i], y, k) for i in (1, 2, 3)]

    counter = [0]
    sent = []
    due = {}

    def new(n=1):
        first = counter[0]
        counter[0] += n
        assert counter[0] <= NSEMS
        return first

    def rcopy(src, dst, n, device):
        return pltpu.make_async_remote_copy(
            src_ref=src,
            dst_ref=dst,
            send_sem=r.ss.at[n],
            recv_sem=r.rs.at[n],
            device_id=device,
            device_id_type=MESH,
        )

    def send(src, dst, n, device, group=None):
        copy = rcopy(src, dst, n, device)
        copy.start()
        (sent if group is None else group).append(copy)
        due[n] = (dst, device)

    def arrived(ref, n, device):
        del due[n]
        rcopy(ref, ref, n, device).wait_recv()

    barrier = pltpu.get_barrier_semaphore()
    partners = [sibling, xdev, ydev] + zdev[1:]
    for partner in partners:
        pl.semaphore_signal(barrier, inc=1, device_id=partner, device_id_type=MESH)

    loads = {}
    for n, name in enumerate(("feat", "w1", "wpool", "og", "gains", "biases", "wproj", "wa")):
        loads[name] = pltpu.make_async_copy(getattr(r, name + "_hbm"), getattr(r, name), r.li.at[n])
        loads[name].start()

    rr = iota((256, 256), 0)
    cc = iota((256, 256), 1)
    perm = jnp.where(cc == lax.rem(rr, 16) * 16 + lax.div(rr, 16), 1.0, 0.0).astype(BF16)
    eye = jnp.where(rr == cc, 1.0, 0.0).astype(BF16)

    def permuted(ref, block):
        return dot(perm, ref[block * 256 : (block + 1) * 256, :]).astype(BF16)

    def pre_group(yy, zz):
        return yy * 4 + zz

    def own_group(yy, zz):
        return zz * 2 + yy

    class Gather:
        def __init__(self, slot, group, across):
            self.slot, self.group, self.across = slot, group, across
            self.nz, self.ny, self.nx = new(3), new(4), new(8) if across else None

        def start(self):
            mine = self.slot(self.group(y, z))
            for i in (2, 1, 3):
                send(mine, mine, self.nz + i - 1, zdev[i])
            send(mine, mine, self.ny, ydev)
            if self.across:
                send(mine, mine, self.nx, xdev)

        def forward_z(self):
            for i in (1, 2, 3):
                ref = self.slot(self.group(y, zfrom[i]))
                arrived(ref, self.nz + i - 1, zdev[i])
                send(ref, ref, self.ny + i, ydev)
                if self.across:
                    send(ref, ref, self.nx + i, xdev)

        def forward_y(self):
            for i in range(4):
                ref = self.slot(self.group(1 - y, z if i == 0 else zfrom[i]))
                arrived(ref, self.ny + i, ydev)
                if self.across:
                    send(ref, ref, self.nx + 4 + i, xdev)

        def finish(self, other):
            if self.across:
                for i in range(8):
                    yy = y if i < 4 else 1 - y
                    zz = z if i % 4 == 0 else zfrom[i % 4]
                    arrived(other(self.group(yy, zz)), self.nx + i, xdev)

    g_og = Gather(lambda g: r.ogs.at[x, g], own_group, True)
    g_par = Gather(lambda g: r.pt.at[g], own_group, False)
    g_wp = Gather(lambda g: r.wp.at[g], own_group, False)
    def sums_slot(piece, image):
        return lambda g: r.g.at[piece[0], image, g, :, lanes_of(piece)]

    g_pre = {}
    g_other = {}
    n_cross = {}
    for piece in PIECES:
        g_pre[piece] = Gather(sums_slot(piece, x), pre_group, piece not in CROSS_FIRST)
        if piece in CROSS_FIRST:
            g_other[piece] = Gather(sums_slot(piece, 1 - x), pre_group, False)
            n_cross[piece] = new()

    mine = own_group(y, z)
    loads["og"].wait()
    og = permuted(r.og, 0)
    for h in range(ROWS):
        r.ogs[x, mine, :, h * 128 : (h + 1) * 128] = og[h * 16 : (h + 1) * 16]
    r.flip[...] = jnp.zeros((128, 128), F32)
    for name in ("gains", "biases", "wproj"):
        loads[name].wait()
    r.flip[0:5, 0:16] = r.gains[...]
    r.flip[8:13, 0:16] = r.biases[...]
    r.pt[mine] = r.flip[...].T[0:16, :]
    r.wp[mine] = r.wproj[...]

    n_w = {b: new() for b in ORDER}

    def weight_ref(b, i, j):
        return r.w1 if b == 0 else r.wa.at[(b - 1) * 9 + 3 * i + j]

    def transpose_into(slot, ref):
        t = dot_nt(eye, ref[...]).astype(BF16)
        r.tw[slot] = t.reshape(GROUPS, 2, 16, 128)
        r.lw[slot, :, :, 0:128] = r.tw[slot, :, k]

    def prepare_weights(b):
        for i, _ in branch_rows(b):
            slot = SLOTS[(b, i)]
            if b == 0:
                transpose_into(slot, r.w1)
                transpose_into(SLOTS["pool"], r.wpool)
            else:
                for j in range(3):
                    transpose_into(slot + j, weight_ref(b, i, j))

    def send_weights(b):
        lo, hi = SPANS[b]
        send(
            r.tw.at[pl.ds(lo, hi - lo), :, 1 - k],
            r.lw.at[pl.ds(lo, hi - lo), :, :, pl.ds(128, 128)],
            n_w[b],
            sibling,
        )

    def wait_weights(b):
        lo, hi = SPANS[b]
        arrived(r.lw.at[pl.ds(lo, hi - lo), :, :, pl.ds(128, 128)], n_w[b], sibling)

    for name in ("w1", "wpool", "feat"):
        loads[name].wait()
    for block in range(8):
        t = permuted(r.feat, block)
        for h in range(ROWS):
            px = slice(h * 128, (h + 1) * 128)
            r.xv[x, 0, block * 16 : (block + 1) * 16, px] = t[h * 16 : (h + 1) * 16]
    prepare_weights(0)
    loads["wa"].wait()
    prepare_weights(ORDER[1])

    pl.semaphore_wait(barrier, len(partners))

    n_feat = new(2)
    n_foth = new()
    halves = [pl.ds(0, PIXELS // 2), pl.ds(PIXELS // 2, PIXELS // 2)]
    send_weights(0)
    for n in range(2):
        send(r.xv.at[x, 0, :, halves[n]], r.xsib.at[:, halves[n]], n_feat + n, sibling)
    send_weights(ORDER[1])
    send(r.xv.at[x, 0], r.xv.at[x, 0], n_foth, xdev)
    arrived(r.xsib.at[:, halves[0]], n_feat, sibling)

    def features_at(px):
        return jnp.concatenate([r.xv[x, 0, :, px], r.xsib[:, px]], axis=0)

    def convolve(piece):
        b = piece[0]
        for q in range(piece[1] // BLOCK, (piece[1] + SPAN) // BLOCK):
            px = slice(q * BLOCK, (q + 1) * BLOCK)
            total = None
            for i, offset in branch_rows(b):
                source = q + offset * COLS // BLOCK
                if source < 0 or source >= PIXELS // BLOCK:
                    continue
                slot = SLOTS[(b, i)]
                count = 1 if b == 0 else 3
                weights = r.lw[slot : slot + count].reshape(count * 128, 256)
                part = dot(weights, features_at(slice(source * BLOCK, (source + 1) * BLOCK)))
                total = part if total is None else total + part
            if b:
                rate = atrous_rates[b - 1]
                total = (
                    total[128:256]
                    + shift_cols(total[0:128], rate)
                    + shift_cols(total[256:384], -rate)
                )
            r.acc[b, :, :, px] = total.reshape(GROUPS, 16, BLOCK)
        if carries_pool(piece):
            pooled = jnp.zeros((256, 128), F32)
            for h in range(ROWS):
                pooled = pooled + features_at(slice(h * 128, (h + 1) * 128)).astype(F32)
            column = lane_sum(pooled) / PIXELS
            r.pooled[x] = jnp.broadcast_to(column[0:128], (128, 128))
            terms = split_lanes(column).astype(BF16)
            slot = SLOTS["pool"]
            sums = lane_sum(dot(r.lw[slot].reshape(128, 256), terms))
            r.acp[...] = jnp.broadcast_to(sums, (128, 128)).reshape(GROUPS, 16, 128)

    n_ry = {piece: new() for piece in PIECES}
    n_rz = {piece: new(3) for piece in PIECES}

    def reduce_y_send(piece):
        b, w = piece[0], lanes_of(piece)
        px = pl.ds(piece[1], SPAN)
        r.ys[b, :, :, px] = r.acc[b, pl.ds(4 * (1 - y), 4), :, px].astype(BF16)
        if carries_pool(piece):
            r.ys[b, :, :, PIXELS:WIDE] = encode_pair(r.acp[pl.ds(4 * (1 - y), 4)])
        send(r.ys.at[b, :, :, w], r.yr.at[b, :, :, w], n_ry[piece], ydev)

    def reduce_z_send(piece):
        b, w = piece[0], lanes_of(piece)
        px = pl.ds(piece[1], SPAN)
        arrived(r.yr.at[b, :, :, w], n_ry[piece], ydev)
        for i in (2, 1, 3, 0):
            zz = z if i == 0 else zpos[i]
            g = 4 * y + zz
            s = r.acc[b, g, :, px] + r.yr[b, zz, :, px].astype(F32)
            if carries_pool(piece):
                e = r.acp[g] + decode_pair(r.yr[b, zz, :, PIXELS:WIDE])
            if i == 0:
                r.acc[b, g, :, px] = s
                if carries_pool(piece):
                    r.acp[g] = e
            else:
                r.zs[b, i, :, px] = s.astype(BF16)
                if carries_pool(piece):
                    r.zs[b, i, :, PIXELS:WIDE] = encode_pair(e)
                send(r.zs.at[b, i, :, w], r.zr.at[b, i, :, w], n_rz[piece] + i - 1, zdev[i])

    def reduce_finish(piece):
        b, w = piece[0], lanes_of(piece)
        px = pl.ds(piece[1], SPAN)
        g = pre_group(y, z)
        total = r.acc[b, g, :, px]
        extra = r.acp[g] if carries_pool(piece) else None
        for i in (1, 2, 3):
            arrived(r.zr.at[b, i, :, w], n_rz[piece] + i - 1, zdev[i])
            total = total + r.zr[b, i, :, px].astype(F32)
            if carries_pool(piece):
                extra = extra + decode_pair(r.zr[b, i, :, PIXELS:WIDE])
        r.g[b, x, g, :, px] = total.astype(BF16)
        if carries_pool(piece):
            r.g[b, x, g, :, PIXELS:WIDE] = encode_pair(extra)
        g_pre[piece].start()
        if piece in CROSS_FIRST:
            ref = sums_slot(piece, x)(g)
            send(ref, ref, n_cross[piece], xdev)

    def cross(piece):
        arrived(sums_slot(piece, 1 - x)(pre_group(y, z)), n_cross[piece], xdev)
        g_other[piece].start()

    shift_pairs = []
    lane_r = iota((128, 128), 0)
    lane_c = iota((128, 128), 1)
    for rate in atrous_rates:
        left = jnp.where(lane_r == lane_c - rate, 1.0, 0.0).astype(BF16)
        right = jnp.where(lane_r == lane_c + rate, 1.0, 0.0).astype(BF16)
        shift_pairs.append(jnp.concatenate([left, right], axis=1))

    local = []

    def keep(src, dst):
        copy = pltpu.make_async_copy(src, dst, r.ls.at[len(local)])
        copy.start()
        local.append(copy)

    def place_shifted(image):
        for h in range(ROWS):
            px = slice(h * 128, (h + 1) * 128)
            for a in range(3):
                both = dot(r.xv[image, 0, :, px], shift_pairs[a]).astype(BF16)
                r.xv[image, 1 + 2 * a, :, px] = both[:, 0:128]
                r.xv[image, 2 + 2 * a, :, px] = both[:, 128:256]

    count = float(2 * PIXELS)

    def each_group(body):
        for g in range(GROUPS):
            body(g, pl.ds(g * 16, 16))

    tiles = [(image, slice(h * 128, (h + 1) * 128)) for image in range(2) for h in range(ROWS)]
    zero_tile = jnp.zeros((16, 128), F32)

    def spread_lanes(column):
        return jnp.broadcast_to(column, (128, 128))

    def norm_params(b):
        mean = lane_sum(r.s1[b]) / count
        inv = lax.rsqrt(lane_sum(r.s2[b]) / count - mean * mean + norm_eps)
        par = r.pt[...].reshape(128, 128)
        scale = par[:, b : b + 1] * inv
        r.pa[b] = spread_lanes(scale)
        r.pb[b] = spread_lanes(par[:, 8 + b : 9 + b] - mean * scale)
        r.pm[b] = spread_lanes(mean)
        r.pi[b] = spread_lanes(inv)

    def grad_params(b):
        s1 = lane_sum(r.s1[b])
        inv, mean = r.pi[b][:, 0:1], r.pm[b][:, 0:1]
        s2 = (lane_sum(r.s2[b]) - mean * s1) * inv
        scale = r.pa[b][:, 0:1]
        c2 = -scale * inv * s2 / count
        r.s1[b] = spread_lanes(s1)
        r.s2[b] = spread_lanes(s2)
        r.c2[b] = spread_lanes(c2)
        r.c1[b] = spread_lanes(-scale * s1 / count - mean * c2)

    def act_and_slope(zed):
        u = 0.5 * jnp.tanh(0.5 * zed)
        sg = 0.5 + u
        act = zed * sg
        return act, sg + act * (0.5 - u)

    def branch_norm(b):
        def sums(g, rows):
            s, q = zero_tile, zero_tile
            for image, px in tiles:
                v = r.g[b, image, g, :, px].astype(F32)
                s = s + v
                q = q + v * v
            r.s1[b, rows] = s
            r.s2[b, rows] = q

        each_group(sums)
        norm_params(b)

        def apply(g, rows):
            scale, base = r.pa[b, rows], r.pb[b, rows]
            for image, px in tiles:
                act, slope = act_and_slope(r.g[b, image, g, :, px].astype(F32) * scale + base)
                r.act[image, b, g, :, px] = act.astype(BF16)
                r.sl[image, b, g, :, px] = slope.astype(BF16)

        each_group(apply)

    g_par.start()
    g_wp.start()
    steps = len(PIECES)
    for s in range(steps + 6):
        if s < steps:
            b = PIECES[s][0]
            if s % HALVES == 0:
                wait_weights(b)
            convolve(PIECES[s])
            if s == 0:
                arrived(r.xsib.at[:, halves[1]], n_feat + 1, sibling)
            reduce_y_send(PIECES[s])
            if s % HALVES == 0 and s // HALVES + 2 < len(ORDER):
                prepare_weights(ORDER[s // HALVES + 2])
                send_weights(ORDER[s // HALVES + 2])
        if s == 0:
            g_og.start()
        if 0 <= s - 2 < steps:
            reduce_z_send(PIECES[s - 2])
        if s == 2:
            g_par.forward_z()
            g_wp.forward_z()
            g_og.forward_z()
        if 0 <= s - 3 < steps:
            reduce_finish(PIECES[s - 3])
        if s == 4:
            g_par.forward_y()
            g_wp.forward_y()
            g_og.forward_y()
        if 0 <= s - 5 < steps:
            g_pre[PIECES[s - 5]].forward_z()
            if PIECES[s - 5] in CROSS_FIRST:
                cross(PIECES[s - 5])
        if 0 <= s - 6 < steps:
            if PIECES[s - 6] in CROSS_FIRST:
                g_other[PIECES[s - 6]].forward_z()
            else:
                g_pre[PIECES[s - 6]].forward_y()
        if s == 6:
            place_shifted(x)
        if s == 7:
            arrived(r.xv.at[1 - x, 0], n_foth, xdev)
            place_shifted(1 - x)
            pooled = jnp.zeros((128, 128), F32)
            for h in range(ROWS):
                pooled = pooled + r.xv[1 - x, 0, :, h * 128 : (h + 1) * 128].astype(F32)
            r.pooled[1 - x] = spread_lanes(lane_sum(pooled) / PIXELS)

    for b in range(5):
        flat = dot_nt(eye, r.wp[:, b].reshape(128, 256)).astype(BF16)
        r.wps[...] = flat.reshape(GROUPS, 2, 16, 128)
        r.wpt[0:128, b * 128 : (b + 1) * 128] = r.wps[:, k].reshape(128, 128)
        r.wpt[128:256, b * 128 : (b + 1) * 128] = r.wps[:, 1 - k].reshape(128, 128)

    for piece in PIECES:
        if piece in CROSS_FIRST:
            g_pre[piece].forward_y()
            g_other[piece].forward_y()
        else:
            g_pre[piece].finish(sums_slot(piece, 1 - x))
        if piece[1] == PIXELS - SPAN:
            branch_norm(piece[0])

    pool_act = []
    lane128 = iota((128, 128), 1)
    pool_cols = jnp.zeros((128, 128), F32)
    for image in range(2):
        pre = decode_pair(r.g[0, image, :, :, PIXELS:WIDE]).reshape(128, 128)
        r.ppool[image] = pre
        pool_cols = pool_cols + jnp.where(lane128 == image, pre * sigmoid(pre), 0.0)
    pool_cols = pool_cols.astype(BF16)
    pool_out = dot(r.wpt[:, 512:640], pool_cols)

    n_pp = new(2)
    for image in range(2):
        column = pool_out[:, image : image + 1]
        for q in range(PIXELS // BLOCK):
            px = slice(q * BLOCK, (q + 1) * BLOCK)
            part = dot(r.wpt[:, 0:512], r.act[image, :, :, :, px].reshape(512, BLOCK)) + column
            r.acc[image, :, :, px] = part[0:128].reshape(GROUPS, 16, BLOCK)
            r.pps[image, :, :, px] = part[128:256].astype(BF16).reshape(GROUPS, 16, BLOCK)
        send(r.pps.at[image], r.pr.at[image], n_pp + image, sibling)

    for image in range(2):
        for b in range(4):
            r.ao[image, b] = r.act[image, b, mine]

    g_og.finish(lambda g: r.ogs.at[1 - x, g])
    for image in range(2):
        arrived(r.pr.at[image], n_pp + image, sibling)

    def proj_sums(g, rows):
        s, q = zero_tile, zero_tile
        for image, px in tiles:
            v = r.acc[image, g, :, px] + r.pr[image, g, :, px].astype(F32)
            r.acc[image, g, :, px] = v
            s = s + v
            q = q + v * v
        r.s1[4, rows] = s
        r.s2[4, rows] = q

    each_group(proj_sums)
    norm_params(4)

    def proj_slope(g, rows):
        scale, base = r.pa[4, rows], r.pb[4, rows]
        s1, s2 = zero_tile, zero_tile
        for image, px in tiles:
            v = r.acc[image, g, :, px]
            _, slope = act_and_slope(v * scale + base)
            dz = r.ogs[image, g, :, px].astype(F32) * slope
            r.dzp[image, g, :, px] = dz
            s1 = s1 + dz
            s2 = s2 + dz * v
        r.s1[4, rows] = s1
        r.s2[4, rows] = s2

    each_group(proj_slope)
    grad_params(4)
    n_dp = new(2)
    for image in range(2):

        def proj_low(g, rows, image=image):
            scale, c1, c2 = r.pa[4, rows], r.c1[4, rows], r.c2[4, rows]
            total = zero_tile
            for h in range(ROWS):
                px = slice(h * 128, (h + 1) * 128)
                low = scale * r.dzp[image, g, :, px] + (r.acc[image, g, :, px] * c2 + c1)
                low = low.astype(BF16)
                r.dp[image, g, k, :, px] = low
                total = total + low.astype(F32)
            r.s1[image, rows] = total

        each_group(proj_low)
        ref = r.dp.at[image, :, k]
        send(ref, ref, n_dp + image, sibling)

    n_rsum = new()
    row_sums = jnp.where(lane128 == 0, lane_sum(r.s1[0]), 0.0)
    row_sums = row_sums + jnp.where(lane128 == 1, lane_sum(r.s1[1]), 0.0)
    r.rsum[:, k] = row_sums.reshape(GROUPS, 16, 128)
    ref = r.rsum.at[:, k]
    send(ref, ref, n_rsum, sibling)

    my_rows = pl.ds(pl.multiple_of(mine * 16, 16), 16)
    scale, base = r.pa[4, my_rows], r.pb[4, my_rows]
    for h in range(ROWS):
        zed = r.acc[x, mine, :, h * 128 : (h + 1) * 128] * scale + base
        r.outv[pl.ds(h, 16, stride=16), :] = zed * sigmoid(zed)
    keep(r.outv, r.out)

    for image in range(2):
        arrived(r.dp.at[image, :, 1 - k], n_dp + image, sibling)

    n_d = {b: new(2) for b in ORDER}

    def back_block(b, turn, image, q):
        px = slice(q * 512, (q + 1) * 512)
        dblock = r.dp[image, :, :, :, px].reshape(256, 512)
        back = dot(r.wp[:, b].reshape(128, 256), dblock)
        r.acc[2 * turn + image, :, :, px] = back.reshape(GROUPS, 16, 512)

    back_order = (1, 2, 3, 0)

    dwp = [jnp.zeros((64, 256), F32)]

    def proj_weights(image, q):
        px = slice(q * 512, (q + 1) * 512)
        acts = r.ao[image, :, :, px].reshape(64, 512)
        dwp[0] = dwp[0] + dot_nt(acts, r.dp[image, :, :, :, px].reshape(256, 512))

    def branch_back(b, turn):
        for image in range(2):
            for q in range(PIXELS // 512):
                back_block(b, turn, image, q)

        def slope(g, rows):
            s1, s2 = zero_tile, zero_tile
            for image, px in tiles:
                dz = r.acc[2 * turn + image, g, :, px] * r.sl[image, b, g, :, px].astype(F32)
                r.acc[2 * turn + image, g, :, px] = dz
                s1 = s1 + dz
                s2 = s2 + dz * r.g[b, image, g, :, px].astype(F32)
            r.s1[b, rows] = s1
            r.s2[b, rows] = s2
            if b == back_order[0]:
                proj_weights(g // 4, g % 4)

        each_group(slope)
        grad_params(b)
        for image in range(2):

            def lower(g, rows, image=image):
                scale, c1, c2 = r.pa[b, rows], r.c1[b, rows], r.c2[b, rows]
                for h in range(ROWS):
                    px = slice(h * 128, (h + 1) * 128)
                    v = r.g[b, image, g, :, px].astype(F32)
                    low = scale * r.acc[2 * turn + image, g, :, px] + (v * c2 + c1)
                    r.d[b, image, g, k, :, px] = low.astype(BF16)

            each_group(lower)
            there = r.d.at[b, image, :, k]
            send(there, there, n_d[b] + image, sibling)

    def branch_grads(b, first_branch, last_branch):
        for image in range(2):
            arrived(r.d.at[b, image, :, 1 - k], n_d[b] + image, sibling)
        planes = (2 * b - 1, 0, 2 * b)
        for i, offset in branch_rows(b):
            first, last = max(0, -offset), min(ROWS, ROWS - offset)
            there = slice((first + offset) * 128, (last + offset) * 128)
            here = slice(first * 128, last * 128)
            total = None
            for image in range(2):
                if b == 0:
                    rows = r.xv[image, 0]
                else:
                    rows = jnp.concatenate([r.xv[image, p, :, there] for p in planes], axis=0)
                part = dot_nt(rows, r.d[b, image, :, :, :, here].reshape(256, -1))
                total = part if total is None else total + part
            total = total.astype(BF16)
            if b == 0:
                slot = pl.ds(27, 1)
                r.dwv[27] = total
            else:
                slot = pl.ds((b - 1) * 9 + 3 * i, 3)
                r.dwv[slot] = total.reshape(3, 128, 256)
            keep(r.dwv.at[slot], r.dwb.at[slot])
        for q in range(PIXELS // BLOCK):
            px = slice(q * BLOCK, (q + 1) * BLOCK)
            total = None
            for i, offset in branch_rows(b):
                source = q - offset * COLS // BLOCK
                if source < 0 or source >= PIXELS // BLOCK:
                    continue
                if b == 0:
                    weights = r.w1[...]
                else:
                    weights = r.wa[pl.ds((b - 1) * 9 + 3 * i, 3)].reshape(384, 256)
                dblock = r.d[b, x, :, :, :, source * BLOCK : (source + 1) * BLOCK]
                part = dot(weights, dblock.reshape(256, BLOCK))
                total = part if total is None else total + part
            if b:
                rate = atrous_rates[b - 1]
                total = (
                    total[128:256]
                    + shift_cols(total[0:128], -rate)
                    + shift_cols(total[256:384], rate)
                )
            if not first_branch:
                total = total + r.fga[:, px]
            if last_branch:
                r.fgv[:, px] = (total + fg_pool).astype(BF16)
            else:
                r.fga[:, px] = total

    arrived(r.rsum.at[:, 1 - k], n_rsum, sibling)
    wp4 = r.wp[:, 4].reshape(128, 256)
    dpo = jnp.zeros((128, 128), F32)
    dwp4 = jnp.zeros((16, 256), F32)
    lane16 = iota((16, 128), 1)
    for image in range(2):
        terms = split_lanes(r.rsum[...].reshape(256, 128)[:, image : image + 1]).astype(BF16)
        pool_grad = lane_sum(dot(wp4, terms))
        pre = r.ppool[image][:, 0:1]
        _, slope = act_and_slope(pre)
        low = (pool_grad * slope).astype(BF16).astype(F32)
        for lane in (image, image + 2, image + 4):
            dpo = dpo + jnp.where(lane128 == lane, low, 0.0)
        mine_act, _ = act_and_slope(r.ppool[image, my_rows][:, 0:1])
        mine_act = mine_act.astype(BF16).astype(F32)
        dwp4 = dwp4 + mine_act * dot_nt(jnp.ones((16, 128), BF16), terms)
    r.dwprojv[4] = dwp4
    r.dpo[:, k] = dpo.astype(BF16).reshape(GROUPS, 16, 128)
    n_dpo = new()
    ref = r.dpo.at[:, k]
    send(ref, ref, n_dpo, sibling)

    for n, b in enumerate(back_order):
        branch_back(b, n % 2)
        if n == 0:
            r.dwprojv[0:4] = dwp[0].reshape(4, 16, 256)
            keep(r.dwprojv, r.dwproj)
    branch_grads(back_order[0], True, False)
    branch_grads(back_order[1], False, False)

    tile = jnp.zeros((16, 128), F32)
    for b in range(5):
        tile = tile + jnp.where(lane16 == b, r.s2[b, my_rows], 0.0)
        tile = tile + jnp.where(lane16 == 8 + b, r.s1[b, my_rows], 0.0)
    r.flip[0:16, :] = tile
    flipped = r.flip[...].T
    r.dgainsv[...] = flipped[0:5, 0:16]
    r.dbiasesv[...] = flipped[8:13, 0:16]
    keep(r.dgainsv, r.dgains)
    keep(r.dbiasesv, r.dbiases)

    branch_grads(back_order[2], False, False)

    arrived(r.dpo.at[:, 1 - k], n_dpo, sibling)
    dpo = r.dpo[...].reshape(256, 128)
    pooled = jnp.zeros((128, 128), F32)
    for image in range(2):
        pooled = pooled + split_lanes(r.pooled[image][:, 0:1], (image, image + 2, image + 4))
    r.dwpoolv[...] = dot_nt(pooled.astype(BF16), dpo)
    keep(r.dwpoolv, r.dwpool)
    spread = dot(r.wpool[...], dpo)
    fg_pool = lane_sum(jnp.where(lane128 == x, spread, 0.0)) / PIXELS

    branch_grads(back_order[3], False, True)
    keep(r.fgv, r.fgb)
    for copy in sent:
        copy.wait_send()
    for copy in local:
        copy.wait()


COPY_INPUTS = ("out", "dwpool", "dwproj", "dgains", "dbiases", "fgb", "dwb")
COPY_OUTPUTS = ("out_o", "dwpool_o", "dwproj_o", "dgains_o", "dbiases_o", "fg", "dw1", "dwa")
COPY_SCRATCH = {
    "outv": pltpu.VMEM((256, 128), F32),
    "dwpoolv": pltpu.VMEM((128, 256), F32),
    "dwprojv": pltpu.VMEM((5, 16, 256), F32),
    "fgbv": pltpu.VMEM((128, PIXELS), BF16),
    "dwbv": pltpu.VMEM((28, 128, 256), BF16),
    "fgv": pltpu.VMEM((2048, 128), F32),
    "dwv": pltpu.VMEM((28, 128, 256), F32),
    "si": pltpu.SemaphoreType.DMA((16,)),
    "so": pltpu.SemaphoreType.DMA((16,)),
}


def copy_kernel(*refs):
    r = Refs()
    names = COPY_INPUTS + COPY_OUTPUTS + tuple(COPY_SCRATCH)
    for name, ref in zip(names, refs, strict=True):
        setattr(r, name, ref)
    loads = []
    stores = []

    def load(src, dst):
        copy = pltpu.make_async_copy(src, dst, r.si.at[len(loads)])
        copy.start()
        loads.append(copy)
        return copy

    def store(src, dst):
        copy = pltpu.make_async_copy(src, dst, r.so.at[len(stores)])
        copy.start()
        stores.append(copy)

    met = [
        (b - 1) * 9 + 3 * i for b in (1, 2, 3) for i in range(3) if i in dict(branch_rows(b))
    ]
    taps = [(n, load(r.dwb.at[pl.ds(n, 3)], r.dwbv.at[pl.ds(n, 3)])) for n in met]
    one = load(r.dwb.at[pl.ds(27, 1)], r.dwbv.at[pl.ds(27, 1)])
    fg = load(r.fgb, r.fgbv)
    passed = [
        (load(getattr(r, name), getattr(r, name + "v")), name)
        for name in ("out", "dwpool", "dwproj")
    ]
    r.dgains_o[...] = r.dgains[...]
    r.dbiases_o[...] = r.dbiases[...]
    for n in range(0, 27, 3):
        if n not in met:
            r.dwv[n : n + 3] = jnp.zeros((3, 128, 256), F32)
            store(r.dwv.at[pl.ds(n, 3)], r.dwa.at[pl.ds(n, 3)])
    for n, copy in taps:
        copy.wait()
        r.dwv[n : n + 3] = r.dwbv[n : n + 3].astype(F32)
        store(r.dwv.at[pl.ds(n, 3)], r.dwa.at[pl.ds(n, 3)])
    one.wait()
    r.dwv[27] = r.dwbv[27].astype(F32)
    store(r.dwv.at[27], r.dw1)
    fg.wait()
    for h in range(ROWS):
        r.fgv[pl.ds(h, 128, stride=16), :] = r.fgbv[:, h * 128 : (h + 1) * 128].astype(F32)
    store(r.fgv, r.fg)
    for copy, name in passed:
        copy.wait()
        store(getattr(r, name + "v"), getattr(r, name + "_o"))
    for copy in stores:
        copy.wait()


def fused(features, w_one, w_atrous, w_pool, w_proj, gains, biases, out_grad):
    vmem = pl.BlockSpec(memory_space=pltpu.VMEM)
    hbm = pl.BlockSpec(memory_space=pl.ANY)
    passed = [(256, 128), (128, 256), (5, 16, 256), (5, 16), (5, 16)]
    shapes = [jax.ShapeDtypeStruct(s, F32) for s in passed]
    shapes.append(jax.ShapeDtypeStruct((128, PIXELS), BF16))
    shapes.append(jax.ShapeDtypeStruct((28, 128, 256), BF16))
    parts = pl.pallas_call(
        head_kernel,
        out_shape=shapes,
        in_specs=[hbm] * len(INPUTS),
        out_specs=[hbm] * len(OUTPUTS),
        scratch_shapes=list(scratch_table(NSEMS).values()),
        compiler_params=pltpu.CompilerParams(
            collective_id=0, has_side_effects=True, vmem_limit_bytes=64 * 2**20
        ),
    )(
        features.reshape(2048, 128),
        out_grad.reshape(256, 128),
        w_one,
        w_atrous.reshape(27, 128, 256),
        w_pool,
        w_proj,
        gains,
        biases,
    )
    result = passed + [(2048, 128), (128, 256), (27, 128, 256)]
    out, dwpool, dwproj, dgains, dbiases, fg, dw1, dwa = pl.pallas_call(
        copy_kernel,
        out_shape=[jax.ShapeDtypeStruct(s, F32) for s in result],
        in_specs=[hbm] * 3 + [vmem] * 2 + [hbm] * 2,
        out_specs=[hbm] * 3 + [vmem] * 2 + [hbm] * 3,
        scratch_shapes=list(COPY_SCRATCH.values()),
        compiler_params=pltpu.CompilerParams(vmem_limit_bytes=64 * 2**20),
    )(*parts)
    return (
        out.reshape(1, 16, ROWS, COLS),
        fg.reshape(1, 128, ROWS, COLS),
        dw1,
        dwa.reshape(3, 9, 128, 256),
        dwpool,
        dwproj,
        dgains,
        dbiases,
    )


def solution(mesh):
    placed = (
        P("dp", "chan", None, None),
        P("chan", None),
        P(None, None, "chan", None),
        P("chan", None),
        P(None, "chan", None),
        P(None, "chan"),
        P(None, "chan"),
        P("dp", "chan", None, None),
    )
    small = mesh.shape["dp"] == 2 and mesh.shape["chan"] == 16
    return jax.shard_map(
        fused if small else local,
        mesh=mesh,
        in_specs=placed,
        out_specs=(
            P("dp", "chan", None, None),
            P("dp", "chan", None, None),
            P("chan", None),
            P(None, None, "chan", None),
            P("chan", None),
            P(None, "chan", None),
            P(None, "chan"),
            P(None, "chan"),
        ),
        check_vma=False,
    )
```

```python
import functools

import jax
import jax.numpy as jnp
from jax import lax
from jax.experimental import pallas as pl
from jax.experimental.pallas import tpu as pltpu
from jax.sharding import PartitionSpec as P

atrous_rates = (6, 12, 18)
norm_eps = 1e-05


def shifted(values, vertical, horizontal):
    margin = max(abs(vertical), abs(horizontal))
    if margin == 0:
        return values
    height = values.shape[-2]
    breadth = values.shape[-1]
    spacing = [(0, 0)] * (values.ndim - 2) + [(margin, margin), (margin, margin)]
    padded = jnp.pad(values, spacing)
    return padded[
        ...,
        margin + vertical : margin + vertical + height,
        margin + horizontal : margin + horizontal + breadth,
    ]


def tap_offsets(dilation):
    return [
        ((along_rows - 1) * dilation, (along_cols - 1) * dilation)
        for along_rows in range(3)
        for along_cols in range(3)
    ]


def make_patches(features, dilation):
    return jnp.stack(
        [shifted(features, vertical, horizontal) for vertical, horizontal in tap_offsets(dilation)]
    )


def silu_slope(values):
    sigmoid = jax.nn.sigmoid(values)
    return sigmoid * (1.0 + values * (1.0 - sigmoid))


def expand_tail(values, extra):
    return values.reshape(values.shape + (1,) * extra)


def local(features, w_one, w_atrous, w_pool, w_proj, gains, biases, out_grad):
    highest = lax.Precision.HIGHEST
    images, local_in, height, columns = features.shape
    pixels = height * columns
    population = images * pixels * lax.axis_size("dp")
    patches = jnp.stack([make_patches(features, dilation) for dilation in atrous_rates])
    pooled = jnp.sum(features, axis=(2, 3), dtype=jnp.float32) / pixels
    one_term = jnp.einsum("nchw,co->onhw", features, w_one, preferred_element_type=jnp.float32)
    rate_terms = jnp.einsum(
        "rtnchw,rtco->ronhw", patches, w_atrous, preferred_element_type=jnp.float32
    )
    spatial_term = jnp.concatenate([one_term[None], rate_terms])
    pool_term = jnp.dot(pooled, w_pool.astype(jnp.float32), precision=highest).T[None]
    branch_pre, pool_pre = (
        lax.psum_scatter(spatial_term, "chan", scatter_dimension=1, tiled=True),
        lax.psum_scatter(pool_term, "chan", scatter_dimension=1, tiled=True),
    )
    branch_totals, branch_squares = lax.psum(
        (jnp.sum(branch_pre, axis=(2, 3, 4)), jnp.sum(branch_pre * branch_pre, axis=(2, 3, 4))),
        "dp",
    )
    branch_mean = branch_totals / population
    branch_inv = lax.rsqrt(branch_squares / population - branch_mean * branch_mean + norm_eps)
    centred = branch_pre - expand_tail(branch_mean, 3)
    branch_z = centred * expand_tail(gains[:4] * branch_inv, 3) + expand_tail(biases[:4], 3)
    branch_hat = centred * expand_tail(branch_inv, 3)
    act_low = jax.nn.silu(branch_z).astype(jnp.bfloat16)
    pool_act = jax.nn.silu(pool_pre).astype(jnp.bfloat16)
    window = w_proj
    spatial = jnp.einsum("bonhw,bod->dnhw", act_low, window[:4], preferred_element_type=jnp.float32)
    pool_part = jnp.einsum("bon,bod->dn", pool_act, window[4:], preferred_element_type=jnp.float32)
    proj_pre = lax.psum_scatter(
        spatial + pool_part[:, :, None, None], "chan", scatter_dimension=0, tiled=True
    )
    proj_totals, proj_squares = lax.psum(
        (jnp.sum(proj_pre, axis=(1, 2, 3)), jnp.sum(proj_pre * proj_pre, axis=(1, 2, 3))), "dp"
    )
    proj_mean = proj_totals / population
    proj_inv = lax.rsqrt(proj_squares / population - proj_mean * proj_mean + norm_eps)
    proj_centred = proj_pre - expand_tail(proj_mean, 3)
    proj_z = proj_centred * expand_tail(gains[4] * proj_inv, 3) + expand_tail(biases[4], 3)
    proj_hat = proj_centred * expand_tail(proj_inv, 3)
    output = jnp.transpose(jax.nn.silu(proj_z), (1, 0, 2, 3))
    grad_out = jnp.transpose(out_grad, (1, 0, 2, 3)).astype(jnp.float32)
    proj_dz = grad_out * silu_slope(proj_z)
    proj_dbias, proj_dgain = lax.psum(
        (jnp.sum(proj_dz, axis=(1, 2, 3)), jnp.sum(proj_dz * proj_hat, axis=(1, 2, 3))), "dp"
    )
    proj_dpre = expand_tail(gains[4] * proj_inv, 3) * (
        proj_dz
        - expand_tail(proj_dbias / population, 3)
        - proj_hat * expand_tail(proj_dgain / population, 3)
    )
    proj_low = proj_dpre.astype(jnp.bfloat16)
    pool_act_wide = pool_act.astype(jnp.float32)
    portion = lax.all_gather(proj_low, "chan", axis=0, tiled=True)
    window = w_proj
    act_grad = jnp.einsum(
        "bod,dnhw->bonhw", window[:4], portion, preferred_element_type=jnp.float32
    )
    portion_sum = jnp.sum(portion, axis=(2, 3), dtype=jnp.float32)
    pool_grad = jnp.einsum(
        "bod,dn->bon", window[4:].astype(jnp.float32), portion_sum, precision=highest
    )
    spatial_part = jnp.einsum(
        "bonhw,dnhw->bod", act_low, portion, preferred_element_type=jnp.float32
    )
    pool_part = jnp.einsum("bon,dn->bod", pool_act_wide, portion_sum, precision=highest)
    weight_grad = jnp.concatenate([spatial_part, pool_part])
    act_grad, pool_grad, proj_wgrad = (act_grad, pool_grad, weight_grad)
    branch_dz = act_grad * silu_slope(branch_z)
    branch_dbias, branch_dgain = lax.psum(
        (jnp.sum(branch_dz, axis=(2, 3, 4)), jnp.sum(branch_dz * branch_hat, axis=(2, 3, 4))), "dp"
    )
    branch_dpre = expand_tail(gains[:4] * branch_inv, 3) * (
        branch_dz
        - expand_tail(branch_dbias / population, 3)
        - branch_hat * expand_tail(branch_dgain / population, 3)
    )
    branch_low = branch_dpre.astype(jnp.bfloat16)
    pool_low = (pool_grad * silu_slope(pool_pre)).astype(jnp.bfloat16)
    spatial_portion = lax.all_gather(branch_low, "chan", axis=1, tiled=True)
    pool_portion = lax.all_gather(pool_low, "chan", axis=1, tiled=True)
    pool_cols = w_pool.astype(jnp.float32)
    feature_grad = jnp.einsum(
        "co,onhw->nchw", w_one, spatial_portion[0], preferred_element_type=jnp.float32
    )
    patch_grad = jnp.einsum(
        "rtco,ronhw->rtnchw", w_atrous, spatial_portion[1:], preferred_element_type=jnp.float32
    )
    pool_wide = pool_portion[0].astype(jnp.float32)
    pooled_grad = jnp.dot(pool_wide.T, pool_cols.T, precision=highest)
    one_piece = jnp.einsum(
        "nchw,onhw->co", features, spatial_portion[0], preferred_element_type=jnp.float32
    )
    rate_piece = jnp.einsum(
        "rtnchw,ronhw->rtco", patches, spatial_portion[1:], preferred_element_type=jnp.float32
    )
    pool_piece = jnp.dot(pooled.T, pool_wide.T, precision=highest)
    one_grad = one_piece
    rate_grad = rate_piece
    pool_wgrad = pool_piece
    feature_grad, patch_grad, pooled_grad, one_grad, rate_grad, pool_wgrad = (
        feature_grad,
        patch_grad,
        pooled_grad,
        one_grad,
        rate_grad,
        pool_wgrad,
    )
    for branch, dilation in enumerate(atrous_rates):
        for tap_index, (vertical, horizontal) in enumerate(tap_offsets(dilation)):
            feature_grad = feature_grad + shifted(
                patch_grad[branch, tap_index], -vertical, -horizontal
            )
    feature_grad = feature_grad + (pooled_grad / pixels)[:, :, None, None]
    one_grad, rate_grad, pool_wgrad, proj_wgrad = (
        lax.psum(one_grad.astype(jnp.bfloat16), "dp").astype(jnp.float32),
        lax.psum(rate_grad.astype(jnp.bfloat16), "dp").astype(jnp.float32),
        lax.psum(pool_wgrad.astype(jnp.bfloat16), "dp").astype(jnp.float32),
        lax.psum(proj_wgrad.astype(jnp.bfloat16), "dp").astype(jnp.float32),
    )
    gains_grad = jnp.concatenate([branch_dgain, proj_dgain[None]])
    biases_grad = jnp.concatenate([branch_dbias, proj_dbias[None]])
    return (
        output,
        feature_grad,
        one_grad,
        rate_grad,
        pool_wgrad,
        proj_wgrad,
        gains_grad,
        biases_grad,
    )


MESH = pl.DeviceIdType.MESH
F32 = jnp.float32
BF16 = jnp.bfloat16
ROWS = 16
COLS = 128
PIXELS = ROWS * COLS
WIDE = PIXELS + 128
CIN_PART = 128
COUT = 256
GROUPS = 8
BLOCK = 256
ORDER = (0, 3, 2, 1)


def branch_rows(branch):
    if branch == 0:
        return [(None, 0)]
    rate = atrous_rates[branch - 1]
    return [(i, (i - 1) * rate) for i in (1, 0, 2) if abs((i - 1) * rate) < ROWS]


def weight_slots():
    slots = {}
    count = 0
    spans = {}
    for branch in ORDER:
        begin = count
        for i, _ in branch_rows(branch):
            slots[(branch, i)] = count
            count += 1 if branch == 0 else 3
        if branch == 0:
            slots["pool"] = count
            count += 1
        spans[branch] = (begin, count)
    return slots, spans, count


SLOTS, SPANS, NSLOTS = weight_slots()


HALVES = 2
SPAN = PIXELS // HALVES
PIECES = [(b, half * SPAN) for b in ORDER for half in range(HALVES)]


CROSS_FIRST = PIECES[-2:]


def carries_pool(piece):
    return piece == (0, PIXELS - SPAN)


def lanes_of(piece):
    return pl.ds(piece[1], SPAN + (128 if carries_pool(piece) else 0))


def dot(a, b):
    return jnp.dot(a, b, preferred_element_type=F32)


def dot_nt(a, b):
    return lax.dot_general(a, b, (((1,), (1,)), ((), ())), preferred_element_type=F32)


def iota(shape, dim):
    return lax.broadcasted_iota(jnp.int32, shape, dim)


def lane_sum(v):
    return jnp.sum(v, axis=1, keepdims=True)


def split_lanes(column, lanes=(0, 1, 2)):
    high = column.astype(BF16).astype(F32)
    mid = (column - high).astype(BF16).astype(F32)
    low = column - high - mid
    lane = iota((column.shape[0], 128), 1)
    out = jnp.where(lane == lanes[0], high, 0.0)
    out = out + jnp.where(lane == lanes[1], mid, 0.0)
    return out + jnp.where(lane == lanes[2], low, 0.0)


def encode_pair(v):
    lane = iota(v.shape, v.ndim - 1)
    high = v.astype(BF16).astype(F32)
    low = v - high
    return jnp.where(lane == 0, high, jnp.where(lane == 1, low, 0.0)).astype(BF16)


def decode_pair(e):
    return jnp.broadcast_to(jnp.sum(e.astype(F32), axis=-1, keepdims=True), e.shape)


def shift_cols(v, by):
    if by == 0:
        return v
    lane = iota((v.shape[0], 128), 1)
    keep = (lane >= by) if by > 0 else (lane < 128 + by)
    parts = []
    for h in range(v.shape[1] // 128):
        tile = v[:, h * 128 : (h + 1) * 128]
        parts.append(jnp.where(keep, pltpu.roll(tile, by % 128, 1), 0.0))
    return jnp.concatenate(parts, axis=1) if len(parts) > 1 else parts[0]


def sigmoid(z):
    return 0.5 * jnp.tanh(0.5 * z) + 0.5


INPUTS = ("feat", "og", "w1", "wa", "wpool", "wproj", "gains", "biases")
OUTPUTS = ("out", "dwpool", "dwproj", "dgains", "dbiases", "fgb", "dwb")


def scratch_table(sems):
    vm = pltpu.VMEM
    return {
        "outv": vm((256, 128), F32),
        "dwpoolv": vm((128, 256), F32),
        "dwprojv": vm((5, 16, 256), F32),
        "dgainsv": vm((5, 16), F32),
        "dbiasesv": vm((5, 16), F32),
        "feat": vm((2048, 128), BF16),
        "og": vm((256, 128), BF16),
        "w1": vm((128, 256), BF16),
        "wa": vm((27, 128, 256), BF16),
        "wpool": vm((128, 256), BF16),
        "wproj": vm((5, 16, 256), BF16),
        "gains": vm((5, 16), F32),
        "biases": vm((5, 16), F32),
        "xsib": vm((128, PIXELS), BF16),
        "tw": vm((NSLOTS, GROUPS, 2, 16, 128), BF16),
        "lw": vm((NSLOTS, GROUPS, 16, 256), BF16),
        "acc": vm((4, GROUPS, 16, PIXELS), F32),
        "acp": vm((GROUPS, 16, 128), F32),
        "ys": vm((4, 4, 16, WIDE), BF16),
        "yr": vm((4, 4, 16, WIDE), BF16),
        "zs": vm((4, 4, 16, WIDE), BF16),
        "zr": vm((4, 4, 16, WIDE), BF16),
        "g": vm((4, 2, GROUPS, 16, WIDE), BF16),
        "ogs": vm((2, GROUPS, 16, PIXELS), BF16),
        "pt": vm((GROUPS, 16, 128), F32),
        "wp": vm((GROUPS, 5, 16, 256), BF16),
        "wpt": vm((256, 640), BF16),
        "wps": vm((GROUPS, 2, 16, 128), BF16),
        "pools": vm((128, 128), F32),
        "poolo": vm((128, 128), F32),
        "poolr": vm((128, 128), F32),
        "pcol": vm((2, 128, 128), F32),
        "pps": vm((2, GROUPS, 16, PIXELS), BF16),
        "xv": vm((2, 7, 128, PIXELS), BF16),
        "sl": vm((2, 4, GROUPS, 16, PIXELS), BF16),
        "flip": vm((128, 128), F32),
        "c1": vm((5, 128, 128), F32),
        "c2": vm((5, 128, 128), F32),
        "act": vm((2, 4, GROUPS, 16, PIXELS), BF16),
        "ao": vm((2, 4, 16, PIXELS), BF16),
        "pa": vm((5, 128, 128), F32),
        "pb": vm((5, 128, 128), F32),
        "pm": vm((5, 128, 128), F32),
        "pi": vm((5, 128, 128), F32),
        "s1": vm((5, 128, 128), F32),
        "s2": vm((5, 128, 128), F32),
        "pr": vm((2, GROUPS, 16, PIXELS), BF16),
        "dzp": vm((2, GROUPS, 16, PIXELS), F32),
        "dp": vm((2, GROUPS, 2, 16, PIXELS), BF16),
        "dpo": vm((GROUPS, 2, 16, 128), BF16),
        "d": vm((4, 2, GROUPS, 2, 16, PIXELS), BF16),
        "dwv": vm((28, 128, 256), BF16),
        "rsum": vm((GROUPS, 2, 16, 128), F32),
        "fga": vm((128, PIXELS), F32),
        "fgv": vm((128, PIXELS), BF16),
        "pooled": vm((2, 128, 128), F32),
        "ppool": vm((2, 128, 128), F32),
        "ss": pltpu.SemaphoreType.DMA((sems,)),
        "rs": pltpu.SemaphoreType.DMA((sems,)),
        "ls": pltpu.SemaphoreType.DMA((32,)),
        "li": pltpu.SemaphoreType.DMA((8,)),
    }


class Refs:
    pass


NSEMS = 224


def head_kernel(*refs):
    names = tuple(n + "_hbm" for n in INPUTS) + OUTPUTS + tuple(scratch_table(NSEMS))
    r = Refs()
    for name, ref in zip(names, refs, strict=True):
        setattr(r, name, ref)
    x = lax.axis_index("dp")
    c = lax.axis_index("chan")
    k = lax.rem(c, 2)
    y = lax.rem(lax.div(c, 2), 2)
    z = lax.div(c, 4)

    def dev(xx, zz, yy, kk):
        return {"dp": xx, "chan": (zz * 2 + yy) * 2 + kk}

    sibling = dev(x, z, y, 1 - k)
    xdev = dev(1 - x, z, y, k)
    ydev = dev(x, z, 1 - y, k)
    zpos = [None] + [lax.rem(z + i, 4) for i in (1, 2, 3)]
    zfrom = [None] + [lax.rem(z + 4 - i, 4) for i in (1, 2, 3)]
    zdev = [None] + [dev(x, zpos[i], y, k) for i in (1, 2, 3)]

    counter = [0]
    sent = []
    due = {}

    def new(n=1):
        first = counter[0]
        counter[0] += n
        assert counter[0] <= NSEMS
        return first

    def rcopy(src, dst, n, device):
        return pltpu.make_async_remote_copy(
            src_ref=src,
            dst_ref=dst,
            send_sem=r.ss.at[n],
            recv_sem=r.rs.at[n],
            device_id=device,
            device_id_type=MESH,
        )

    def send(src, dst, n, device, group=None):
        copy = rcopy(src, dst, n, device)
        copy.start()
        (sent if group is None else group).append(copy)
        due[n] = (dst, device)

    def arrived(ref, n, device):
        del due[n]
        rcopy(ref, ref, n, device).wait_recv()

    barrier = pltpu.get_barrier_semaphore()
    partners = [sibling, xdev, ydev] + zdev[1:]
    for partner in partners:
        pl.semaphore_signal(barrier, inc=1, device_id=partner, device_id_type=MESH)

    loads = {}
    for n, name in enumerate(("feat", "w1", "wpool", "og", "gains", "biases", "wproj", "wa")):
        loads[name] = pltpu.make_async_copy(getattr(r, name + "_hbm"), getattr(r, name), r.li.at[n])
        loads[name].start()

    rr = iota((256, 256), 0)
    cc = iota((256, 256), 1)
    perm = jnp.where(cc == lax.rem(rr, 16) * 16 + lax.div(rr, 16), 1.0, 0.0).astype(BF16)
    eye = jnp.where(rr == cc, 1.0, 0.0).astype(BF16)

    def permuted(ref, block):
        return dot(perm, ref[block * 256 : (block + 1) * 256, :]).astype(BF16)

    def pre_group(yy, zz):
        return yy * 4 + zz

    def own_group(yy, zz):
        return zz * 2 + yy

    class Gather:
        def __init__(self, slot, group, across):
            self.slot, self.group, self.across = slot, group, across
            self.nz, self.ny, self.nx = new(3), new(4), new(8) if across else None

        def start(self):
            mine = self.slot(self.group(y, z))
            for i in (2, 1, 3):
                send(mine, mine, self.nz + i - 1, zdev[i])
            send(mine, mine, self.ny, ydev)
            if self.across:
                send(mine, mine, self.nx, xdev)

        def forward_z(self):
            for i in (1, 2, 3):
                ref = self.slot(self.group(y, zfrom[i]))
                arrived(ref, self.nz + i - 1, zdev[i])
                send(ref, ref, self.ny + i, ydev)
                if self.across:
                    send(ref, ref, self.nx + i, xdev)

        def forward_y(self):
            for i in range(4):
                ref = self.slot(self.group(1 - y, z if i == 0 else zfrom[i]))
                arrived(ref, self.ny + i, ydev)
                if self.across:
                    send(ref, ref, self.nx + 4 + i, xdev)

        def finish(self, other):
            if self.across:
                for i in range(8):
                    yy = y if i < 4 else 1 - y
                    zz = z if i % 4 == 0 else zfrom[i % 4]
                    arrived(other(self.group(yy, zz)), self.nx + i, xdev)

    g_og = Gather(lambda g: r.ogs.at[x, g], own_group, True)
    g_par = Gather(lambda g: r.pt.at[g], own_group, False)
    g_wp = Gather(lambda g: r.wp.at[g], own_group, False)
    def sums_slot(piece, image):
        return lambda g: r.g.at[piece[0], image, g, :, lanes_of(piece)]

    g_pre = {}
    g_other = {}
    n_cross = {}
    for piece in PIECES:
        g_pre[piece] = Gather(sums_slot(piece, x), pre_group, piece not in CROSS_FIRST)
        if piece in CROSS_FIRST:
            g_other[piece] = Gather(sums_slot(piece, 1 - x), pre_group, False)
            n_cross[piece] = new()

    mine = own_group(y, z)
    loads["og"].wait()
    og = permuted(r.og, 0)
    for h in range(ROWS):
        r.ogs[x, mine, :, h * 128 : (h + 1) * 128] = og[h * 16 : (h + 1) * 16]
    r.flip[...] = jnp.zeros((128, 128), F32)
    for name in ("gains", "biases", "wproj"):
        loads[name].wait()
    r.flip[0:5, 0:16] = r.gains[...]
    r.flip[8:13, 0:16] = r.biases[...]
    r.pt[mine] = r.flip[...].T[0:16, :]
    r.wp[mine] = r.wproj[...]

    n_w = {b: new() for b in ORDER}

    def weight_ref(b, i, j):
        return r.w1 if b == 0 else r.wa.at[(b - 1) * 9 + 3 * i + j]

    def transpose_into(slot, ref):
        t = dot_nt(eye, ref[...]).astype(BF16)
        r.tw[slot] = t.reshape(GROUPS, 2, 16, 128)
        r.lw[slot, :, :, 0:128] = r.tw[slot, :, k]

    def prepare_weights(b):
        for i, _ in branch_rows(b):
            slot = SLOTS[(b, i)]
            if b == 0:
                transpose_into(slot, r.w1)
                transpose_into(SLOTS["pool"], r.wpool)
            else:
                for j in range(3):
                    transpose_into(slot + j, weight_ref(b, i, j))

    def send_weights(b):
        lo, hi = SPANS[b]
        send(
            r.tw.at[pl.ds(lo, hi - lo), :, 1 - k],
            r.lw.at[pl.ds(lo, hi - lo), :, :, pl.ds(128, 128)],
            n_w[b],
            sibling,
        )

    def wait_weights(b):
        lo, hi = SPANS[b]
        arrived(r.lw.at[pl.ds(lo, hi - lo), :, :, pl.ds(128, 128)], n_w[b], sibling)

    for name in ("w1", "wpool", "feat"):
        loads[name].wait()
    for block in range(8):
        t = permuted(r.feat, block)
        for h in range(ROWS):
            px = slice(h * 128, (h + 1) * 128)
            r.xv[x, 0, block * 16 : (block + 1) * 16, px] = t[h * 16 : (h + 1) * 16]
    pooled = jnp.zeros((128, 128), F32)
    for h in range(ROWS):
        pooled = pooled + r.xv[x, 0, :, h * 128 : (h + 1) * 128].astype(F32)
    r.pooled[x] = jnp.broadcast_to(lane_sum(pooled) / PIXELS, (128, 128))
    prepare_weights(0)
    loads["wa"].wait()
    prepare_weights(ORDER[1])

    pl.semaphore_wait(barrier, len(partners))

    n_feat = new(2)
    n_foth = new()
    halves = [pl.ds(0, PIXELS // 2), pl.ds(PIXELS // 2, PIXELS // 2)]
    send_weights(0)
    for n in range(2):
        send(r.xv.at[x, 0, :, halves[n]], r.xsib.at[:, halves[n]], n_feat + n, sibling)
    send_weights(ORDER[1])
    send(r.xv.at[x, 0], r.xv.at[x, 0], n_foth, xdev)
    arrived(r.xsib.at[:, halves[0]], n_feat, sibling)

    def features_at(px):
        return jnp.concatenate([r.xv[x, 0, :, px], r.xsib[:, px]], axis=0)

    def convolve(piece):
        b = piece[0]
        for q in range(piece[1] // BLOCK, (piece[1] + SPAN) // BLOCK):
            px = slice(q * BLOCK, (q + 1) * BLOCK)
            total = None
            for i, offset in branch_rows(b):
                source = q + offset * COLS // BLOCK
                if source < 0 or source >= PIXELS // BLOCK:
                    continue
                slot = SLOTS[(b, i)]
                count = 1 if b == 0 else 3
                weights = r.lw[slot : slot + count].reshape(count * 128, 256)
                part = dot(weights, features_at(slice(source * BLOCK, (source + 1) * BLOCK)))
                total = part if total is None else total + part
            if b:
                rate = atrous_rates[b - 1]
                total = (
                    total[128:256]
                    + shift_cols(total[0:128], rate)
                    + shift_cols(total[256:384], -rate)
                )
            r.acc[b, :, :, px] = total.reshape(GROUPS, 16, BLOCK)
        if carries_pool(piece):
            pooled = jnp.zeros((128, 128), F32)
            for h in range(ROWS):
                pooled = pooled + r.xsib[:, h * 128 : (h + 1) * 128].astype(F32)
            column = jnp.concatenate([r.pooled[x][:, 0:1], lane_sum(pooled) / PIXELS], axis=0)
            terms = split_lanes(column).astype(BF16)
            slot = SLOTS["pool"]
            sums = lane_sum(dot(r.lw[slot].reshape(128, 256), terms))
            r.acp[...] = jnp.broadcast_to(sums, (128, 128)).reshape(GROUPS, 16, 128)

    n_ry = {piece: new() for piece in PIECES}
    n_rz = {piece: new(3) for piece in PIECES}

    def reduce_y_send(piece):
        b, w = piece[0], lanes_of(piece)
        px = pl.ds(piece[1], SPAN)
        r.ys[b, :, :, px] = r.acc[b, pl.ds(4 * (1 - y), 4), :, px].astype(BF16)
        if carries_pool(piece):
            r.ys[b, :, :, PIXELS:WIDE] = encode_pair(r.acp[pl.ds(4 * (1 - y), 4)])
        send(r.ys.at[b, :, :, w], r.yr.at[b, :, :, w], n_ry[piece], ydev)

    def reduce_z_send(piece):
        b, w = piece[0], lanes_of(piece)
        px = pl.ds(piece[1], SPAN)
        arrived(r.yr.at[b, :, :, w], n_ry[piece], ydev)
        for i in (2, 1, 3, 0):
            zz = z if i == 0 else zpos[i]
            g = 4 * y + zz
            s = r.acc[b, g, :, px] + r.yr[b, zz, :, px].astype(F32)
            if carries_pool(piece):
                e = r.acp[g] + decode_pair(r.yr[b, zz, :, PIXELS:WIDE])
            if i == 0:
                r.acc[b, g, :, px] = s
                if carries_pool(piece):
                    r.acp[g] = e
            else:
                r.zs[b, i, :, px] = s.astype(BF16)
                if carries_pool(piece):
                    r.zs[b, i, :, PIXELS:WIDE] = encode_pair(e)
                send(r.zs.at[b, i, :, w], r.zr.at[b, i, :, w], n_rz[piece] + i - 1, zdev[i])

    def reduce_finish(piece):
        b, w = piece[0], lanes_of(piece)
        px = pl.ds(piece[1], SPAN)
        g = pre_group(y, z)
        total = r.acc[b, g, :, px]
        extra = r.acp[g] if carries_pool(piece) else None
        for i in (1, 2, 3):
            arrived(r.zr.at[b, i, :, w], n_rz[piece] + i - 1, zdev[i])
            total = total + r.zr[b, i, :, px].astype(F32)
            if carries_pool(piece):
                extra = extra + decode_pair(r.zr[b, i, :, PIXELS:WIDE])
        r.g[b, x, g, :, px] = total.astype(BF16)
        if carries_pool(piece):
            r.g[b, x, g, :, PIXELS:WIDE] = encode_pair(extra)
        g_pre[piece].start()
        if piece in CROSS_FIRST:
            ref = sums_slot(piece, x)(g)
            send(ref, ref, n_cross[piece], xdev)

    def cross(piece):
        arrived(sums_slot(piece, 1 - x)(pre_group(y, z)), n_cross[piece], xdev)
        g_other[piece].start()

    shift_pairs = []
    lane_r = iota((128, 128), 0)
    lane_c = iota((128, 128), 1)
    for rate in atrous_rates:
        left = jnp.where(lane_r == lane_c - rate, 1.0, 0.0).astype(BF16)
        right = jnp.where(lane_r == lane_c + rate, 1.0, 0.0).astype(BF16)
        shift_pairs.append(jnp.concatenate([left, right], axis=1))

    local = []

    def keep(src, dst):
        copy = pltpu.make_async_copy(src, dst, r.ls.at[len(local)])
        copy.start()
        local.append(copy)

    def place_shifted(image):
        for h in range(ROWS):
            px = slice(h * 128, (h + 1) * 128)
            for a in range(3):
                both = dot(r.xv[image, 0, :, px], shift_pairs[a]).astype(BF16)
                r.xv[image, 1 + 2 * a, :, px] = both[:, 0:128]
                r.xv[image, 2 + 2 * a, :, px] = both[:, 128:256]

    count = float(2 * PIXELS)

    def each_group_loop(body):
        def step(g, _):
            body(g, pl.ds(pl.multiple_of(g * 16, 16), 16))
            return 0

        lax.fori_loop(0, GROUPS, step, 0)

    def each_group(body):
        for g in range(GROUPS):
            body(g, pl.ds(g * 16, 16))

    tiles = [(image, slice(h * 128, (h + 1) * 128)) for image in range(2) for h in range(ROWS)]
    zero_tile = jnp.zeros((16, 128), F32)

    def spread_lanes(column):
        return jnp.broadcast_to(column, (128, 128))

    def norm_params(b):
        mean = lane_sum(r.s1[b]) / count
        inv = lax.rsqrt(lane_sum(r.s2[b]) / count - mean * mean + norm_eps)
        par = r.pt[...].reshape(128, 128)
        scale = par[:, b : b + 1] * inv
        r.pa[b] = spread_lanes(scale)
        r.pb[b] = spread_lanes(par[:, 8 + b : 9 + b] - mean * scale)
        r.pm[b] = spread_lanes(mean)
        r.pi[b] = spread_lanes(inv)

    def grad_params(b):
        s1 = lane_sum(r.s1[b])
        inv, mean = r.pi[b][:, 0:1], r.pm[b][:, 0:1]
        s2 = (lane_sum(r.s2[b]) - mean * s1) * inv
        scale = r.pa[b][:, 0:1]
        c2 = -scale * inv * s2 / count
        r.s1[b] = spread_lanes(s1)
        r.s2[b] = spread_lanes(s2)
        r.c2[b] = spread_lanes(c2)
        r.c1[b] = spread_lanes(-scale * s1 / count - mean * c2)

    def act_and_slope(zed):
        u = 0.5 * jnp.tanh(0.5 * zed)
        sg = 0.5 + u
        act = zed * sg
        return act, sg + act * (0.5 - u)

    def branch_norm(b, each_group):
        def sums(g, rows):
            s, q = zero_tile, zero_tile
            for image, px in tiles:
                v = r.g[b, image, g, :, px].astype(F32)
                s = s + v
                q = q + v * v
            r.s1[b, rows] = s
            r.s2[b, rows] = q

        each_group(sums)
        norm_params(b)

        def apply(g, rows):
            scale, base = r.pa[b, rows], r.pb[b, rows]
            for image, px in tiles:
                act, slope = act_and_slope(r.g[b, image, g, :, px].astype(F32) * scale + base)
                r.act[image, b, g, :, px] = act.astype(BF16)
                r.sl[image, b, g, :, px] = slope.astype(BF16)

        each_group(apply)

    lane128 = iota((128, 128), 1)
    n_pool = new()

    def pool_part():
        pool_cols = jnp.zeros((128, 128), F32)
        for image in range(2):
            pre = decode_pair(r.g[0, image, :, :, PIXELS:WIDE]).reshape(128, 128)
            r.ppool[image] = pre
            pool_cols = pool_cols + jnp.where(lane128 == image, pre * sigmoid(pre), 0.0)
        pool_cols = pool_cols.astype(BF16)
        pool_out = dot(r.wpt[:, 512:640], pool_cols)
        r.poolo[...] = pool_out[0:128]

        r.pools[...] = pool_out[128:256]
        send(r.pools, r.poolr, n_pool, sibling)

    def finish_branch(b, groups):
        for piece in PIECES:
            if piece[0] != b:
                continue
            if piece in CROSS_FIRST:
                g_pre[piece].forward_y()
                g_other[piece].forward_y()
            else:
                g_pre[piece].finish(sums_slot(piece, 1 - x))
        branch_norm(b, groups)

    def projection_weights():
        for b in range(5):
            flat = dot_nt(eye, r.wp[:, b].reshape(128, 256)).astype(BF16)
            r.wps[...] = flat.reshape(GROUPS, 2, 16, 128)
            r.wpt[0:128, b * 128 : (b + 1) * 128] = r.wps[:, k].reshape(128, 128)
            r.wpt[128:256, b * 128 : (b + 1) * 128] = r.wps[:, 1 - k].reshape(128, 128)

    g_par.start()
    g_wp.start()
    steps = len(PIECES)
    for s in range(steps + 6):
        if s < steps:
            b = PIECES[s][0]
            if s % HALVES == 0:
                wait_weights(b)
            convolve(PIECES[s])
            if s == 0:
                arrived(r.xsib.at[:, halves[1]], n_feat + 1, sibling)
            reduce_y_send(PIECES[s])
            if s % HALVES == 0 and s // HALVES + 2 < len(ORDER):
                prepare_weights(ORDER[s // HALVES + 2])
                send_weights(ORDER[s // HALVES + 2])
        if s == 0:
            g_og.start()
        if 0 <= s - 2 < steps:
            reduce_z_send(PIECES[s - 2])
        if s == 2:
            g_par.forward_z()
            g_wp.forward_z()
            g_og.forward_z()
        if 0 <= s - 3 < steps:
            reduce_finish(PIECES[s - 3])
        if s == 4:
            g_par.forward_y()
            g_wp.forward_y()
            g_og.forward_y()
        if s == 8:
            projection_weights()
        if 0 <= s - 5 < steps:
            g_pre[PIECES[s - 5]].forward_z()
            if PIECES[s - 5] in CROSS_FIRST:
                cross(PIECES[s - 5])
        if 0 <= s - 6 < steps:
            if PIECES[s - 6] in CROSS_FIRST:
                g_other[PIECES[s - 6]].forward_z()
            else:
                g_pre[PIECES[s - 6]].forward_y()
        if s == 6:
            place_shifted(x)
        if s == 7:
            arrived(r.xv.at[1 - x, 0], n_foth, xdev)
            place_shifted(1 - x)
            pooled = jnp.zeros((128, 128), F32)
            for h in range(ROWS):
                pooled = pooled + r.xv[1 - x, 0, :, h * 128 : (h + 1) * 128].astype(F32)
            r.pooled[1 - x] = spread_lanes(lane_sum(pooled) / PIXELS)
        if s == 11:
            finish_branch(ORDER[0], each_group_loop)
            pool_part()
        if s == 12:
            finish_branch(ORDER[1], each_group_loop)

    for b in ORDER[2:]:
        finish_branch(b, each_group)

    n_pp = new(2)
    for image in range(2):
        for q in range(PIXELS // BLOCK):
            px = slice(q * BLOCK, (q + 1) * BLOCK)
            part = dot(r.wpt[:, 0:512], r.act[image, :, :, :, px].reshape(512, BLOCK))
            r.acc[image, :, :, px] = part[0:128].reshape(GROUPS, 16, BLOCK)
            r.pps[image, :, :, px] = part[128:256].astype(BF16).reshape(GROUPS, 16, BLOCK)
        send(r.pps.at[image], r.pr.at[image], n_pp + image, sibling)

    for image in range(2):
        for b in range(4):
            r.ao[image, b] = r.act[image, b, mine]

    g_og.finish(lambda g: r.ogs.at[1 - x, g])
    for image in range(2):
        arrived(r.pr.at[image], n_pp + image, sibling)

    arrived(r.poolr, n_pool, sibling)
    for image in range(2):
        r.pcol[image] = spread_lanes((r.poolo[...] + r.poolr[...])[:, image : image + 1])

    def proj_sums(g, rows):
        s, q = zero_tile, zero_tile
        for image, px in tiles:
            v = r.acc[image, g, :, px] + r.pr[image, g, :, px].astype(F32)
            v = v + r.pcol[image, rows]
            r.acc[image, g, :, px] = v
            s = s + v
            q = q + v * v
        r.s1[4, rows] = s
        r.s2[4, rows] = q

    each_group(proj_sums)
    norm_params(4)

    def proj_slope(g, rows):
        scale, base = r.pa[4, rows], r.pb[4, rows]
        s1, s2 = zero_tile, zero_tile
        for image, px in tiles:
            v = r.acc[image, g, :, px]
            _, slope = act_and_slope(v * scale + base)
            dz = r.ogs[image, g, :, px].astype(F32) * slope
            r.dzp[image, g, :, px] = dz
            s1 = s1 + dz
            s2 = s2 + dz * v
        r.s1[4, rows] = s1
        r.s2[4, rows] = s2

    each_group(proj_slope)
    grad_params(4)
    n_dp = new(2)
    for image in range(2):

        def proj_low(g, rows, image=image):
            scale, c1, c2 = r.pa[4, rows], r.c1[4, rows], r.c2[4, rows]
            total = zero_tile
            for h in range(ROWS):
                px = slice(h * 128, (h + 1) * 128)
                low = scale * r.dzp[image, g, :, px] + (r.acc[image, g, :, px] * c2 + c1)
                low = low.astype(BF16)
                r.dp[image, g, k, :, px] = low
                total = total + low.astype(F32)
            r.s1[image, rows] = total

        each_group(proj_low)
        ref = r.dp.at[image, :, k]
        send(ref, ref, n_dp + image, sibling)

    n_rsum = new()
    row_sums = jnp.where(lane128 == 0, lane_sum(r.s1[0]), 0.0)
    row_sums = row_sums + jnp.where(lane128 == 1, lane_sum(r.s1[1]), 0.0)
    r.rsum[:, k] = row_sums.reshape(GROUPS, 16, 128)
    ref = r.rsum.at[:, k]
    send(ref, ref, n_rsum, sibling)

    my_rows = pl.ds(pl.multiple_of(mine * 16, 16), 16)
    scale, base = r.pa[4, my_rows], r.pb[4, my_rows]
    for h in range(ROWS):
        zed = r.acc[x, mine, :, h * 128 : (h + 1) * 128] * scale + base
        r.outv[pl.ds(h, 16, stride=16), :] = zed * sigmoid(zed)
    keep(r.outv, r.out)

    for image in range(2):
        arrived(r.dp.at[image, :, 1 - k], n_dp + image, sibling)
    arrived(r.rsum.at[:, 1 - k], n_rsum, sibling)

    n_d = {b: new(2) for b in ORDER}

    def back_block(b, turn, image, q):
        px = slice(q * 512, (q + 1) * 512)
        dblock = r.dp[image, :, :, :, px].reshape(256, 512)
        back = dot(r.wp[:, b].reshape(128, 256), dblock)
        r.acc[2 * turn + image, :, :, px] = back.reshape(GROUPS, 16, 512)

    back_order = (1, 2, 3, 0)

    dwp = [jnp.zeros((64, 256), F32)]

    def proj_weights(image, q):
        px = slice(q * 512, (q + 1) * 512)
        acts = r.ao[image, :, :, px].reshape(64, 512)
        dwp[0] = dwp[0] + dot_nt(acts, r.dp[image, :, :, :, px].reshape(256, 512))

    def branch_back(b, turn):
        for image in range(2):
            for q in range(PIXELS // 512):
                back_block(b, turn, image, q)

        def slope(g, rows):
            s1, s2 = zero_tile, zero_tile
            for image, px in tiles:
                dz = r.acc[2 * turn + image, g, :, px] * r.sl[image, b, g, :, px].astype(F32)
                r.acc[2 * turn + image, g, :, px] = dz
                s1 = s1 + dz
                s2 = s2 + dz * r.g[b, image, g, :, px].astype(F32)
            r.s1[b, rows] = s1
            r.s2[b, rows] = s2
            if b == back_order[0]:
                proj_weights(g // 4, g % 4)

        each_group(slope)
        grad_params(b)
        for image in range(2):

            def lower(g, rows, image=image):
                scale, c1, c2 = r.pa[b, rows], r.c1[b, rows], r.c2[b, rows]
                for h in range(ROWS):
                    px = slice(h * 128, (h + 1) * 128)
                    v = r.g[b, image, g, :, px].astype(F32)
                    low = scale * r.acc[2 * turn + image, g, :, px] + (v * c2 + c1)
                    r.d[b, image, g, k, :, px] = low.astype(BF16)

            each_group(lower)
            there = r.d.at[b, image, :, k]
            send(there, there, n_d[b] + image, sibling)

    def wait_grads(*branches):
        for b in branches:
            for image in range(2):
                arrived(r.d.at[b, image, :, 1 - k], n_d[b] + image, sibling)

    def branch_grads(b, first_branch, last_branch):
        planes = (2 * b - 1, 0, 2 * b)
        for i, offset in branch_rows(b):
            first, last = max(0, -offset), min(ROWS, ROWS - offset)
            there = slice((first + offset) * 128, (last + offset) * 128)
            here = slice(first * 128, last * 128)
            total = None
            for image in range(2):
                if b == 0:
                    rows = r.xv[image, 0]
                else:
                    rows = jnp.concatenate([r.xv[image, p, :, there] for p in planes], axis=0)
                part = dot_nt(rows, r.d[b, image, :, :, :, here].reshape(256, -1))
                total = part if total is None else total + part
            total = total.astype(BF16)
            if b == 0:
                slot = pl.ds(27, 1)
                r.dwv[27] = total
            else:
                slot = pl.ds((b - 1) * 9 + 3 * i, 3)
                r.dwv[slot] = total.reshape(3, 128, 256)
            keep(r.dwv.at[slot], r.dwb.at[slot])
        for q in range(PIXELS // BLOCK):
            px = slice(q * BLOCK, (q + 1) * BLOCK)
            total = None
            for i, offset in branch_rows(b):
                source = q - offset * COLS // BLOCK
                if source < 0 or source >= PIXELS // BLOCK:
                    continue
                if b == 0:
                    weights = r.w1[...]
                else:
                    weights = r.wa[pl.ds((b - 1) * 9 + 3 * i, 3)].reshape(384, 256)
                dblock = r.d[b, x, :, :, :, source * BLOCK : (source + 1) * BLOCK]
                part = dot(weights, dblock.reshape(256, BLOCK))
                total = part if total is None else total + part
            if b:
                rate = atrous_rates[b - 1]
                total = (
                    total[128:256]
                    + shift_cols(total[0:128], -rate)
                    + shift_cols(total[256:384], rate)
                )
            if not first_branch:
                total = total + r.fga[:, px]
            if last_branch:
                r.fgv[:, px] = (total + fg_pool).astype(BF16)
            else:
                r.fga[:, px] = total

    wp4 = r.wp[:, 4].reshape(128, 256)
    dpo = jnp.zeros((128, 128), F32)
    dwp4 = jnp.zeros((16, 256), F32)
    lane16 = iota((16, 128), 1)
    for image in range(2):
        terms = split_lanes(r.rsum[...].reshape(256, 128)[:, image : image + 1]).astype(BF16)
        pool_grad = lane_sum(dot(wp4, terms))
        pre = r.ppool[image][:, 0:1]
        _, slope = act_and_slope(pre)
        low = (pool_grad * slope).astype(BF16).astype(F32)
        for lane in (image, image + 2, image + 4):
            dpo = dpo + jnp.where(lane128 == lane, low, 0.0)
        mine_act, _ = act_and_slope(r.ppool[image, my_rows][:, 0:1])
        mine_act = mine_act.astype(BF16).astype(F32)
        dwp4 = dwp4 + mine_act * dot_nt(jnp.ones((16, 128), BF16), terms)
    r.dwprojv[4] = dwp4
    r.dpo[:, k] = dpo.astype(BF16).reshape(GROUPS, 16, 128)
    n_dpo = new()
    for n, b in enumerate(back_order):
        branch_back(b, n % 2)
        if n == 0:
            ref = r.dpo.at[:, k]
            send(ref, ref, n_dpo, sibling)
            r.dwprojv[0:4] = dwp[0].reshape(4, 16, 256)
            keep(r.dwprojv, r.dwproj)
    wait_grads(back_order[0])
    branch_grads(back_order[0], True, False)
    wait_grads(*back_order[1:])
    branch_grads(back_order[1], False, False)

    tile = jnp.zeros((16, 128), F32)
    for b in range(5):
        tile = tile + jnp.where(lane16 == b, r.s2[b, my_rows], 0.0)
        tile = tile + jnp.where(lane16 == 8 + b, r.s1[b, my_rows], 0.0)
    r.flip[0:16, :] = tile
    flipped = r.flip[...].T
    r.dgainsv[...] = flipped[0:5, 0:16]
    r.dbiasesv[...] = flipped[8:13, 0:16]
    keep(r.dgainsv, r.dgains)
    keep(r.dbiasesv, r.dbiases)

    branch_grads(back_order[2], False, False)

    arrived(r.dpo.at[:, 1 - k], n_dpo, sibling)
    dpo = r.dpo[...].reshape(256, 128)
    pooled = jnp.zeros((128, 128), F32)
    for image in range(2):
        pooled = pooled + split_lanes(r.pooled[image][:, 0:1], (image, image + 2, image + 4))
    r.dwpoolv[...] = dot_nt(pooled.astype(BF16), dpo)
    keep(r.dwpoolv, r.dwpool)
    spread = dot(r.wpool[...], dpo)
    fg_pool = lane_sum(jnp.where(lane128 == x, spread, 0.0)) / PIXELS

    branch_grads(back_order[3], False, True)
    keep(r.fgv, r.fgb)
    for copy in sent:
        copy.wait_send()
    for copy in local:
        copy.wait()


COPY_INPUTS = ("out", "dwpool", "dwproj", "dgains", "dbiases", "fgb", "dwb")
COPY_OUTPUTS = ("out_o", "dwpool_o", "dwproj_o", "dgains_o", "dbiases_o", "fg", "dw1", "dwa")
COPY_SCRATCH = {
    "outv": pltpu.VMEM((256, 128), F32),
    "dwpoolv": pltpu.VMEM((128, 256), F32),
    "dwprojv": pltpu.VMEM((5, 16, 256), F32),
    "fgbv": pltpu.VMEM((128, PIXELS), BF16),
    "dwbv": pltpu.VMEM((28, 128, 256), BF16),
    "fgv": pltpu.VMEM((2048, 128), F32),
    "dwv": pltpu.VMEM((28, 128, 256), F32),
    "si": pltpu.SemaphoreType.DMA((16,)),
    "so": pltpu.SemaphoreType.DMA((16,)),
}


def copy_kernel(*refs):
    r = Refs()
    names = COPY_INPUTS + COPY_OUTPUTS + tuple(COPY_SCRATCH)
    for name, ref in zip(names, refs, strict=True):
        setattr(r, name, ref)
    loads = []
    stores = []

    def load(src, dst):
        copy = pltpu.make_async_copy(src, dst, r.si.at[len(loads)])
        copy.start()
        loads.append(copy)
        return copy

    def store(src, dst):
        copy = pltpu.make_async_copy(src, dst, r.so.at[len(stores)])
        copy.start()
        stores.append(copy)

    met = [
        (b - 1) * 9 + 3 * i for b in (1, 2, 3) for i in range(3) if i in dict(branch_rows(b))
    ]
    taps = [(n, load(r.dwb.at[pl.ds(n, 3)], r.dwbv.at[pl.ds(n, 3)])) for n in met]
    one = load(r.dwb.at[pl.ds(27, 1)], r.dwbv.at[pl.ds(27, 1)])
    fg = load(r.fgb, r.fgbv)
    passed = [
        (load(getattr(r, name), getattr(r, name + "v")), name)
        for name in ("out", "dwpool", "dwproj")
    ]
    r.dgains_o[...] = r.dgains[...]
    r.dbiases_o[...] = r.dbiases[...]
    for n in range(0, 27, 3):
        if n not in met:
            r.dwv[n : n + 3] = jnp.zeros((3, 128, 256), F32)
            store(r.dwv.at[pl.ds(n, 3)], r.dwa.at[pl.ds(n, 3)])
    for n, copy in taps:
        copy.wait()
        r.dwv[n : n + 3] = r.dwbv[n : n + 3].astype(F32)
        store(r.dwv.at[pl.ds(n, 3)], r.dwa.at[pl.ds(n, 3)])
    one.wait()
    r.dwv[27] = r.dwbv[27].astype(F32)
    store(r.dwv.at[27], r.dw1)
    fg.wait()
    for h in range(ROWS):
        r.fgv[pl.ds(h, 128, stride=16), :] = r.fgbv[:, h * 128 : (h + 1) * 128].astype(F32)
    store(r.fgv, r.fg)
    for copy, name in passed:
        copy.wait()
        store(getattr(r, name + "v"), getattr(r, name + "_o"))
    for copy in stores:
        copy.wait()


def fused(features, w_one, w_atrous, w_pool, w_proj, gains, biases, out_grad):
    vmem = pl.BlockSpec(memory_space=pltpu.VMEM)
    hbm = pl.BlockSpec(memory_space=pl.ANY)
    passed = [(256, 128), (128, 256), (5, 16, 256), (5, 16), (5, 16)]
    shapes = [jax.ShapeDtypeStruct(s, F32) for s in passed]
    shapes.append(jax.ShapeDtypeStruct((128, PIXELS), BF16))
    shapes.append(jax.ShapeDtypeStruct((28, 128, 256), BF16))
    parts = pl.pallas_call(
        head_kernel,
        out_shape=shapes,
        in_specs=[hbm] * len(INPUTS),
        out_specs=[hbm] * len(OUTPUTS),
        scratch_shapes=list(scratch_table(NSEMS).values()),
        compiler_params=pltpu.CompilerParams(
            collective_id=0, has_side_effects=True, vmem_limit_bytes=64 * 2**20
        ),
    )(
        features.reshape(2048, 128),
        out_grad.reshape(256, 128),
        w_one,
        w_atrous.reshape(27, 128, 256),
        w_pool,
        w_proj,
        gains,
        biases,
    )
    result = passed + [(2048, 128), (128, 256), (27, 128, 256)]
    out, dwpool, dwproj, dgains, dbiases, fg, dw1, dwa = pl.pallas_call(
        copy_kernel,
        out_shape=[jax.ShapeDtypeStruct(s, F32) for s in result],
        in_specs=[hbm] * 3 + [vmem] * 2 + [hbm] * 2,
        out_specs=[hbm] * 3 + [vmem] * 2 + [hbm] * 3,
        scratch_shapes=list(COPY_SCRATCH.values()),
        compiler_params=pltpu.CompilerParams(vmem_limit_bytes=64 * 2**20),
    )(*parts)
    return (
        out.reshape(1, 16, ROWS, COLS),
        fg.reshape(1, 128, ROWS, COLS),
        dw1,
        dwa.reshape(3, 9, 128, 256),
        dwpool,
        dwproj,
        dgains,
        dbiases,
    )


def solution(mesh):
    placed = (
        P("dp", "chan", None, None),
        P("chan", None),
        P(None, None, "chan", None),
        P("chan", None),
        P(None, "chan", None),
        P(None, "chan"),
        P(None, "chan"),
        P("dp", "chan", None, None),
    )
    small = mesh.shape["dp"] == 2 and mesh.shape["chan"] == 16
    return jax.shard_map(
        fused if small else local,
        mesh=mesh,
        in_specs=placed,
        out_specs=(
            P("dp", "chan", None, None),
            P("dp", "chan", None, None),
            P("chan", None),
            P(None, None, "chan", None),
            P("chan", None),
            P(None, "chan", None),
            P(None, "chan"),
            P(None, "chan"),
        ),
        check_vma=False,
    )
```

```python
import functools

import jax
import jax.numpy as jnp
from jax import lax
from jax.experimental import pallas as pl
from jax.experimental.pallas import tpu as pltpu
from jax.sharding import PartitionSpec as P

atrous_rates = (6, 12, 18)
norm_eps = 1e-05


def shifted(values, vertical, horizontal):
    margin = max(abs(vertical), abs(horizontal))
    if margin == 0:
        return values
    height = values.shape[-2]
    breadth = values.shape[-1]
    spacing = [(0, 0)] * (values.ndim - 2) + [(margin, margin), (margin, margin)]
    padded = jnp.pad(values, spacing)
    return padded[
        ...,
        margin + vertical : margin + vertical + height,
        margin + horizontal : margin + horizontal + breadth,
    ]


def tap_offsets(dilation):
    return [
        ((along_rows - 1) * dilation, (along_cols - 1) * dilation)
        for along_rows in range(3)
        for along_cols in range(3)
    ]


def make_patches(features, dilation):
    return jnp.stack(
        [shifted(features, vertical, horizontal) for vertical, horizontal in tap_offsets(dilation)]
    )


def silu_slope(values):
    sigmoid = jax.nn.sigmoid(values)
    return sigmoid * (1.0 + values * (1.0 - sigmoid))


def expand_tail(values, extra):
    return values.reshape(values.shape + (1,) * extra)


def local(features, w_one, w_atrous, w_pool, w_proj, gains, biases, out_grad):
    highest = lax.Precision.HIGHEST
    images, local_in, height, columns = features.shape
    pixels = height * columns
    population = images * pixels * lax.axis_size("dp")
    patches = jnp.stack([make_patches(features, dilation) for dilation in atrous_rates])
    pooled = jnp.sum(features, axis=(2, 3), dtype=jnp.float32) / pixels
    one_term = jnp.einsum("nchw,co->onhw", features, w_one, preferred_element_type=jnp.float32)
    rate_terms = jnp.einsum(
        "rtnchw,rtco->ronhw", patches, w_atrous, preferred_element_type=jnp.float32
    )
    spatial_term = jnp.concatenate([one_term[None], rate_terms])
    pool_term = jnp.dot(pooled, w_pool.astype(jnp.float32), precision=highest).T[None]
    branch_pre, pool_pre = (
        lax.psum_scatter(spatial_term, "chan", scatter_dimension=1, tiled=True),
        lax.psum_scatter(pool_term, "chan", scatter_dimension=1, tiled=True),
    )
    branch_totals, branch_squares = lax.psum(
        (jnp.sum(branch_pre, axis=(2, 3, 4)), jnp.sum(branch_pre * branch_pre, axis=(2, 3, 4))),
        "dp",
    )
    branch_mean = branch_totals / population
    branch_inv = lax.rsqrt(branch_squares / population - branch_mean * branch_mean + norm_eps)
    centred = branch_pre - expand_tail(branch_mean, 3)
    branch_z = centred * expand_tail(gains[:4] * branch_inv, 3) + expand_tail(biases[:4], 3)
    branch_hat = centred * expand_tail(branch_inv, 3)
    act_low = jax.nn.silu(branch_z).astype(jnp.bfloat16)
    pool_act = jax.nn.silu(pool_pre).astype(jnp.bfloat16)
    window = w_proj
    spatial = jnp.einsum("bonhw,bod->dnhw", act_low, window[:4], preferred_element_type=jnp.float32)
    pool_part = jnp.einsum("bon,bod->dn", pool_act, window[4:], preferred_element_type=jnp.float32)
    proj_pre = lax.psum_scatter(
        spatial + pool_part[:, :, None, None], "chan", scatter_dimension=0, tiled=True
    )
    proj_totals, proj_squares = lax.psum(
        (jnp.sum(proj_pre, axis=(1, 2, 3)), jnp.sum(proj_pre * proj_pre, axis=(1, 2, 3))), "dp"
    )
    proj_mean = proj_totals / population
    proj_inv = lax.rsqrt(proj_squares / population - proj_mean * proj_mean + norm_eps)
    proj_centred = proj_pre - expand_tail(proj_mean, 3)
    proj_z = proj_centred * expand_tail(gains[4] * proj_inv, 3) + expand_tail(biases[4], 3)
    proj_hat = proj_centred * expand_tail(proj_inv, 3)
    output = jnp.transpose(jax.nn.silu(proj_z), (1, 0, 2, 3))
    grad_out = jnp.transpose(out_grad, (1, 0, 2, 3)).astype(jnp.float32)
    proj_dz = grad_out * silu_slope(proj_z)
    proj_dbias, proj_dgain = lax.psum(
        (jnp.sum(proj_dz, axis=(1, 2, 3)), jnp.sum(proj_dz * proj_hat, axis=(1, 2, 3))), "dp"
    )
    proj_dpre = expand_tail(gains[4] * proj_inv, 3) * (
        proj_dz
        - expand_tail(proj_dbias / population, 3)
        - proj_hat * expand_tail(proj_dgain / population, 3)
    )
    proj_low = proj_dpre.astype(jnp.bfloat16)
    pool_act_wide = pool_act.astype(jnp.float32)
    portion = lax.all_gather(proj_low, "chan", axis=0, tiled=True)
    window = w_proj
    act_grad = jnp.einsum(
        "bod,dnhw->bonhw", window[:4], portion, preferred_element_type=jnp.float32
    )
    portion_sum = jnp.sum(portion, axis=(2, 3), dtype=jnp.float32)
    pool_grad = jnp.einsum(
        "bod,dn->bon", window[4:].astype(jnp.float32), portion_sum, precision=highest
    )
    spatial_part = jnp.einsum(
        "bonhw,dnhw->bod", act_low, portion, preferred_element_type=jnp.float32
    )
    pool_part = jnp.einsum("bon,dn->bod", pool_act_wide, portion_sum, precision=highest)
    weight_grad = jnp.concatenate([spatial_part, pool_part])
    act_grad, pool_grad, proj_wgrad = (act_grad, pool_grad, weight_grad)
    branch_dz = act_grad * silu_slope(branch_z)
    branch_dbias, branch_dgain = lax.psum(
        (jnp.sum(branch_dz, axis=(2, 3, 4)), jnp.sum(branch_dz * branch_hat, axis=(2, 3, 4))), "dp"
    )
    branch_dpre = expand_tail(gains[:4] * branch_inv, 3) * (
        branch_dz
        - expand_tail(branch_dbias / population, 3)
        - branch_hat * expand_tail(branch_dgain / population, 3)
    )
    branch_low = branch_dpre.astype(jnp.bfloat16)
    pool_low = (pool_grad * silu_slope(pool_pre)).astype(jnp.bfloat16)
    spatial_portion = lax.all_gather(branch_low, "chan", axis=1, tiled=True)
    pool_portion = lax.all_gather(pool_low, "chan", axis=1, tiled=True)
    pool_cols = w_pool.astype(jnp.float32)
    feature_grad = jnp.einsum(
        "co,onhw->nchw", w_one, spatial_portion[0], preferred_element_type=jnp.float32
    )
    patch_grad = jnp.einsum(
        "rtco,ronhw->rtnchw", w_atrous, spatial_portion[1:], preferred_element_type=jnp.float32
    )
    pool_wide = pool_portion[0].astype(jnp.float32)
    pooled_grad = jnp.dot(pool_wide.T, pool_cols.T, precision=highest)
    one_piece = jnp.einsum(
        "nchw,onhw->co", features, spatial_portion[0], preferred_element_type=jnp.float32
    )
    rate_piece = jnp.einsum(
        "rtnchw,ronhw->rtco", patches, spatial_portion[1:], preferred_element_type=jnp.float32
    )
    pool_piece = jnp.dot(pooled.T, pool_wide.T, precision=highest)
    one_grad = one_piece
    rate_grad = rate_piece
    pool_wgrad = pool_piece
    feature_grad, patch_grad, pooled_grad, one_grad, rate_grad, pool_wgrad = (
        feature_grad,
        patch_grad,
        pooled_grad,
        one_grad,
        rate_grad,
        pool_wgrad,
    )
    for branch, dilation in enumerate(atrous_rates):
        for tap_index, (vertical, horizontal) in enumerate(tap_offsets(dilation)):
            feature_grad = feature_grad + shifted(
                patch_grad[branch, tap_index], -vertical, -horizontal
            )
    feature_grad = feature_grad + (pooled_grad / pixels)[:, :, None, None]
    one_grad, rate_grad, pool_wgrad, proj_wgrad = (
        lax.psum(one_grad.astype(jnp.bfloat16), "dp").astype(jnp.float32),
        lax.psum(rate_grad.astype(jnp.bfloat16), "dp").astype(jnp.float32),
        lax.psum(pool_wgrad.astype(jnp.bfloat16), "dp").astype(jnp.float32),
        lax.psum(proj_wgrad.astype(jnp.bfloat16), "dp").astype(jnp.float32),
    )
    gains_grad = jnp.concatenate([branch_dgain, proj_dgain[None]])
    biases_grad = jnp.concatenate([branch_dbias, proj_dbias[None]])
    return (
        output,
        feature_grad,
        one_grad,
        rate_grad,
        pool_wgrad,
        proj_wgrad,
        gains_grad,
        biases_grad,
    )


MESH = pl.DeviceIdType.MESH
F32 = jnp.float32
BF16 = jnp.bfloat16
ROWS = 16
COLS = 128
PIXELS = ROWS * COLS
WIDE = PIXELS + 128
CIN_PART = 128
COUT = 256
GROUPS = 8
BLOCK = 256
ORDER = (0, 3, 2, 1)


def branch_rows(branch):
    if branch == 0:
        return [(None, 0)]
    rate = atrous_rates[branch - 1]
    return [(i, (i - 1) * rate) for i in (1, 0, 2) if abs((i - 1) * rate) < ROWS]


def weight_slots():
    slots = {}
    count = 0
    spans = {}
    for branch in ORDER:
        begin = count
        for i, _ in branch_rows(branch):
            slots[(branch, i)] = count
            count += 1 if branch == 0 else 3
        if branch == 0:
            slots["pool"] = count
            count += 1
        spans[branch] = (begin, count)
    return slots, spans, count


SLOTS, SPANS, NSLOTS = weight_slots()


HALVES = 2
SPAN = PIXELS // HALVES
PIECES = [(b, half * SPAN) for b in ORDER for half in range(HALVES)]


CROSS_FIRST = PIECES[-2:]


def carries_pool(piece):
    return piece == (0, PIXELS - SPAN)


def lanes_of(piece):
    return pl.ds(piece[1], SPAN + (128 if carries_pool(piece) else 0))


def dot(a, b):
    return jnp.dot(a, b, preferred_element_type=F32)


def dot_nt(a, b):
    return lax.dot_general(a, b, (((1,), (1,)), ((), ())), preferred_element_type=F32)


def iota(shape, dim):
    return lax.broadcasted_iota(jnp.int32, shape, dim)


def lane_sum(v):
    return jnp.sum(v, axis=1, keepdims=True)


def split_lanes(column, lanes=(0, 1, 2)):
    high = column.astype(BF16).astype(F32)
    mid = (column - high).astype(BF16).astype(F32)
    low = column - high - mid
    lane = iota((column.shape[0], 128), 1)
    out = jnp.where(lane == lanes[0], high, 0.0)
    out = out + jnp.where(lane == lanes[1], mid, 0.0)
    return out + jnp.where(lane == lanes[2], low, 0.0)


def encode_pair(v):
    lane = iota(v.shape, v.ndim - 1)
    high = v.astype(BF16).astype(F32)
    low = v - high
    return jnp.where(lane == 0, high, jnp.where(lane == 1, low, 0.0)).astype(BF16)


def decode_pair(e):
    return jnp.broadcast_to(jnp.sum(e.astype(F32), axis=-1, keepdims=True), e.shape)


def shift_cols(v, by):
    if by == 0:
        return v
    lane = iota((v.shape[0], 128), 1)
    keep = (lane >= by) if by > 0 else (lane < 128 + by)
    parts = []
    for h in range(v.shape[1] // 128):
        tile = v[:, h * 128 : (h + 1) * 128]
        parts.append(jnp.where(keep, pltpu.roll(tile, by % 128, 1), 0.0))
    return jnp.concatenate(parts, axis=1) if len(parts) > 1 else parts[0]


def sigmoid(z):
    return 0.5 * jnp.tanh(0.5 * z) + 0.5


INPUTS = ("feat", "og", "w1", "wa", "wpool", "wproj", "gains", "biases")
OUTPUTS = ("out", "dwpool", "dwproj", "dgains", "dbiases", "fgb", "dwb")


def scratch_table(sems):
    vm = pltpu.VMEM
    return {
        "outv": vm((256, 128), F32),
        "dwpoolv": vm((128, 256), F32),
        "dwprojv": vm((5, 16, 256), F32),
        "dgainsv": vm((5, 16), F32),
        "dbiasesv": vm((5, 16), F32),
        "feat": vm((2048, 128), BF16),
        "og": vm((256, 128), BF16),
        "w1": vm((128, 256), BF16),
        "wa": vm((27, 128, 256), BF16),
        "wpool": vm((128, 256), BF16),
        "wproj": vm((5, 16, 256), BF16),
        "gains": vm((5, 16), F32),
        "biases": vm((5, 16), F32),
        "xsib": vm((128, PIXELS), BF16),
        "tw": vm((NSLOTS, GROUPS, 2, 16, 128), BF16),
        "lw": vm((NSLOTS, GROUPS, 16, 256), BF16),
        "acc": vm((4, GROUPS, 16, PIXELS), F32),
        "acp": vm((GROUPS, 16, 128), F32),
        "ys": vm((4, 4, 16, WIDE), BF16),
        "yr": vm((4, 4, 16, WIDE), BF16),
        "zs": vm((4, 4, 16, WIDE), BF16),
        "zr": vm((4, 4, 16, WIDE), BF16),
        "g": vm((4, 2, GROUPS, 16, WIDE), BF16),
        "ogs": vm((2, GROUPS, 16, PIXELS), BF16),
        "pt": vm((GROUPS, 16, 128), F32),
        "wp": vm((GROUPS, 5, 16, 256), BF16),
        "wpt": vm((256, 640), BF16),
        "wps": vm((GROUPS, 2, 16, 128), BF16),
        "pools": vm((128, 128), F32),
        "poolo": vm((128, 128), F32),
        "poolr": vm((128, 128), F32),
        "pcol": vm((2, 128, 128), F32),
        "pps": vm((2, GROUPS, 16, PIXELS), BF16),
        "xv": vm((2, 7, 128, PIXELS), BF16),
        "sl": vm((2, 4, GROUPS, 16, PIXELS), BF16),
        "flip": vm((128, 128), F32),
        "c1": vm((5, 128, 128), F32),
        "c2": vm((5, 128, 128), F32),
        "act": vm((2, 4, GROUPS, 16, PIXELS), BF16),
        "ao": vm((2, 4, 16, PIXELS), BF16),
        "pa": vm((5, 128, 128), F32),
        "pb": vm((5, 128, 128), F32),
        "pm": vm((5, 128, 128), F32),
        "pi": vm((5, 128, 128), F32),
        "s1": vm((5, 128, 128), F32),
        "s2": vm((5, 128, 128), F32),
        "pr": vm((2, GROUPS, 16, PIXELS), BF16),
        "dzp": vm((2, GROUPS, 16, PIXELS), F32),
        "dp": vm((2, GROUPS, 2, 16, PIXELS), BF16),
        "dpo": vm((GROUPS, 2, 16, 128), BF16),
        "d": vm((4, 2, GROUPS, 2, 16, PIXELS), BF16),
        "dwv": vm((28, 128, 256), BF16),
        "rsum": vm((GROUPS, 2, 16, 128), F32),
        "fga": vm((128, PIXELS), F32),
        "fgv": vm((128, PIXELS), BF16),
        "pooled": vm((2, 128, 128), F32),
        "ppool": vm((2, 128, 128), F32),
        "ss": pltpu.SemaphoreType.DMA((sems,)),
        "rs": pltpu.SemaphoreType.DMA((sems,)),
        "ls": pltpu.SemaphoreType.DMA((32,)),
        "li": pltpu.SemaphoreType.DMA((8,)),
    }


class Refs:
    pass


NSEMS = 224


def head_kernel(*refs):
    names = tuple(n + "_hbm" for n in INPUTS) + OUTPUTS + tuple(scratch_table(NSEMS))
    r = Refs()
    for name, ref in zip(names, refs, strict=True):
        setattr(r, name, ref)
    x = lax.axis_index("dp")
    c = lax.axis_index("chan")
    k = lax.rem(c, 2)
    y = lax.rem(lax.div(c, 2), 2)
    z = lax.div(c, 4)

    def dev(xx, zz, yy, kk):
        return {"dp": xx, "chan": (zz * 2 + yy) * 2 + kk}

    sibling = dev(x, z, y, 1 - k)
    xdev = dev(1 - x, z, y, k)
    ydev = dev(x, z, 1 - y, k)
    zpos = [None] + [lax.rem(z + i, 4) for i in (1, 2, 3)]
    zfrom = [None] + [lax.rem(z + 4 - i, 4) for i in (1, 2, 3)]
    zdev = [None] + [dev(x, zpos[i], y, k) for i in (1, 2, 3)]

    counter = [0]
    sent = []
    due = {}

    def new(n=1):
        first = counter[0]
        counter[0] += n
        assert counter[0] <= NSEMS
        return first

    def rcopy(src, dst, n, device):
        return pltpu.make_async_remote_copy(
            src_ref=src,
            dst_ref=dst,
            send_sem=r.ss.at[n],
            recv_sem=r.rs.at[n],
            device_id=device,
            device_id_type=MESH,
        )

    def send(src, dst, n, device, group=None):
        copy = rcopy(src, dst, n, device)
        copy.start()
        (sent if group is None else group).append(copy)
        due[n] = (dst, device)

    def arrived(ref, n, device):
        del due[n]
        rcopy(ref, ref, n, device).wait_recv()

    barrier = pltpu.get_barrier_semaphore()
    partners = [sibling, xdev, ydev] + zdev[1:]
    for partner in partners:
        pl.semaphore_signal(barrier, inc=1, device_id=partner, device_id_type=MESH)

    loads = {}
    for n, name in enumerate(("feat", "w1", "wpool", "og", "gains", "biases", "wproj", "wa")):
        loads[name] = pltpu.make_async_copy(getattr(r, name + "_hbm"), getattr(r, name), r.li.at[n])
        loads[name].start()

    rr = iota((256, 256), 0)
    cc = iota((256, 256), 1)
    perm = jnp.where(cc == lax.rem(rr, 16) * 16 + lax.div(rr, 16), 1.0, 0.0).astype(BF16)
    eye = jnp.where(rr == cc, 1.0, 0.0).astype(BF16)

    def permuted(ref, block):
        return dot(perm, ref[block * 256 : (block + 1) * 256, :]).astype(BF16)

    def pre_group(yy, zz):
        return yy * 4 + zz

    def own_group(yy, zz):
        return zz * 2 + yy

    class Gather:
        def __init__(self, slot, group, across):
            self.slot, self.group, self.across = slot, group, across
            self.nz, self.ny, self.nx = new(3), new(4), new(8) if across else None

        def start(self):
            mine = self.slot(self.group(y, z))
            for i in (2, 1, 3):
                send(mine, mine, self.nz + i - 1, zdev[i])
            send(mine, mine, self.ny, ydev)
            if self.across:
                send(mine, mine, self.nx, xdev)

        def forward_z(self):
            for i in (1, 2, 3):
                ref = self.slot(self.group(y, zfrom[i]))
                arrived(ref, self.nz + i - 1, zdev[i])
                send(ref, ref, self.ny + i, ydev)
                if self.across:
                    send(ref, ref, self.nx + i, xdev)

        def forward_y(self):
            for i in range(4):
                ref = self.slot(self.group(1 - y, z if i == 0 else zfrom[i]))
                arrived(ref, self.ny + i, ydev)
                if self.across:
                    send(ref, ref, self.nx + 4 + i, xdev)

        def finish(self, other):
            if self.across:
                for i in range(8):
                    yy = y if i < 4 else 1 - y
                    zz = z if i % 4 == 0 else zfrom[i % 4]
                    arrived(other(self.group(yy, zz)), self.nx + i, xdev)

    g_og = Gather(lambda g: r.ogs.at[x, g], own_group, True)
    g_par = Gather(lambda g: r.pt.at[g], own_group, False)
    g_wp = Gather(lambda g: r.wp.at[g], own_group, False)
    def sums_slot(piece, image):
        return lambda g: r.g.at[piece[0], image, g, :, lanes_of(piece)]

    g_pre = {}
    g_other = {}
    n_cross = {}
    for piece in PIECES:
        g_pre[piece] = Gather(sums_slot(piece, x), pre_group, piece not in CROSS_FIRST)
        if piece in CROSS_FIRST:
            g_other[piece] = Gather(sums_slot(piece, 1 - x), pre_group, False)
            n_cross[piece] = new()

    mine = own_group(y, z)
    loads["og"].wait()
    og = permuted(r.og, 0)
    for h in range(ROWS):
        r.ogs[x, mine, :, h * 128 : (h + 1) * 128] = og[h * 16 : (h + 1) * 16]
    r.flip[...] = jnp.zeros((128, 128), F32)
    for name in ("gains", "biases", "wproj"):
        loads[name].wait()
    r.flip[0:5, 0:16] = r.gains[...]
    r.flip[8:13, 0:16] = r.biases[...]
    r.pt[mine] = r.flip[...].T[0:16, :]
    r.wp[mine] = r.wproj[...]

    n_w = {b: new() for b in ORDER}

    def weight_ref(b, i, j):
        return r.w1 if b == 0 else r.wa.at[(b - 1) * 9 + 3 * i + j]

    def transpose_into(slot, ref):
        t = dot_nt(eye, ref[...]).astype(BF16)
        r.tw[slot] = t.reshape(GROUPS, 2, 16, 128)
        r.lw[slot, :, :, 0:128] = r.tw[slot, :, k]

    def prepare_weights(b):
        for i, _ in branch_rows(b):
            slot = SLOTS[(b, i)]
            if b == 0:
                transpose_into(slot, r.w1)
                transpose_into(SLOTS["pool"], r.wpool)
            else:
                for j in range(3):
                    transpose_into(slot + j, weight_ref(b, i, j))

    def send_weights(b):
        lo, hi = SPANS[b]
        send(
            r.tw.at[pl.ds(lo, hi - lo), :, 1 - k],
            r.lw.at[pl.ds(lo, hi - lo), :, :, pl.ds(128, 128)],
            n_w[b],
            sibling,
        )

    def wait_weights(b):
        lo, hi = SPANS[b]
        arrived(r.lw.at[pl.ds(lo, hi - lo), :, :, pl.ds(128, 128)], n_w[b], sibling)

    for name in ("w1", "wpool", "feat"):
        loads[name].wait()
    for block in range(8):
        t = permuted(r.feat, block)
        for h in range(ROWS):
            px = slice(h * 128, (h + 1) * 128)
            r.xv[x, 0, block * 16 : (block + 1) * 16, px] = t[h * 16 : (h + 1) * 16]
    pooled = jnp.zeros((128, 128), F32)
    for h in range(ROWS):
        pooled = pooled + r.xv[x, 0, :, h * 128 : (h + 1) * 128].astype(F32)
    r.pooled[x] = jnp.broadcast_to(lane_sum(pooled) / PIXELS, (128, 128))
    prepare_weights(0)
    loads["wa"].wait()
    prepare_weights(ORDER[1])

    pl.semaphore_wait(barrier, len(partners))

    n_feat = new(2)
    n_foth = new()
    halves = [pl.ds(0, PIXELS // 2), pl.ds(PIXELS // 2, PIXELS // 2)]
    send_weights(0)
    for n in range(2):
        send(r.xv.at[x, 0, :, halves[n]], r.xsib.at[:, halves[n]], n_feat + n, sibling)
    g_og.start()
    send_weights(ORDER[1])
    send(r.xv.at[x, 0], r.xv.at[x, 0], n_foth, xdev)
    g_par.start()
    g_wp.start()
    arrived(r.xsib.at[:, halves[0]], n_feat, sibling)

    def features_at(px):
        return jnp.concatenate([r.xv[x, 0, :, px], r.xsib[:, px]], axis=0)

    def convolve(piece):
        b = piece[0]
        for q in range(piece[1] // BLOCK, (piece[1] + SPAN) // BLOCK):
            px = slice(q * BLOCK, (q + 1) * BLOCK)
            total = None
            for i, offset in branch_rows(b):
                source = q + offset * COLS // BLOCK
                if source < 0 or source >= PIXELS // BLOCK:
                    continue
                slot = SLOTS[(b, i)]
                count = 1 if b == 0 else 3
                weights = r.lw[slot : slot + count].reshape(count * 128, 256)
                part = dot(weights, features_at(slice(source * BLOCK, (source + 1) * BLOCK)))
                total = part if total is None else total + part
            if b:
                rate = atrous_rates[b - 1]
                total = (
                    total[128:256]
                    + shift_cols(total[0:128], rate)
                    + shift_cols(total[256:384], -rate)
                )
            r.acc[b, :, :, px] = total.reshape(GROUPS, 16, BLOCK)
        if carries_pool(piece):
            pooled = jnp.zeros((128, 128), F32)
            for h in range(ROWS):
                pooled = pooled + r.xsib[:, h * 128 : (h + 1) * 128].astype(F32)
            column = jnp.concatenate([r.pooled[x][:, 0:1], lane_sum(pooled) / PIXELS], axis=0)
            terms = split_lanes(column).astype(BF16)
            slot = SLOTS["pool"]
            sums = lane_sum(dot(r.lw[slot].reshape(128, 256), terms))
            r.acp[...] = jnp.broadcast_to(sums, (128, 128)).reshape(GROUPS, 16, 128)

    n_ry = {piece: new() for piece in PIECES}
    n_rz = {piece: new(3) for piece in PIECES}

    def reduce_y_send(piece):
        b, w = piece[0], lanes_of(piece)
        px = pl.ds(piece[1], SPAN)
        r.ys[b, :, :, px] = r.acc[b, pl.ds(4 * (1 - y), 4), :, px].astype(BF16)
        if carries_pool(piece):
            r.ys[b, :, :, PIXELS:WIDE] = encode_pair(r.acp[pl.ds(4 * (1 - y), 4)])
        send(r.ys.at[b, :, :, w], r.yr.at[b, :, :, w], n_ry[piece], ydev)

    def reduce_z_send(piece):
        b, w = piece[0], lanes_of(piece)
        px = pl.ds(piece[1], SPAN)
        arrived(r.yr.at[b, :, :, w], n_ry[piece], ydev)
        for i in (2, 1, 3, 0):
            zz = z if i == 0 else zpos[i]
            g = 4 * y + zz
            s = r.acc[b, g, :, px] + r.yr[b, zz, :, px].astype(F32)
            if carries_pool(piece):
                e = r.acp[g] + decode_pair(r.yr[b, zz, :, PIXELS:WIDE])
            if i == 0:
                r.acc[b, g, :, px] = s
                if carries_pool(piece):
                    r.acp[g] = e
            else:
                r.zs[b, i, :, px] = s.astype(BF16)
                if carries_pool(piece):
                    r.zs[b, i, :, PIXELS:WIDE] = encode_pair(e)
                send(r.zs.at[b, i, :, w], r.zr.at[b, i, :, w], n_rz[piece] + i - 1, zdev[i])

    def reduce_finish(piece):
        b, w = piece[0], lanes_of(piece)
        px = pl.ds(piece[1], SPAN)
        g = pre_group(y, z)
        total = r.acc[b, g, :, px]
        extra = r.acp[g] if carries_pool(piece) else None
        for i in (1, 2, 3):
            arrived(r.zr.at[b, i, :, w], n_rz[piece] + i - 1, zdev[i])
            total = total + r.zr[b, i, :, px].astype(F32)
            if carries_pool(piece):
                extra = extra + decode_pair(r.zr[b, i, :, PIXELS:WIDE])
        r.g[b, x, g, :, px] = total.astype(BF16)
        if carries_pool(piece):
            r.g[b, x, g, :, PIXELS:WIDE] = encode_pair(extra)
        g_pre[piece].start()
        if piece in CROSS_FIRST:
            ref = sums_slot(piece, x)(g)
            send(ref, ref, n_cross[piece], xdev)

    def cross(piece):
        arrived(sums_slot(piece, 1 - x)(pre_group(y, z)), n_cross[piece], xdev)
        g_other[piece].start()

    shift_pairs = []
    lane_r = iota((128, 128), 0)
    lane_c = iota((128, 128), 1)
    for rate in atrous_rates:
        left = jnp.where(lane_r == lane_c - rate, 1.0, 0.0).astype(BF16)
        right = jnp.where(lane_r == lane_c + rate, 1.0, 0.0).astype(BF16)
        shift_pairs.append(jnp.concatenate([left, right], axis=1))

    local = []

    def keep(src, dst):
        copy = pltpu.make_async_copy(src, dst, r.ls.at[len(local)])
        copy.start()
        local.append(copy)

    def place_shifted(image):
        for h in range(ROWS):
            px = slice(h * 128, (h + 1) * 128)
            for a in range(3):
                both = dot(r.xv[image, 0, :, px], shift_pairs[a]).astype(BF16)
                r.xv[image, 1 + 2 * a, :, px] = both[:, 0:128]
                r.xv[image, 2 + 2 * a, :, px] = both[:, 128:256]

    count = float(2 * PIXELS)

    def each_group_loop(body):
        def step(g, _):
            body(g, pl.ds(pl.multiple_of(g * 16, 16), 16))
            return 0

        lax.fori_loop(0, GROUPS, step, 0)

    def each_group(body):
        for g in range(GROUPS):
            body(g, pl.ds(g * 16, 16))

    tiles = [(image, slice(h * 128, (h + 1) * 128)) for image in range(2) for h in range(ROWS)]
    zero_tile = jnp.zeros((16, 128), F32)

    def spread_lanes(column):
        return jnp.broadcast_to(column, (128, 128))

    def norm_params(b):
        mean = lane_sum(r.s1[b]) / count
        inv = lax.rsqrt(lane_sum(r.s2[b]) / count - mean * mean + norm_eps)
        par = r.pt[...].reshape(128, 128)
        scale = par[:, b : b + 1] * inv
        r.pa[b] = spread_lanes(scale)
        r.pb[b] = spread_lanes(par[:, 8 + b : 9 + b] - mean * scale)
        r.pm[b] = spread_lanes(mean)
        r.pi[b] = spread_lanes(inv)

    def grad_params(b):
        s1 = lane_sum(r.s1[b])
        inv, mean = r.pi[b][:, 0:1], r.pm[b][:, 0:1]
        s2 = (lane_sum(r.s2[b]) - mean * s1) * inv
        scale = r.pa[b][:, 0:1]
        c2 = -scale * inv * s2 / count
        r.s1[b] = spread_lanes(s1)
        r.s2[b] = spread_lanes(s2)
        r.c2[b] = spread_lanes(c2)
        r.c1[b] = spread_lanes(-scale * s1 / count - mean * c2)

    def act_and_slope(zed):
        u = 0.5 * jnp.tanh(0.5 * zed)
        sg = 0.5 + u
        act = zed * sg
        return act, sg + act * (0.5 - u)

    def branch_norm(b, each_group):
        def sums(g, rows):
            s, q = zero_tile, zero_tile
            for image, px in tiles:
                v = r.g[b, image, g, :, px].astype(F32)
                s = s + v
                q = q + v * v
            r.s1[b, rows] = s
            r.s2[b, rows] = q

        each_group(sums)
        norm_params(b)

        def apply(g, rows):
            scale, base = r.pa[b, rows], r.pb[b, rows]
            for image, px in tiles:
                act, slope = act_and_slope(r.g[b, image, g, :, px].astype(F32) * scale + base)
                r.act[image, b, g, :, px] = act.astype(BF16)
                r.sl[image, b, g, :, px] = slope.astype(BF16)

        each_group(apply)

    lane128 = iota((128, 128), 1)
    n_pool = new()

    def pool_part():
        pool_cols = jnp.zeros((128, 128), F32)
        for image in range(2):
            pre = decode_pair(r.g[0, image, :, :, PIXELS:WIDE]).reshape(128, 128)
            r.ppool[image] = pre
            pool_cols = pool_cols + jnp.where(lane128 == image, pre * sigmoid(pre), 0.0)
        pool_cols = pool_cols.astype(BF16)
        pool_out = dot(r.wpt[:, 512:640], pool_cols)
        r.poolo[...] = pool_out[0:128]

        r.pools[...] = pool_out[128:256]
        send(r.pools, r.poolr, n_pool, sibling)

    def finish_branch(b, groups):
        for piece in PIECES:
            if piece[0] != b:
                continue
            if piece in CROSS_FIRST:
                g_pre[piece].forward_y()
                g_other[piece].forward_y()
            else:
                g_pre[piece].finish(sums_slot(piece, 1 - x))
        branch_norm(b, groups)

    def projection_weights():
        for b in range(5):
            flat = dot_nt(eye, r.wp[:, b].reshape(128, 256)).astype(BF16)
            r.wps[...] = flat.reshape(GROUPS, 2, 16, 128)
            r.wpt[0:128, b * 128 : (b + 1) * 128] = r.wps[:, k].reshape(128, 128)
            r.wpt[128:256, b * 128 : (b + 1) * 128] = r.wps[:, 1 - k].reshape(128, 128)

    steps = len(PIECES)
    for s in range(steps + 5):
        if s < steps:
            b = PIECES[s][0]
            if s % HALVES == 0:
                wait_weights(b)
            convolve(PIECES[s])
            if s == 0:
                arrived(r.xsib.at[:, halves[1]], n_feat + 1, sibling)
            reduce_y_send(PIECES[s])
            if s % HALVES == 0 and s // HALVES + 2 < len(ORDER):
                prepare_weights(ORDER[s // HALVES + 2])
                send_weights(ORDER[s // HALVES + 2])
        if 0 <= s - 1 < steps:
            reduce_z_send(PIECES[s - 1])
        if s == 2:
            g_par.forward_z()
            g_wp.forward_z()
            g_og.forward_z()
        if 0 <= s - 2 < steps:
            reduce_finish(PIECES[s - 2])
        if s == 3:
            g_par.forward_y()
            g_wp.forward_y()
            g_og.forward_y()
        if s == 8:
            projection_weights()
        if 0 <= s - 3 < steps:
            g_pre[PIECES[s - 3]].forward_z()
            if PIECES[s - 3] in CROSS_FIRST:
                cross(PIECES[s - 3])
        if 0 <= s - 5 < steps:
            if PIECES[s - 5] in CROSS_FIRST:
                g_other[PIECES[s - 5]].forward_z()
            else:
                g_pre[PIECES[s - 5]].forward_y()
        if s == 6:
            place_shifted(x)
        if s == 7:
            arrived(r.xv.at[1 - x, 0], n_foth, xdev)
            place_shifted(1 - x)
            pooled = jnp.zeros((128, 128), F32)
            for h in range(ROWS):
                pooled = pooled + r.xv[1 - x, 0, :, h * 128 : (h + 1) * 128].astype(F32)
            r.pooled[1 - x] = spread_lanes(lane_sum(pooled) / PIXELS)
        if s == 11:
            finish_branch(ORDER[0], each_group_loop)
            pool_part()
        if s == 12:
            finish_branch(ORDER[1], each_group_loop)

    for b in ORDER[2:]:
        finish_branch(b, each_group)

    n_pp = new(2)
    for image in range(2):
        for q in range(PIXELS // BLOCK):
            px = slice(q * BLOCK, (q + 1) * BLOCK)
            part = dot(r.wpt[:, 0:512], r.act[image, :, :, :, px].reshape(512, BLOCK))
            r.acc[image, :, :, px] = part[0:128].reshape(GROUPS, 16, BLOCK)
            r.pps[image, :, :, px] = part[128:256].astype(BF16).reshape(GROUPS, 16, BLOCK)
        send(r.pps.at[image], r.pr.at[image], n_pp + image, sibling)

    for image in range(2):
        for b in range(4):
            r.ao[image, b] = r.act[image, b, mine]

    g_og.finish(lambda g: r.ogs.at[1 - x, g])
    for image in range(2):
        arrived(r.pr.at[image], n_pp + image, sibling)

    arrived(r.poolr, n_pool, sibling)
    for image in range(2):
        r.pcol[image] = spread_lanes((r.poolo[...] + r.poolr[...])[:, image : image + 1])

    def proj_sums(g, rows):
        s, q = zero_tile, zero_tile
        for image, px in tiles:
            v = r.acc[image, g, :, px] + r.pr[image, g, :, px].astype(F32)
            v = v + r.pcol[image, rows]
            r.acc[image, g, :, px] = v
            s = s + v
            q = q + v * v
        r.s1[4, rows] = s
        r.s2[4, rows] = q

    each_group(proj_sums)
    norm_params(4)

    def proj_slope(g, rows):
        scale, base = r.pa[4, rows], r.pb[4, rows]
        s1, s2 = zero_tile, zero_tile
        for image, px in tiles:
            v = r.acc[image, g, :, px]
            _, slope = act_and_slope(v * scale + base)
            dz = r.ogs[image, g, :, px].astype(F32) * slope
            r.dzp[image, g, :, px] = dz
            s1 = s1 + dz
            s2 = s2 + dz * v
        r.s1[4, rows] = s1
        r.s2[4, rows] = s2

    each_group(proj_slope)
    grad_params(4)
    n_dp = new(2)
    for image in range(2):

        def proj_low(g, rows, image=image):
            scale, c1, c2 = r.pa[4, rows], r.c1[4, rows], r.c2[4, rows]
            total = zero_tile
            for h in range(ROWS):
                px = slice(h * 128, (h + 1) * 128)
                low = scale * r.dzp[image, g, :, px] + (r.acc[image, g, :, px] * c2 + c1)
                low = low.astype(BF16)
                r.dp[image, g, k, :, px] = low
                total = total + low.astype(F32)
            r.s1[image, rows] = total

        each_group(proj_low)
        ref = r.dp.at[image, :, k]
        send(ref, ref, n_dp + image, sibling)

    n_rsum = new()
    row_sums = jnp.where(lane128 == 0, lane_sum(r.s1[0]), 0.0)
    row_sums = row_sums + jnp.where(lane128 == 1, lane_sum(r.s1[1]), 0.0)
    r.rsum[:, k] = row_sums.reshape(GROUPS, 16, 128)
    ref = r.rsum.at[:, k]
    send(ref, ref, n_rsum, sibling)

    my_rows = pl.ds(pl.multiple_of(mine * 16, 16), 16)
    scale, base = r.pa[4, my_rows], r.pb[4, my_rows]
    for h in range(ROWS):
        zed = r.acc[x, mine, :, h * 128 : (h + 1) * 128] * scale + base
        r.outv[pl.ds(h, 16, stride=16), :] = zed * sigmoid(zed)
    keep(r.outv, r.out)

    for image in range(2):
        arrived(r.dp.at[image, :, 1 - k], n_dp + image, sibling)
    arrived(r.rsum.at[:, 1 - k], n_rsum, sibling)

    n_d = {b: new(2) for b in ORDER}

    def back_block(b, turn, image, q):
        px = slice(q * 512, (q + 1) * 512)
        dblock = r.dp[image, :, :, :, px].reshape(256, 512)
        back = dot(r.wp[:, b].reshape(128, 256), dblock)
        r.acc[2 * turn + image, :, :, px] = back.reshape(GROUPS, 16, 512)

    back_order = (1, 2, 3, 0)

    dwp = [jnp.zeros((64, 256), F32)]

    def proj_weights(image, q):
        px = slice(q * 512, (q + 1) * 512)
        acts = r.ao[image, :, :, px].reshape(64, 512)
        dwp[0] = dwp[0] + dot_nt(acts, r.dp[image, :, :, :, px].reshape(256, 512))

    def branch_slope(b, turn):
        for image in range(2):
            for q in range(PIXELS // 512):
                back_block(b, turn, image, q)

        def slope(g, rows):
            s1, s2 = zero_tile, zero_tile
            for image, px in tiles:
                dz = r.acc[2 * turn + image, g, :, px] * r.sl[image, b, g, :, px].astype(F32)
                r.acc[2 * turn + image, g, :, px] = dz
                s1 = s1 + dz
                s2 = s2 + dz * r.g[b, image, g, :, px].astype(F32)
            r.s1[b, rows] = s1
            r.s2[b, rows] = s2
            if b == back_order[0]:
                proj_weights(g // 4, g % 4)

        each_group(slope)

    def branch_low(b, turn):
        grad_params(b)
        for image in range(2):

            def lower(g, rows, image=image):
                scale, c1, c2 = r.pa[b, rows], r.c1[b, rows], r.c2[b, rows]
                for h in range(ROWS):
                    px = slice(h * 128, (h + 1) * 128)
                    v = r.g[b, image, g, :, px].astype(F32)
                    low = scale * r.acc[2 * turn + image, g, :, px] + (v * c2 + c1)
                    r.d[b, image, g, k, :, px] = low.astype(BF16)

            each_group(lower)
            there = r.d.at[b, image, :, k]
            send(there, there, n_d[b] + image, sibling)

    def wait_grads(*branches):
        for b in branches:
            for image in range(2):
                arrived(r.d.at[b, image, :, 1 - k], n_d[b] + image, sibling)

    def branch_grads(b, first_branch, last_branch):
        planes = (2 * b - 1, 0, 2 * b)
        for i, offset in branch_rows(b):
            first, last = max(0, -offset), min(ROWS, ROWS - offset)
            there = slice((first + offset) * 128, (last + offset) * 128)
            here = slice(first * 128, last * 128)
            total = None
            for image in range(2):
                if b == 0:
                    rows = r.xv[image, 0]
                else:
                    rows = jnp.concatenate([r.xv[image, p, :, there] for p in planes], axis=0)
                part = dot_nt(rows, r.d[b, image, :, :, :, here].reshape(256, -1))
                total = part if total is None else total + part
            total = total.astype(BF16)
            if b == 0:
                slot = pl.ds(27, 1)
                r.dwv[27] = total
            else:
                slot = pl.ds((b - 1) * 9 + 3 * i, 3)
                r.dwv[slot] = total.reshape(3, 128, 256)
            keep(r.dwv.at[slot], r.dwb.at[slot])
        for q in range(PIXELS // BLOCK):
            px = slice(q * BLOCK, (q + 1) * BLOCK)
            total = None
            for i, offset in branch_rows(b):
                source = q - offset * COLS // BLOCK
                if source < 0 or source >= PIXELS // BLOCK:
                    continue
                if b == 0:
                    weights = r.w1[...]
                else:
                    weights = r.wa[pl.ds((b - 1) * 9 + 3 * i, 3)].reshape(384, 256)
                dblock = r.d[b, x, :, :, :, source * BLOCK : (source + 1) * BLOCK]
                part = dot(weights, dblock.reshape(256, BLOCK))
                total = part if total is None else total + part
            if b:
                rate = atrous_rates[b - 1]
                total = (
                    total[128:256]
                    + shift_cols(total[0:128], -rate)
                    + shift_cols(total[256:384], rate)
                )
            if not first_branch:
                total = total + r.fga[:, px]
            if last_branch:
                r.fgv[:, px] = (total + fg_pool).astype(BF16)
            else:
                r.fga[:, px] = total

    wp4 = r.wp[:, 4].reshape(128, 256)
    dpo = jnp.zeros((128, 128), F32)
    dwp4 = jnp.zeros((16, 256), F32)
    lane16 = iota((16, 128), 1)
    for image in range(2):
        terms = split_lanes(r.rsum[...].reshape(256, 128)[:, image : image + 1]).astype(BF16)
        pool_grad = lane_sum(dot(wp4, terms))
        pre = r.ppool[image][:, 0:1]
        _, slope = act_and_slope(pre)
        low = (pool_grad * slope).astype(BF16).astype(F32)
        for lane in (image, image + 2, image + 4):
            dpo = dpo + jnp.where(lane128 == lane, low, 0.0)
        mine_act, _ = act_and_slope(r.ppool[image, my_rows][:, 0:1])
        mine_act = mine_act.astype(BF16).astype(F32)
        dwp4 = dwp4 + mine_act * dot_nt(jnp.ones((16, 128), BF16), terms)
    r.dwprojv[4] = dwp4
    r.dpo[:, k] = dpo.astype(BF16).reshape(GROUPS, 16, 128)
    n_dpo = new()
    branch_slope(back_order[0], 0)
    for n, b in enumerate(back_order):
        if n + 1 < len(back_order):
            branch_slope(back_order[n + 1], (n + 1) % 2)
        branch_low(b, n % 2)
        if n == 0:
            ref = r.dpo.at[:, k]
            send(ref, ref, n_dpo, sibling)
            r.dwprojv[0:4] = dwp[0].reshape(4, 16, 256)
            keep(r.dwprojv, r.dwproj)
    wait_grads(back_order[0])
    branch_grads(back_order[0], True, False)
    wait_grads(*back_order[1:])
    branch_grads(back_order[1], False, False)

    tile = jnp.zeros((16, 128), F32)
    for b in range(5):
        tile = tile + jnp.where(lane16 == b, r.s2[b, my_rows], 0.0)
        tile = tile + jnp.where(lane16 == 8 + b, r.s1[b, my_rows], 0.0)
    r.flip[0:16, :] = tile
    flipped = r.flip[...].T
    r.dgainsv[...] = flipped[0:5, 0:16]
    r.dbiasesv[...] = flipped[8:13, 0:16]
    keep(r.dgainsv, r.dgains)
    keep(r.dbiasesv, r.dbiases)

    branch_grads(back_order[2], False, False)

    arrived(r.dpo.at[:, 1 - k], n_dpo, sibling)
    dpo = r.dpo[...].reshape(256, 128)
    pooled = jnp.zeros((128, 128), F32)
    for image in range(2):
        pooled = pooled + split_lanes(r.pooled[image][:, 0:1], (image, image + 2, image + 4))
    r.dwpoolv[...] = dot_nt(pooled.astype(BF16), dpo)
    keep(r.dwpoolv, r.dwpool)
    spread = dot(r.wpool[...], dpo)
    fg_pool = lane_sum(jnp.where(lane128 == x, spread, 0.0)) / PIXELS

    branch_grads(back_order[3], False, True)
    keep(r.fgv, r.fgb)
    for copy in sent:
        copy.wait_send()
    for copy in local:
        copy.wait()


COPY_INPUTS = ("out", "dwpool", "dwproj", "dgains", "dbiases", "fgb", "dwb")
COPY_OUTPUTS = ("out_o", "dwpool_o", "dwproj_o", "dgains_o", "dbiases_o", "fg", "dw1", "dwa")
COPY_SCRATCH = {
    "outv": pltpu.VMEM((256, 128), F32),
    "dwpoolv": pltpu.VMEM((128, 256), F32),
    "dwprojv": pltpu.VMEM((5, 16, 256), F32),
    "fgbv": pltpu.VMEM((128, PIXELS), BF16),
    "dwbv": pltpu.VMEM((28, 128, 256), BF16),
    "fgv": pltpu.VMEM((2048, 128), F32),
    "dwv": pltpu.VMEM((28, 128, 256), F32),
    "si": pltpu.SemaphoreType.DMA((16,)),
    "so": pltpu.SemaphoreType.DMA((16,)),
}


def copy_kernel(*refs):
    r = Refs()
    names = COPY_INPUTS + COPY_OUTPUTS + tuple(COPY_SCRATCH)
    for name, ref in zip(names, refs, strict=True):
        setattr(r, name, ref)
    loads = []
    stores = []

    def load(src, dst):
        copy = pltpu.make_async_copy(src, dst, r.si.at[len(loads)])
        copy.start()
        loads.append(copy)
        return copy

    def store(src, dst):
        copy = pltpu.make_async_copy(src, dst, r.so.at[len(stores)])
        copy.start()
        stores.append(copy)

    met = [
        (b - 1) * 9 + 3 * i for b in (1, 2, 3) for i in range(3) if i in dict(branch_rows(b))
    ]
    taps = [(n, load(r.dwb.at[pl.ds(n, 3)], r.dwbv.at[pl.ds(n, 3)])) for n in met]
    one = load(r.dwb.at[pl.ds(27, 1)], r.dwbv.at[pl.ds(27, 1)])
    fg = load(r.fgb, r.fgbv)
    passed = [
        (load(getattr(r, name), getattr(r, name + "v")), name)
        for name in ("out", "dwpool", "dwproj")
    ]
    r.dgains_o[...] = r.dgains[...]
    r.dbiases_o[...] = r.dbiases[...]
    for n in range(0, 27, 3):
        if n not in met:
            r.dwv[n : n + 3] = jnp.zeros((3, 128, 256), F32)
            store(r.dwv.at[pl.ds(n, 3)], r.dwa.at[pl.ds(n, 3)])
    for n, copy in taps:
        copy.wait()
        r.dwv[n : n + 3] = r.dwbv[n : n + 3].astype(F32)
        store(r.dwv.at[pl.ds(n, 3)], r.dwa.at[pl.ds(n, 3)])
    one.wait()
    r.dwv[27] = r.dwbv[27].astype(F32)
    store(r.dwv.at[27], r.dw1)
    fg.wait()
    for h in range(ROWS):
        r.fgv[pl.ds(h, 128, stride=16), :] = r.fgbv[:, h * 128 : (h + 1) * 128].astype(F32)
    store(r.fgv, r.fg)
    for copy, name in passed:
        copy.wait()
        store(getattr(r, name + "v"), getattr(r, name + "_o"))
    for copy in stores:
        copy.wait()


def fused(features, w_one, w_atrous, w_pool, w_proj, gains, biases, out_grad):
    vmem = pl.BlockSpec(memory_space=pltpu.VMEM)
    hbm = pl.BlockSpec(memory_space=pl.ANY)
    passed = [(256, 128), (128, 256), (5, 16, 256), (5, 16), (5, 16)]
    shapes = [jax.ShapeDtypeStruct(s, F32) for s in passed]
    shapes.append(jax.ShapeDtypeStruct((128, PIXELS), BF16))
    shapes.append(jax.ShapeDtypeStruct((28, 128, 256), BF16))
    parts = pl.pallas_call(
        head_kernel,
        out_shape=shapes,
        in_specs=[hbm] * len(INPUTS),
        out_specs=[hbm] * len(OUTPUTS),
        scratch_shapes=list(scratch_table(NSEMS).values()),
        compiler_params=pltpu.CompilerParams(
            collective_id=0, has_side_effects=True, vmem_limit_bytes=64 * 2**20
        ),
    )(
        features.reshape(2048, 128),
        out_grad.reshape(256, 128),
        w_one,
        w_atrous.reshape(27, 128, 256),
        w_pool,
        w_proj,
        gains,
        biases,
    )
    result = passed + [(2048, 128), (128, 256), (27, 128, 256)]
    out, dwpool, dwproj, dgains, dbiases, fg, dw1, dwa = pl.pallas_call(
        copy_kernel,
        out_shape=[jax.ShapeDtypeStruct(s, F32) for s in result],
        in_specs=[hbm] * 3 + [vmem] * 2 + [hbm] * 2,
        out_specs=[hbm] * 3 + [vmem] * 2 + [hbm] * 3,
        scratch_shapes=list(COPY_SCRATCH.values()),
        compiler_params=pltpu.CompilerParams(vmem_limit_bytes=64 * 2**20),
    )(*parts)
    return (
        out.reshape(1, 16, ROWS, COLS),
        fg.reshape(1, 128, ROWS, COLS),
        dw1,
        dwa.reshape(3, 9, 128, 256),
        dwpool,
        dwproj,
        dgains,
        dbiases,
    )


def solution(mesh):
    placed = (
        P("dp", "chan", None, None),
        P("chan", None),
        P(None, None, "chan", None),
        P("chan", None),
        P(None, "chan", None),
        P(None, "chan"),
        P(None, "chan"),
        P("dp", "chan", None, None),
    )
    small = mesh.shape["dp"] == 2 and mesh.shape["chan"] == 16
    return jax.shard_map(
        fused if small else local,
        mesh=mesh,
        in_specs=placed,
        out_specs=(
            P("dp", "chan", None, None),
            P("dp", "chan", None, None),
            P("chan", None),
            P(None, None, "chan", None),
            P("chan", None),
            P(None, "chan", None),
            P(None, "chan"),
            P(None, "chan"),
        ),
        check_vma=False,
    )
```

```python
import functools

import jax
import jax.numpy as jnp
from jax import lax
from jax.experimental import pallas as pl
from jax.experimental.pallas import tpu as pltpu
from jax.sharding import PartitionSpec as P

atrous_rates = (6, 12, 18)
norm_eps = 1e-05


def shifted(values, vertical, horizontal):
    margin = max(abs(vertical), abs(horizontal))
    if margin == 0:
        return values
    height = values.shape[-2]
    breadth = values.shape[-1]
    spacing = [(0, 0)] * (values.ndim - 2) + [(margin, margin), (margin, margin)]
    padded = jnp.pad(values, spacing)
    return padded[
        ...,
        margin + vertical : margin + vertical + height,
        margin + horizontal : margin + horizontal + breadth,
    ]


def tap_offsets(dilation):
    return [
        ((along_rows - 1) * dilation, (along_cols - 1) * dilation)
        for along_rows in range(3)
        for along_cols in range(3)
    ]


def make_patches(features, dilation):
    return jnp.stack(
        [shifted(features, vertical, horizontal) for vertical, horizontal in tap_offsets(dilation)]
    )


def silu_slope(values):
    sigmoid = jax.nn.sigmoid(values)
    return sigmoid * (1.0 + values * (1.0 - sigmoid))


def expand_tail(values, extra):
    return values.reshape(values.shape + (1,) * extra)


def local(features, w_one, w_atrous, w_pool, w_proj, gains, biases, out_grad):
    highest = lax.Precision.HIGHEST
    images, local_in, height, columns = features.shape
    pixels = height * columns
    population = images * pixels * lax.axis_size("dp")
    patches = jnp.stack([make_patches(features, dilation) for dilation in atrous_rates])
    pooled = jnp.sum(features, axis=(2, 3), dtype=jnp.float32) / pixels
    one_term = jnp.einsum("nchw,co->onhw", features, w_one, preferred_element_type=jnp.float32)
    rate_terms = jnp.einsum(
        "rtnchw,rtco->ronhw", patches, w_atrous, preferred_element_type=jnp.float32
    )
    spatial_term = jnp.concatenate([one_term[None], rate_terms])
    pool_term = jnp.dot(pooled, w_pool.astype(jnp.float32), precision=highest).T[None]
    branch_pre, pool_pre = (
        lax.psum_scatter(spatial_term, "chan", scatter_dimension=1, tiled=True),
        lax.psum_scatter(pool_term, "chan", scatter_dimension=1, tiled=True),
    )
    branch_totals, branch_squares = lax.psum(
        (jnp.sum(branch_pre, axis=(2, 3, 4)), jnp.sum(branch_pre * branch_pre, axis=(2, 3, 4))),
        "dp",
    )
    branch_mean = branch_totals / population
    branch_inv = lax.rsqrt(branch_squares / population - branch_mean * branch_mean + norm_eps)
    centred = branch_pre - expand_tail(branch_mean, 3)
    branch_z = centred * expand_tail(gains[:4] * branch_inv, 3) + expand_tail(biases[:4], 3)
    branch_hat = centred * expand_tail(branch_inv, 3)
    act_low = jax.nn.silu(branch_z).astype(jnp.bfloat16)
    pool_act = jax.nn.silu(pool_pre).astype(jnp.bfloat16)
    window = w_proj
    spatial = jnp.einsum("bonhw,bod->dnhw", act_low, window[:4], preferred_element_type=jnp.float32)
    pool_part = jnp.einsum("bon,bod->dn", pool_act, window[4:], preferred_element_type=jnp.float32)
    proj_pre = lax.psum_scatter(
        spatial + pool_part[:, :, None, None], "chan", scatter_dimension=0, tiled=True
    )
    proj_totals, proj_squares = lax.psum(
        (jnp.sum(proj_pre, axis=(1, 2, 3)), jnp.sum(proj_pre * proj_pre, axis=(1, 2, 3))), "dp"
    )
    proj_mean = proj_totals / population
    proj_inv = lax.rsqrt(proj_squares / population - proj_mean * proj_mean + norm_eps)
    proj_centred = proj_pre - expand_tail(proj_mean, 3)
    proj_z = proj_centred * expand_tail(gains[4] * proj_inv, 3) + expand_tail(biases[4], 3)
    proj_hat = proj_centred * expand_tail(proj_inv, 3)
    output = jnp.transpose(jax.nn.silu(proj_z), (1, 0, 2, 3))
    grad_out = jnp.transpose(out_grad, (1, 0, 2, 3)).astype(jnp.float32)
    proj_dz = grad_out * silu_slope(proj_z)
    proj_dbias, proj_dgain = lax.psum(
        (jnp.sum(proj_dz, axis=(1, 2, 3)), jnp.sum(proj_dz * proj_hat, axis=(1, 2, 3))), "dp"
    )
    proj_dpre = expand_tail(gains[4] * proj_inv, 3) * (
        proj_dz
        - expand_tail(proj_dbias / population, 3)
        - proj_hat * expand_tail(proj_dgain / population, 3)
    )
    proj_low = proj_dpre.astype(jnp.bfloat16)
    pool_act_wide = pool_act.astype(jnp.float32)
    portion = lax.all_gather(proj_low, "chan", axis=0, tiled=True)
    window = w_proj
    act_grad = jnp.einsum(
        "bod,dnhw->bonhw", window[:4], portion, preferred_element_type=jnp.float32
    )
    portion_sum = jnp.sum(portion, axis=(2, 3), dtype=jnp.float32)
    pool_grad = jnp.einsum(
        "bod,dn->bon", window[4:].astype(jnp.float32), portion_sum, precision=highest
    )
    spatial_part = jnp.einsum(
        "bonhw,dnhw->bod", act_low, portion, preferred_element_type=jnp.float32
    )
    pool_part = jnp.einsum("bon,dn->bod", pool_act_wide, portion_sum, precision=highest)
    weight_grad = jnp.concatenate([spatial_part, pool_part])
    act_grad, pool_grad, proj_wgrad = (act_grad, pool_grad, weight_grad)
    branch_dz = act_grad * silu_slope(branch_z)
    branch_dbias, branch_dgain = lax.psum(
        (jnp.sum(branch_dz, axis=(2, 3, 4)), jnp.sum(branch_dz * branch_hat, axis=(2, 3, 4))), "dp"
    )
    branch_dpre = expand_tail(gains[:4] * branch_inv, 3) * (
        branch_dz
        - expand_tail(branch_dbias / population, 3)
        - branch_hat * expand_tail(branch_dgain / population, 3)
    )
    branch_low = branch_dpre.astype(jnp.bfloat16)
    pool_low = (pool_grad * silu_slope(pool_pre)).astype(jnp.bfloat16)
    spatial_portion = lax.all_gather(branch_low, "chan", axis=1, tiled=True)
    pool_portion = lax.all_gather(pool_low, "chan", axis=1, tiled=True)
    pool_cols = w_pool.astype(jnp.float32)
    feature_grad = jnp.einsum(
        "co,onhw->nchw", w_one, spatial_portion[0], preferred_element_type=jnp.float32
    )
    patch_grad = jnp.einsum(
        "rtco,ronhw->rtnchw", w_atrous, spatial_portion[1:], preferred_element_type=jnp.float32
    )
    pool_wide = pool_portion[0].astype(jnp.float32)
    pooled_grad = jnp.dot(pool_wide.T, pool_cols.T, precision=highest)
    one_piece = jnp.einsum(
        "nchw,onhw->co", features, spatial_portion[0], preferred_element_type=jnp.float32
    )
    rate_piece = jnp.einsum(
        "rtnchw,ronhw->rtco", patches, spatial_portion[1:], preferred_element_type=jnp.float32
    )
    pool_piece = jnp.dot(pooled.T, pool_wide.T, precision=highest)
    one_grad = one_piece
    rate_grad = rate_piece
    pool_wgrad = pool_piece
    feature_grad, patch_grad, pooled_grad, one_grad, rate_grad, pool_wgrad = (
        feature_grad,
        patch_grad,
        pooled_grad,
        one_grad,
        rate_grad,
        pool_wgrad,
    )
    for branch, dilation in enumerate(atrous_rates):
        for tap_index, (vertical, horizontal) in enumerate(tap_offsets(dilation)):
            feature_grad = feature_grad + shifted(
                patch_grad[branch, tap_index], -vertical, -horizontal
            )
    feature_grad = feature_grad + (pooled_grad / pixels)[:, :, None, None]
    one_grad, rate_grad, pool_wgrad, proj_wgrad = (
        lax.psum(one_grad.astype(jnp.bfloat16), "dp").astype(jnp.float32),
        lax.psum(rate_grad.astype(jnp.bfloat16), "dp").astype(jnp.float32),
        lax.psum(pool_wgrad.astype(jnp.bfloat16), "dp").astype(jnp.float32),
        lax.psum(proj_wgrad.astype(jnp.bfloat16), "dp").astype(jnp.float32),
    )
    gains_grad = jnp.concatenate([branch_dgain, proj_dgain[None]])
    biases_grad = jnp.concatenate([branch_dbias, proj_dbias[None]])
    return (
        output,
        feature_grad,
        one_grad,
        rate_grad,
        pool_wgrad,
        proj_wgrad,
        gains_grad,
        biases_grad,
    )


MESH = pl.DeviceIdType.MESH
F32 = jnp.float32
BF16 = jnp.bfloat16
ROWS = 16
COLS = 128
PIXELS = ROWS * COLS
WIDE = PIXELS + 128
CIN_PART = 128
COUT = 256
GROUPS = 8
BLOCK = 256
ORDER = (0, 3, 2, 1)


def branch_rows(branch):
    if branch == 0:
        return [(None, 0)]
    rate = atrous_rates[branch - 1]
    return [(i, (i - 1) * rate) for i in (1, 0, 2) if abs((i - 1) * rate) < ROWS]


def weight_slots():
    slots = {}
    count = 0
    spans = {}
    for branch in ORDER:
        begin = count
        for i, _ in branch_rows(branch):
            slots[(branch, i)] = count
            count += 1 if branch == 0 else 3
        if branch == 0:
            slots["pool"] = count
            count += 1
        spans[branch] = (begin, count)
    return slots, spans, count


SLOTS, SPANS, NSLOTS = weight_slots()


HALVES = 2
SPAN = PIXELS // HALVES
PIECES = [(b, half * SPAN) for b in ORDER for half in range(HALVES)]


CROSS_FIRST = PIECES[-2:]


def carries_pool(piece):
    return piece == (0, PIXELS - SPAN)


def lanes_of(piece):
    return pl.ds(piece[1], SPAN + (128 if carries_pool(piece) else 0))


def dot(a, b):
    return jnp.dot(a, b, preferred_element_type=F32)


def dot_nt(a, b):
    return lax.dot_general(a, b, (((1,), (1,)), ((), ())), preferred_element_type=F32)


def iota(shape, dim):
    return lax.broadcasted_iota(jnp.int32, shape, dim)


def lane_sum(v):
    return jnp.sum(v, axis=1, keepdims=True)


def split_lanes(column, lanes=(0, 1, 2)):
    high = column.astype(BF16).astype(F32)
    mid = (column - high).astype(BF16).astype(F32)
    low = column - high - mid
    lane = iota((column.shape[0], 128), 1)
    out = jnp.where(lane == lanes[0], high, 0.0)
    out = out + jnp.where(lane == lanes[1], mid, 0.0)
    return out + jnp.where(lane == lanes[2], low, 0.0)


def encode_pair(v):
    lane = iota(v.shape, v.ndim - 1)
    high = v.astype(BF16).astype(F32)
    low = v - high
    return jnp.where(lane == 0, high, jnp.where(lane == 1, low, 0.0)).astype(BF16)


def decode_pair(e):
    return jnp.broadcast_to(jnp.sum(e.astype(F32), axis=-1, keepdims=True), e.shape)


def shift_cols(v, by):
    if by == 0:
        return v
    lane = iota((v.shape[0], 128), 1)
    keep = (lane >= by) if by > 0 else (lane < 128 + by)
    parts = []
    for h in range(v.shape[1] // 128):
        tile = v[:, h * 128 : (h + 1) * 128]
        parts.append(jnp.where(keep, pltpu.roll(tile, by % 128, 1), 0.0))
    return jnp.concatenate(parts, axis=1) if len(parts) > 1 else parts[0]


def sigmoid(z):
    return 0.5 * jnp.tanh(0.5 * z) + 0.5


INPUTS = ("feat", "og", "w1", "wa", "wpool", "wproj", "gains", "biases")
OUTPUTS = ("out", "dwpool", "dwproj", "dgains", "dbiases", "fgb", "dwb")


def scratch_table(sems):
    vm = pltpu.VMEM
    return {
        "outv": vm((256, 128), F32),
        "dwpoolv": vm((128, 256), F32),
        "dwprojv": vm((5, 16, 256), F32),
        "dgainsv": vm((5, 16), F32),
        "dbiasesv": vm((5, 16), F32),
        "feat": vm((2048, 128), BF16),
        "og": vm((256, 128), BF16),
        "w1": vm((128, 256), BF16),
        "wa": vm((27, 128, 256), BF16),
        "wpool": vm((128, 256), BF16),
        "wproj": vm((5, 16, 256), BF16),
        "gains": vm((5, 16), F32),
        "biases": vm((5, 16), F32),
        "xsib": vm((128, PIXELS), BF16),
        "tw": vm((NSLOTS, GROUPS, 2, 16, 128), BF16),
        "lw": vm((NSLOTS, GROUPS, 16, 256), BF16),
        "acc": vm((4, GROUPS, 16, PIXELS), F32),
        "acp": vm((GROUPS, 16, 128), F32),
        "ys": vm((4, 4, 16, WIDE), BF16),
        "yr": vm((4, 4, 16, WIDE), BF16),
        "zs": vm((4, 4, 16, WIDE), BF16),
        "zr": vm((4, 4, 16, WIDE), BF16),
        "g": vm((4, 2, GROUPS, 16, WIDE), BF16),
        "ogs": vm((2, GROUPS, 16, PIXELS), BF16),
        "pt": vm((GROUPS, 16, 128), F32),
        "wp": vm((GROUPS, 5, 16, 256), BF16),
        "wpt": vm((256, 640), BF16),
        "wps": vm((GROUPS, 2, 16, 128), BF16),
        "pools": vm((128, 128), F32),
        "poolo": vm((128, 128), F32),
        "poolr": vm((128, 128), F32),
        "pcol": vm((2, 128, 128), F32),
        "pps": vm((2, GROUPS, 16, PIXELS), BF16),
        "xv": vm((2, 7, 128, PIXELS), BF16),
        "sl": vm((2, 4, GROUPS, 16, PIXELS), BF16),
        "flip": vm((128, 128), F32),
        "c1": vm((5, 128, 128), F32),
        "c2": vm((5, 128, 128), F32),
        "act": vm((2, 4, GROUPS, 16, PIXELS), BF16),
        "ao": vm((2, 4, 16, PIXELS), BF16),
        "pa": vm((5, 128, 128), F32),
        "pb": vm((5, 128, 128), F32),
        "pm": vm((5, 128, 128), F32),
        "pi": vm((5, 128, 128), F32),
        "s1": vm((5, 128, 128), F32),
        "s2": vm((5, 128, 128), F32),
        "pr": vm((2, GROUPS, 16, PIXELS), BF16),
        "dzp": vm((2, GROUPS, 16, PIXELS), F32),
        "dp": vm((2, GROUPS, 2, 16, PIXELS), BF16),
        "dpo": vm((GROUPS, 2, 16, 128), BF16),
        "d": vm((4, 2, GROUPS, 2, 16, PIXELS), BF16),
        "dwv": vm((28, 128, 256), BF16),
        "rsum": vm((GROUPS, 2, 16, 128), F32),
        "fga": vm((128, PIXELS), F32),
        "fgv": vm((128, PIXELS), BF16),
        "pooled": vm((2, 128, 128), F32),
        "ppool": vm((2, 128, 128), F32),
        "ss": pltpu.SemaphoreType.DMA((sems,)),
        "rs": pltpu.SemaphoreType.DMA((sems,)),
        "ls": pltpu.SemaphoreType.DMA((32,)),
        "li": pltpu.SemaphoreType.DMA((8,)),
    }


class Refs:
    pass


NSEMS = 224


def head_kernel(*refs):
    names = tuple(n + "_hbm" for n in INPUTS) + OUTPUTS + tuple(scratch_table(NSEMS))
    r = Refs()
    for name, ref in zip(names, refs, strict=True):
        setattr(r, name, ref)
    x = lax.axis_index("dp")
    c = lax.axis_index("chan")
    k = lax.rem(c, 2)
    y = lax.rem(lax.div(c, 2), 2)
    z = lax.div(c, 4)

    def dev(xx, zz, yy, kk):
        return {"dp": xx, "chan": (zz * 2 + yy) * 2 + kk}

    sibling = dev(x, z, y, 1 - k)
    xdev = dev(1 - x, z, y, k)
    ydev = dev(x, z, 1 - y, k)
    zpos = [None] + [lax.rem(z + i, 4) for i in (1, 2, 3)]
    zfrom = [None] + [lax.rem(z + 4 - i, 4) for i in (1, 2, 3)]
    zdev = [None] + [dev(x, zpos[i], y, k) for i in (1, 2, 3)]

    counter = [0]
    sent = []
    due = {}

    def new(n=1):
        first = counter[0]
        counter[0] += n
        assert counter[0] <= NSEMS
        return first

    def rcopy(src, dst, n, device):
        return pltpu.make_async_remote_copy(
            src_ref=src,
            dst_ref=dst,
            send_sem=r.ss.at[n],
            recv_sem=r.rs.at[n],
            device_id=device,
            device_id_type=MESH,
        )

    def send(src, dst, n, device, group=None):
        copy = rcopy(src, dst, n, device)
        copy.start()
        (sent if group is None else group).append(copy)
        due[n] = (dst, device)

    def arrived(ref, n, device):
        del due[n]
        rcopy(ref, ref, n, device).wait_recv()

    barrier = pltpu.get_barrier_semaphore()
    partners = [sibling, xdev, ydev] + zdev[1:]
    for partner in partners:
        pl.semaphore_signal(barrier, inc=1, device_id=partner, device_id_type=MESH)

    loads = {}
    for n, name in enumerate(("feat", "w1", "wpool", "og", "gains", "biases", "wproj", "wa")):
        loads[name] = pltpu.make_async_copy(getattr(r, name + "_hbm"), getattr(r, name), r.li.at[n])
        loads[name].start()

    rr = iota((256, 256), 0)
    cc = iota((256, 256), 1)
    perm = jnp.where(cc == lax.rem(rr, 16) * 16 + lax.div(rr, 16), 1.0, 0.0).astype(BF16)
    eye = jnp.where(rr == cc, 1.0, 0.0).astype(BF16)

    def permuted(ref, block):
        return dot(perm, ref[block * 256 : (block + 1) * 256, :]).astype(BF16)

    def pre_group(yy, zz):
        return yy * 4 + zz

    def own_group(yy, zz):
        return zz * 2 + yy

    class Gather:
        def __init__(self, slot, group, across):
            self.slot, self.group, self.across = slot, group, across
            self.nz, self.ny, self.nx = new(3), new(4), new(8) if across else None

        def start(self):
            mine = self.slot(self.group(y, z))
            for i in (2, 1, 3):
                send(mine, mine, self.nz + i - 1, zdev[i])
            send(mine, mine, self.ny, ydev)
            if self.across:
                send(mine, mine, self.nx, xdev)

        def forward_z(self):
            for i in (1, 2, 3):
                ref = self.slot(self.group(y, zfrom[i]))
                arrived(ref, self.nz + i - 1, zdev[i])
                send(ref, ref, self.ny + i, ydev)
                if self.across:
                    send(ref, ref, self.nx + i, xdev)

        def forward_y(self):
            for i in range(4):
                ref = self.slot(self.group(1 - y, z if i == 0 else zfrom[i]))
                arrived(ref, self.ny + i, ydev)
                if self.across:
                    send(ref, ref, self.nx + 4 + i, xdev)

        def finish(self, other):
            if self.across:
                for i in range(8):
                    yy = y if i < 4 else 1 - y
                    zz = z if i % 4 == 0 else zfrom[i % 4]
                    arrived(other(self.group(yy, zz)), self.nx + i, xdev)

    g_og = Gather(lambda g: r.ogs.at[x, g], own_group, True)
    g_par = Gather(lambda g: r.pt.at[g], own_group, False)
    g_wp = Gather(lambda g: r.wp.at[g], own_group, False)
    def sums_slot(piece, image):
        return lambda g: r.g.at[piece[0], image, g, :, lanes_of(piece)]

    g_pre = {}
    g_other = {}
    n_cross = {}
    for piece in PIECES:
        g_pre[piece] = Gather(sums_slot(piece, x), pre_group, piece not in CROSS_FIRST)
        if piece in CROSS_FIRST:
            g_other[piece] = Gather(sums_slot(piece, 1 - x), pre_group, False)
            n_cross[piece] = new()

    mine = own_group(y, z)
    loads["og"].wait()
    og = permuted(r.og, 0)
    for h in range(ROWS):
        r.ogs[x, mine, :, h * 128 : (h + 1) * 128] = og[h * 16 : (h + 1) * 16]
    r.flip[...] = jnp.zeros((128, 128), F32)
    for name in ("gains", "biases", "wproj"):
        loads[name].wait()
    r.flip[0:5, 0:16] = r.gains[...]
    r.flip[8:13, 0:16] = r.biases[...]
    r.pt[mine] = r.flip[...].T[0:16, :]
    r.wp[mine] = r.wproj[...]

    n_w = {b: new() for b in ORDER}

    def weight_ref(b, i, j):
        return r.w1 if b == 0 else r.wa.at[(b - 1) * 9 + 3 * i + j]

    def transpose_into(slot, ref):
        t = dot_nt(eye, ref[...]).astype(BF16)
        r.tw[slot] = t.reshape(GROUPS, 2, 16, 128)
        r.lw[slot, :, :, 0:128] = r.tw[slot, :, k]

    def prepare_weights(b):
        for i, _ in branch_rows(b):
            slot = SLOTS[(b, i)]
            if b == 0:
                transpose_into(slot, r.w1)
                transpose_into(SLOTS["pool"], r.wpool)
            else:
                for j in range(3):
                    transpose_into(slot + j, weight_ref(b, i, j))

    def send_weights(b):
        lo, hi = SPANS[b]
        send(
            r.tw.at[pl.ds(lo, hi - lo), :, 1 - k],
            r.lw.at[pl.ds(lo, hi - lo), :, :, pl.ds(128, 128)],
            n_w[b],
            sibling,
        )

    def wait_weights(b):
        lo, hi = SPANS[b]
        arrived(r.lw.at[pl.ds(lo, hi - lo), :, :, pl.ds(128, 128)], n_w[b], sibling)

    for name in ("w1", "wpool", "feat"):
        loads[name].wait()
    for block in range(8):
        t = permuted(r.feat, block)
        for h in range(ROWS):
            px = slice(h * 128, (h + 1) * 128)
            r.xv[x, 0, block * 16 : (block + 1) * 16, px] = t[h * 16 : (h + 1) * 16]
    pooled = jnp.zeros((128, 128), F32)
    for h in range(ROWS):
        pooled = pooled + r.xv[x, 0, :, h * 128 : (h + 1) * 128].astype(F32)
    r.pooled[x] = jnp.broadcast_to(lane_sum(pooled) / PIXELS, (128, 128))
    prepare_weights(0)
    loads["wa"].wait()
    prepare_weights(ORDER[1])

    pl.semaphore_wait(barrier, len(partners))

    n_feat = new(2)
    n_foth = new()
    halves = [pl.ds(0, PIXELS // 2), pl.ds(PIXELS // 2, PIXELS // 2)]
    send_weights(0)
    for n in range(2):
        send(r.xv.at[x, 0, :, halves[n]], r.xsib.at[:, halves[n]], n_feat + n, sibling)
    g_og.start()
    send_weights(ORDER[1])
    send(r.xv.at[x, 0], r.xv.at[x, 0], n_foth, xdev)
    g_par.start()
    g_wp.start()
    arrived(r.xsib.at[:, halves[0]], n_feat, sibling)

    def features_at(px):
        return jnp.concatenate([r.xv[x, 0, :, px], r.xsib[:, px]], axis=0)

    def convolve(piece):
        b = piece[0]
        for q in range(piece[1] // BLOCK, (piece[1] + SPAN) // BLOCK):
            px = slice(q * BLOCK, (q + 1) * BLOCK)
            total = None
            for i, offset in branch_rows(b):
                source = q + offset * COLS // BLOCK
                if source < 0 or source >= PIXELS // BLOCK:
                    continue
                slot = SLOTS[(b, i)]
                count = 1 if b == 0 else 3
                weights = r.lw[slot : slot + count].reshape(count * 128, 256)
                part = dot(weights, features_at(slice(source * BLOCK, (source + 1) * BLOCK)))
                total = part if total is None else total + part
            if b:
                rate = atrous_rates[b - 1]
                total = (
                    total[128:256]
                    + shift_cols(total[0:128], rate)
                    + shift_cols(total[256:384], -rate)
                )
            r.acc[b, :, :, px] = total.reshape(GROUPS, 16, BLOCK)
        if carries_pool(piece):
            pooled = jnp.zeros((128, 128), F32)
            for h in range(ROWS):
                pooled = pooled + r.xsib[:, h * 128 : (h + 1) * 128].astype(F32)
            column = jnp.concatenate([r.pooled[x][:, 0:1], lane_sum(pooled) / PIXELS], axis=0)
            terms = split_lanes(column).astype(BF16)
            slot = SLOTS["pool"]
            sums = lane_sum(dot(r.lw[slot].reshape(128, 256), terms))
            r.acp[...] = jnp.broadcast_to(sums, (128, 128)).reshape(GROUPS, 16, 128)

    n_ry = {piece: new() for piece in PIECES}
    n_rz = {piece: new(3) for piece in PIECES}

    def reduce_y_send(piece):
        b, w = piece[0], lanes_of(piece)
        px = pl.ds(piece[1], SPAN)
        r.ys[b, :, :, px] = r.acc[b, pl.ds(4 * (1 - y), 4), :, px].astype(BF16)
        if carries_pool(piece):
            r.ys[b, :, :, PIXELS:WIDE] = encode_pair(r.acp[pl.ds(4 * (1 - y), 4)])
        send(r.ys.at[b, :, :, w], r.yr.at[b, :, :, w], n_ry[piece], ydev)

    def reduce_z_send(piece):
        b, w = piece[0], lanes_of(piece)
        px = pl.ds(piece[1], SPAN)
        arrived(r.yr.at[b, :, :, w], n_ry[piece], ydev)
        for i in (2, 1, 3, 0):
            zz = z if i == 0 else zpos[i]
            g = 4 * y + zz
            s = r.acc[b, g, :, px] + r.yr[b, zz, :, px].astype(F32)
            if carries_pool(piece):
                e = r.acp[g] + decode_pair(r.yr[b, zz, :, PIXELS:WIDE])
            if i == 0:
                r.acc[b, g, :, px] = s
                if carries_pool(piece):
                    r.acp[g] = e
            else:
                r.zs[b, i, :, px] = s.astype(BF16)
                if carries_pool(piece):
                    r.zs[b, i, :, PIXELS:WIDE] = encode_pair(e)
                send(r.zs.at[b, i, :, w], r.zr.at[b, i, :, w], n_rz[piece] + i - 1, zdev[i])

    def reduce_finish(piece):
        b, w = piece[0], lanes_of(piece)
        px = pl.ds(piece[1], SPAN)
        g = pre_group(y, z)
        total = r.acc[b, g, :, px]
        extra = r.acp[g] if carries_pool(piece) else None
        for i in (1, 2, 3):
            arrived(r.zr.at[b, i, :, w], n_rz[piece] + i - 1, zdev[i])
            total = total + r.zr[b, i, :, px].astype(F32)
            if carries_pool(piece):
                extra = extra + decode_pair(r.zr[b, i, :, PIXELS:WIDE])
        r.g[b, x, g, :, px] = total.astype(BF16)
        if carries_pool(piece):
            r.g[b, x, g, :, PIXELS:WIDE] = encode_pair(extra)
        g_pre[piece].start()
        if piece in CROSS_FIRST:
            ref = sums_slot(piece, x)(g)
            send(ref, ref, n_cross[piece], xdev)

    def cross(piece):
        arrived(sums_slot(piece, 1 - x)(pre_group(y, z)), n_cross[piece], xdev)
        g_other[piece].start()

    shift_pairs = []
    lane_r = iota((128, 128), 0)
    lane_c = iota((128, 128), 1)
    for rate in atrous_rates:
        left = jnp.where(lane_r == lane_c - rate, 1.0, 0.0).astype(BF16)
        right = jnp.where(lane_r == lane_c + rate, 1.0, 0.0).astype(BF16)
        shift_pairs.append(jnp.concatenate([left, right], axis=1))

    local = []

    def keep(src, dst):
        copy = pltpu.make_async_copy(src, dst, r.ls.at[len(local)])
        copy.start()
        local.append(copy)

    def place_shifted(image):
        for h in range(ROWS):
            px = slice(h * 128, (h + 1) * 128)
            for a in range(3):
                both = dot(r.xv[image, 0, :, px], shift_pairs[a]).astype(BF16)
                r.xv[image, 1 + 2 * a, :, px] = both[:, 0:128]
                r.xv[image, 2 + 2 * a, :, px] = both[:, 128:256]

    count = float(2 * PIXELS)

    def each_group_loop(body):
        def step(g, _):
            body(g, pl.ds(pl.multiple_of(g * 16, 16), 16))
            return 0

        lax.fori_loop(0, GROUPS, step, 0)

    def each_group(body):
        for g in range(GROUPS):
            body(g, pl.ds(g * 16, 16))

    tiles = [(image, slice(h * 128, (h + 1) * 128)) for image in range(2) for h in range(ROWS)]
    zero_tile = jnp.zeros((16, 128), F32)

    def spread_lanes(column):
        return jnp.broadcast_to(column, (128, 128))

    def norm_params(b):
        mean = lane_sum(r.s1[b]) / count
        inv = lax.rsqrt(lane_sum(r.s2[b]) / count - mean * mean + norm_eps)
        par = r.pt[...].reshape(128, 128)
        scale = par[:, b : b + 1] * inv
        r.pa[b] = spread_lanes(scale)
        r.pb[b] = spread_lanes(par[:, 8 + b : 9 + b] - mean * scale)
        r.pm[b] = spread_lanes(mean)
        r.pi[b] = spread_lanes(inv)

    def grad_params(b):
        s1 = lane_sum(r.s1[b])
        inv, mean = r.pi[b][:, 0:1], r.pm[b][:, 0:1]
        s2 = (lane_sum(r.s2[b]) - mean * s1) * inv
        scale = r.pa[b][:, 0:1]
        c2 = -scale * inv * s2 / count
        r.s1[b] = spread_lanes(s1)
        r.s2[b] = spread_lanes(s2)
        r.c2[b] = spread_lanes(c2)
        r.c1[b] = spread_lanes(-scale * s1 / count - mean * c2)

    def act_and_slope(zed):
        u = 0.5 * jnp.tanh(0.5 * zed)
        sg = 0.5 + u
        act = zed * sg
        return act, sg + act * (0.5 - u)

    def branch_norm(b, each_group):
        def sums(g, rows):
            s, q = zero_tile, zero_tile
            for image, px in tiles:
                v = r.g[b, image, g, :, px].astype(F32)
                s = s + v
                q = q + v * v
            r.s1[b, rows] = s
            r.s2[b, rows] = q

        each_group(sums)
        norm_params(b)

        def apply(g, rows):
            scale, base = r.pa[b, rows], r.pb[b, rows]
            for image, px in tiles:
                act, slope = act_and_slope(r.g[b, image, g, :, px].astype(F32) * scale + base)
                r.act[image, b, g, :, px] = act.astype(BF16)
                r.sl[image, b, g, :, px] = slope.astype(BF16)

        each_group(apply)

    lane128 = iota((128, 128), 1)
    n_pool = new()

    def pool_part():
        pool_cols = jnp.zeros((128, 128), F32)
        for image in range(2):
            pre = decode_pair(r.g[0, image, :, :, PIXELS:WIDE]).reshape(128, 128)
            r.ppool[image] = pre
            pool_cols = pool_cols + jnp.where(lane128 == image, pre * sigmoid(pre), 0.0)
        pool_cols = pool_cols.astype(BF16)
        pool_out = dot(r.wpt[:, 512:640], pool_cols)
        r.poolo[...] = pool_out[0:128]

        r.pools[...] = pool_out[128:256]
        send(r.pools, r.poolr, n_pool, sibling)

    def finish_branch(b, groups):
        for piece in PIECES:
            if piece[0] != b:
                continue
            if piece in CROSS_FIRST:
                g_pre[piece].forward_y()
                g_other[piece].forward_y()
            else:
                g_pre[piece].finish(sums_slot(piece, 1 - x))
        branch_norm(b, groups)

    def projection_weights():
        for b in range(5):
            flat = dot_nt(eye, r.wp[:, b].reshape(128, 256)).astype(BF16)
            r.wps[...] = flat.reshape(GROUPS, 2, 16, 128)
            r.wpt[0:128, b * 128 : (b + 1) * 128] = r.wps[:, k].reshape(128, 128)
            r.wpt[128:256, b * 128 : (b + 1) * 128] = r.wps[:, 1 - k].reshape(128, 128)

    steps = len(PIECES)
    for s in range(steps + 5):
        if s < steps:
            b = PIECES[s][0]
            if s % HALVES == 0:
                wait_weights(b)
            convolve(PIECES[s])
            if s == 0:
                arrived(r.xsib.at[:, halves[1]], n_feat + 1, sibling)
            reduce_y_send(PIECES[s])
            if s % HALVES == 0 and s // HALVES + 2 < len(ORDER):
                prepare_weights(ORDER[s // HALVES + 2])
                send_weights(ORDER[s // HALVES + 2])
        if 0 <= s - 1 < steps:
            reduce_z_send(PIECES[s - 1])
        if s == 2:
            g_par.forward_z()
            g_wp.forward_z()
            g_og.forward_z()
        if 0 <= s - 2 < steps:
            reduce_finish(PIECES[s - 2])
        if s == 3:
            g_par.forward_y()
            g_wp.forward_y()
            g_og.forward_y()
        if s == 8:
            projection_weights()
        if 0 <= s - 3 < steps:
            g_pre[PIECES[s - 3]].forward_z()
            if PIECES[s - 3] in CROSS_FIRST:
                cross(PIECES[s - 3])
        if 0 <= s - 5 < steps:
            if PIECES[s - 5] in CROSS_FIRST:
                g_other[PIECES[s - 5]].forward_z()
            else:
                g_pre[PIECES[s - 5]].forward_y()
        if s == 6:
            place_shifted(x)
        if s == 7:
            arrived(r.xv.at[1 - x, 0], n_foth, xdev)
            place_shifted(1 - x)
            pooled = jnp.zeros((128, 128), F32)
            for h in range(ROWS):
                pooled = pooled + r.xv[1 - x, 0, :, h * 128 : (h + 1) * 128].astype(F32)
            r.pooled[1 - x] = spread_lanes(lane_sum(pooled) / PIXELS)
        if s == 11:
            finish_branch(ORDER[0], each_group_loop)
            pool_part()
        if s == 12:
            finish_branch(ORDER[1], each_group_loop)

    for b in ORDER[2:]:
        finish_branch(b, each_group)

    n_pp = new(4)
    for image in range(2):
        for q in range(PIXELS // BLOCK):
            px = slice(q * BLOCK, (q + 1) * BLOCK)
            part = dot(r.wpt[:, 0:512], r.act[image, :, :, :, px].reshape(512, BLOCK))
            r.acc[image, :, :, px] = part[0:128].reshape(GROUPS, 16, BLOCK)
            r.pps[image, :, :, px] = part[128:256].astype(BF16).reshape(GROUPS, 16, BLOCK)
            if q % 4 == 3:
                span = halves[q // 4]
                number = n_pp + 2 * image + q // 4
                send(r.pps.at[image, :, :, span], r.pr.at[image, :, :, span], number, sibling)

    for image in range(2):
        for b in range(4):
            r.ao[image, b] = r.act[image, b, mine]

    g_og.finish(lambda g: r.ogs.at[1 - x, g])
    for image in range(2):
        for n in range(2):
            arrived(r.pr.at[image, :, :, halves[n]], n_pp + 2 * image + n, sibling)

    arrived(r.poolr, n_pool, sibling)
    for image in range(2):
        r.pcol[image] = spread_lanes((r.poolo[...] + r.poolr[...])[:, image : image + 1])

    def proj_sums(g, rows):
        s, q = zero_tile, zero_tile
        for image, px in tiles:
            v = r.acc[image, g, :, px] + r.pr[image, g, :, px].astype(F32)
            v = v + r.pcol[image, rows]
            r.acc[image, g, :, px] = v
            s = s + v
            q = q + v * v
        r.s1[4, rows] = s
        r.s2[4, rows] = q

    each_group(proj_sums)
    norm_params(4)

    def proj_slope(g, rows):
        scale, base = r.pa[4, rows], r.pb[4, rows]
        s1, s2 = zero_tile, zero_tile
        for image, px in tiles:
            v = r.acc[image, g, :, px]
            _, slope = act_and_slope(v * scale + base)
            dz = r.ogs[image, g, :, px].astype(F32) * slope
            r.dzp[image, g, :, px] = dz
            s1 = s1 + dz
            s2 = s2 + dz * v
        r.s1[4, rows] = s1
        r.s2[4, rows] = s2

    each_group(proj_slope)
    grad_params(4)
    n_dp = new(2)
    for image in range(2):

        def proj_low(g, rows, image=image):
            scale, c1, c2 = r.pa[4, rows], r.c1[4, rows], r.c2[4, rows]
            total = zero_tile
            for h in range(ROWS):
                px = slice(h * 128, (h + 1) * 128)
                low = scale * r.dzp[image, g, :, px] + (r.acc[image, g, :, px] * c2 + c1)
                low = low.astype(BF16)
                r.dp[image, g, k, :, px] = low
                total = total + low.astype(F32)
            r.s1[image, rows] = total

        each_group(proj_low)
        ref = r.dp.at[image, :, k]
        send(ref, ref, n_dp + image, sibling)

    n_rsum = new()
    row_sums = jnp.where(lane128 == 0, lane_sum(r.s1[0]), 0.0)
    row_sums = row_sums + jnp.where(lane128 == 1, lane_sum(r.s1[1]), 0.0)
    r.rsum[:, k] = row_sums.reshape(GROUPS, 16, 128)
    ref = r.rsum.at[:, k]
    send(ref, ref, n_rsum, sibling)

    my_rows = pl.ds(pl.multiple_of(mine * 16, 16), 16)
    scale, base = r.pa[4, my_rows], r.pb[4, my_rows]
    for h in range(ROWS):
        zed = r.acc[x, mine, :, h * 128 : (h + 1) * 128] * scale + base
        r.outv[pl.ds(h, 16, stride=16), :] = zed * sigmoid(zed)
    keep(r.outv, r.out)

    for image in range(2):
        arrived(r.dp.at[image, :, 1 - k], n_dp + image, sibling)
    arrived(r.rsum.at[:, 1 - k], n_rsum, sibling)

    n_d = {b: new(2) for b in ORDER}

    def back_block(b, turn, image, q):
        px = slice(q * 512, (q + 1) * 512)
        dblock = r.dp[image, :, :, :, px].reshape(256, 512)
        back = dot(r.wp[:, b].reshape(128, 256), dblock)
        r.acc[2 * turn + image, :, :, px] = back.reshape(GROUPS, 16, 512)

    back_order = (1, 2, 3, 0)

    dwp = [jnp.zeros((64, 256), F32)]

    def proj_weights(image, q):
        px = slice(q * 512, (q + 1) * 512)
        acts = r.ao[image, :, :, px].reshape(64, 512)
        dwp[0] = dwp[0] + dot_nt(acts, r.dp[image, :, :, :, px].reshape(256, 512))

    def branch_slope(b, turn):
        for image in range(2):
            for q in range(PIXELS // 512):
                back_block(b, turn, image, q)

        def slope(g, rows):
            s1, s2 = zero_tile, zero_tile
            for image, px in tiles:
                dz = r.acc[2 * turn + image, g, :, px] * r.sl[image, b, g, :, px].astype(F32)
                r.acc[2 * turn + image, g, :, px] = dz
                s1 = s1 + dz
                s2 = s2 + dz * r.g[b, image, g, :, px].astype(F32)
            r.s1[b, rows] = s1
            r.s2[b, rows] = s2
            if b == back_order[0]:
                proj_weights(g // 4, g % 4)

        each_group(slope)

    def branch_low(b, turn):
        grad_params(b)
        for image in range(2):

            def lower(g, rows, image=image):
                scale, c1, c2 = r.pa[b, rows], r.c1[b, rows], r.c2[b, rows]
                for h in range(ROWS):
                    px = slice(h * 128, (h + 1) * 128)
                    v = r.g[b, image, g, :, px].astype(F32)
                    low = scale * r.acc[2 * turn + image, g, :, px] + (v * c2 + c1)
                    r.d[b, image, g, k, :, px] = low.astype(BF16)

            each_group(lower)
            there = r.d.at[b, image, :, k]
            send(there, there, n_d[b] + image, sibling)

    def wait_grads(*branches):
        for b in branches:
            for image in range(2):
                arrived(r.d.at[b, image, :, 1 - k], n_d[b] + image, sibling)

    def branch_grads(b, first_branch, last_branch):
        planes = (2 * b - 1, 0, 2 * b)
        for i, offset in branch_rows(b):
            first, last = max(0, -offset), min(ROWS, ROWS - offset)
            there = slice((first + offset) * 128, (last + offset) * 128)
            here = slice(first * 128, last * 128)
            total = None
            for image in range(2):
                if b == 0:
                    rows = r.xv[image, 0]
                else:
                    rows = jnp.concatenate([r.xv[image, p, :, there] for p in planes], axis=0)
                part = dot_nt(rows, r.d[b, image, :, :, :, here].reshape(256, -1))
                total = part if total is None else total + part
            total = total.astype(BF16)
            if b == 0:
                slot = pl.ds(27, 1)
                r.dwv[27] = total
            else:
                slot = pl.ds((b - 1) * 9 + 3 * i, 3)
                r.dwv[slot] = total.reshape(3, 128, 256)
            keep(r.dwv.at[slot], r.dwb.at[slot])
        for q in range(PIXELS // BLOCK):
            px = slice(q * BLOCK, (q + 1) * BLOCK)
            total = None
            for i, offset in branch_rows(b):
                source = q - offset * COLS // BLOCK
                if source < 0 or source >= PIXELS // BLOCK:
                    continue
                if b == 0:
                    weights = r.w1[...]
                else:
                    weights = r.wa[pl.ds((b - 1) * 9 + 3 * i, 3)].reshape(384, 256)
                dblock = r.d[b, x, :, :, :, source * BLOCK : (source + 1) * BLOCK]
                part = dot(weights, dblock.reshape(256, BLOCK))
                total = part if total is None else total + part
            if b:
                rate = atrous_rates[b - 1]
                total = (
                    total[128:256]
                    + shift_cols(total[0:128], -rate)
                    + shift_cols(total[256:384], rate)
                )
            if not first_branch:
                total = total + r.fga[:, px]
            if last_branch:
                r.fgv[:, px] = (total + fg_pool).astype(BF16)
            else:
                r.fga[:, px] = total

    wp4 = r.wp[:, 4].reshape(128, 256)
    dpo = jnp.zeros((128, 128), F32)
    dwp4 = jnp.zeros((16, 256), F32)
    lane16 = iota((16, 128), 1)
    for image in range(2):
        terms = split_lanes(r.rsum[...].reshape(256, 128)[:, image : image + 1]).astype(BF16)
        pool_grad = lane_sum(dot(wp4, terms))
        pre = r.ppool[image][:, 0:1]
        _, slope = act_and_slope(pre)
        low = (pool_grad * slope).astype(BF16).astype(F32)
        for lane in (image, image + 2, image + 4):
            dpo = dpo + jnp.where(lane128 == lane, low, 0.0)
        mine_act, _ = act_and_slope(r.ppool[image, my_rows][:, 0:1])
        mine_act = mine_act.astype(BF16).astype(F32)
        dwp4 = dwp4 + mine_act * dot_nt(jnp.ones((16, 128), BF16), terms)
    r.dwprojv[4] = dwp4
    r.dpo[:, k] = dpo.astype(BF16).reshape(GROUPS, 16, 128)
    n_dpo = new()
    branch_slope(back_order[0], 0)
    for n, b in enumerate(back_order):
        if n + 1 < len(back_order):
            branch_slope(back_order[n + 1], (n + 1) % 2)
        branch_low(b, n % 2)
        if n == 0:
            ref = r.dpo.at[:, k]
            send(ref, ref, n_dpo, sibling)
            r.dwprojv[0:4] = dwp[0].reshape(4, 16, 256)
            keep(r.dwprojv, r.dwproj)
    wait_grads(back_order[0])
    branch_grads(back_order[0], True, False)
    wait_grads(*back_order[1:])
    branch_grads(back_order[1], False, False)

    tile = jnp.zeros((16, 128), F32)
    for b in range(5):
        tile = tile + jnp.where(lane16 == b, r.s2[b, my_rows], 0.0)
        tile = tile + jnp.where(lane16 == 8 + b, r.s1[b, my_rows], 0.0)
    r.flip[0:16, :] = tile
    flipped = r.flip[...].T
    r.dgainsv[...] = flipped[0:5, 0:16]
    r.dbiasesv[...] = flipped[8:13, 0:16]
    keep(r.dgainsv, r.dgains)
    keep(r.dbiasesv, r.dbiases)

    branch_grads(back_order[2], False, False)

    arrived(r.dpo.at[:, 1 - k], n_dpo, sibling)
    dpo = r.dpo[...].reshape(256, 128)
    pooled = jnp.zeros((128, 128), F32)
    for image in range(2):
        pooled = pooled + split_lanes(r.pooled[image][:, 0:1], (image, image + 2, image + 4))
    r.dwpoolv[...] = dot_nt(pooled.astype(BF16), dpo)
    keep(r.dwpoolv, r.dwpool)
    spread = dot(r.wpool[...], dpo)
    fg_pool = lane_sum(jnp.where(lane128 == x, spread, 0.0)) / PIXELS

    branch_grads(back_order[3], False, True)
    keep(r.fgv, r.fgb)
    for copy in sent:
        copy.wait_send()
    for copy in local:
        copy.wait()


COPY_INPUTS = ("out", "dwpool", "dwproj", "dgains", "dbiases", "fgb", "dwb")
COPY_OUTPUTS = ("out_o", "dwpool_o", "dwproj_o", "dgains_o", "dbiases_o", "fg", "dw1", "dwa")
COPY_SCRATCH = {
    "outv": pltpu.VMEM((256, 128), F32),
    "dwpoolv": pltpu.VMEM((128, 256), F32),
    "dwprojv": pltpu.VMEM((5, 16, 256), F32),
    "fgbv": pltpu.VMEM((128, PIXELS), BF16),
    "dwbv": pltpu.VMEM((28, 128, 256), BF16),
    "fgv": pltpu.VMEM((2048, 128), F32),
    "dwv": pltpu.VMEM((28, 128, 256), F32),
    "si": pltpu.SemaphoreType.DMA((16,)),
    "so": pltpu.SemaphoreType.DMA((16,)),
}


def copy_kernel(*refs):
    r = Refs()
    names = COPY_INPUTS + COPY_OUTPUTS + tuple(COPY_SCRATCH)
    for name, ref in zip(names, refs, strict=True):
        setattr(r, name, ref)
    loads = []
    stores = []

    def load(src, dst):
        copy = pltpu.make_async_copy(src, dst, r.si.at[len(loads)])
        copy.start()
        loads.append(copy)
        return copy

    def store(src, dst):
        copy = pltpu.make_async_copy(src, dst, r.so.at[len(stores)])
        copy.start()
        stores.append(copy)

    met = [
        (b - 1) * 9 + 3 * i for b in (1, 2, 3) for i in range(3) if i in dict(branch_rows(b))
    ]
    taps = [(n, load(r.dwb.at[pl.ds(n, 3)], r.dwbv.at[pl.ds(n, 3)])) for n in met]
    one = load(r.dwb.at[pl.ds(27, 1)], r.dwbv.at[pl.ds(27, 1)])
    fg = load(r.fgb, r.fgbv)
    passed = [
        (load(getattr(r, name), getattr(r, name + "v")), name)
        for name in ("out", "dwpool", "dwproj")
    ]
    r.dgains_o[...] = r.dgains[...]
    r.dbiases_o[...] = r.dbiases[...]
    for n, copy in taps:
        copy.wait()
        r.dwv[n : n + 3] = r.dwbv[n : n + 3].astype(F32)
        store(r.dwv.at[pl.ds(n, 3)], r.dwa.at[pl.ds(n, 3)])
    for n in range(0, 27, 3):
        if n not in met:
            r.dwv[n : n + 3] = jnp.zeros((3, 128, 256), F32)
            store(r.dwv.at[pl.ds(n, 3)], r.dwa.at[pl.ds(n, 3)])
    one.wait()
    r.dwv[27] = r.dwbv[27].astype(F32)
    store(r.dwv.at[27], r.dw1)
    fg.wait()
    rr = iota((256, 256), 0)
    cc = iota((256, 256), 1)
    perm = jnp.where(cc == lax.rem(rr, 16) * 16 + lax.div(rr, 16), 1.0, 0.0).astype(BF16)
    for block in range(8):
        channels = slice(block * 16, (block + 1) * 16)
        parts = [r.fgbv[channels, h * 128 : (h + 1) * 128] for h in range(ROWS)]
        r.fgv[block * 256 : (block + 1) * 256] = dot(perm, jnp.concatenate(parts, axis=0))
        if block % 4 == 3:
            half = pl.ds((block - 3) * 256, 1024)
            store(r.fgv.at[half], r.fg.at[half])
    for copy, name in passed:
        copy.wait()
        store(getattr(r, name + "v"), getattr(r, name + "_o"))
    for copy in stores:
        copy.wait()


def fused(features, w_one, w_atrous, w_pool, w_proj, gains, biases, out_grad):
    vmem = pl.BlockSpec(memory_space=pltpu.VMEM)
    hbm = pl.BlockSpec(memory_space=pl.ANY)
    passed = [(256, 128), (128, 256), (5, 16, 256), (5, 16), (5, 16)]
    shapes = [jax.ShapeDtypeStruct(s, F32) for s in passed]
    shapes.append(jax.ShapeDtypeStruct((128, PIXELS), BF16))
    shapes.append(jax.ShapeDtypeStruct((28, 128, 256), BF16))
    parts = pl.pallas_call(
        head_kernel,
        out_shape=shapes,
        in_specs=[hbm] * len(INPUTS),
        out_specs=[hbm] * len(OUTPUTS),
        scratch_shapes=list(scratch_table(NSEMS).values()),
        compiler_params=pltpu.CompilerParams(
            collective_id=0, has_side_effects=True, vmem_limit_bytes=64 * 2**20
        ),
    )(
        features.reshape(2048, 128),
        out_grad.reshape(256, 128),
        w_one,
        w_atrous.reshape(27, 128, 256),
        w_pool,
        w_proj,
        gains,
        biases,
    )
    result = passed + [(2048, 128), (128, 256), (27, 128, 256)]
    out, dwpool, dwproj, dgains, dbiases, fg, dw1, dwa = pl.pallas_call(
        copy_kernel,
        out_shape=[jax.ShapeDtypeStruct(s, F32) for s in result],
        in_specs=[hbm] * 3 + [vmem] * 2 + [hbm] * 2,
        out_specs=[hbm] * 3 + [vmem] * 2 + [hbm] * 3,
        scratch_shapes=list(COPY_SCRATCH.values()),
        compiler_params=pltpu.CompilerParams(vmem_limit_bytes=64 * 2**20),
    )(*parts)
    return (
        out.reshape(1, 16, ROWS, COLS),
        fg.reshape(1, 128, ROWS, COLS),
        dw1,
        dwa.reshape(3, 9, 128, 256),
        dwpool,
        dwproj,
        dgains,
        dbiases,
    )


def solution(mesh):
    placed = (
        P("dp", "chan", None, None),
        P("chan", None),
        P(None, None, "chan", None),
        P("chan", None),
        P(None, "chan", None),
        P(None, "chan"),
        P(None, "chan"),
        P("dp", "chan", None, None),
    )
    small = mesh.shape["dp"] == 2 and mesh.shape["chan"] == 16
    return jax.shard_map(
        fused if small else local,
        mesh=mesh,
        in_specs=placed,
        out_specs=(
            P("dp", "chan", None, None),
            P("dp", "chan", None, None),
            P("chan", None),
            P(None, None, "chan", None),
            P("chan", None),
            P(None, "chan", None),
            P(None, "chan"),
            P(None, "chan"),
        ),
        check_vma=False,
    )
```
